128 devices in a mesh: section: 2 (over core), dp: 64 (over x, y, z).
Axes of the slice: x: 4, y: 4, z: 4, core: 2. Of those that a mesh axis runs over, the one named last changes fastest.
Arguments:
- tokens: bfloat16 [16384, 768], P('dp'), may hold values from -6 to 6
- lengths: int32 [256, 4], P('dp'), may hold values from 1 to 32, 64 in all within a row
- w_qkv: float32 [2, 768, 576], P('section', 'dp'), may hold values from -0.4375 to 0.4375
- b_qv: float32 [2, 1536], P('section', 'dp'), may hold values from -3 to 3
- w_post: float32 [2, 768, 768], P('section', 'dp'), may hold values from -0.625 to 0.625
- b_post: float32 [2, 768], P('section', 'dp'), may hold values from -3 to 3
- gain_one: float32 [2, 768], P('section', 'dp'), may hold values from 0.25 to 1.75
- shift_one: float32 [2, 768], P('section', 'dp'), may hold values from -3 to 3
- w_inter: float32 [2, 768, 768], P('section', 'dp'), may hold values from -0.4375 to 0.4375
- b_inter: float32 [2, 3072], P('section', 'dp'), may hold values from -3 to 3
- w_out: float32 [2, 3072, 192], P('section', 'dp'), may hold values from -0.21875 to 0.21875
- b_out: float32 [2, 768], P('section', 'dp'), may hold values from -3 to 3
- gain_two: float32 [2, 768], P('section', 'dp'), may hold values from 0.25 to 1.75
- shift_two: float32 [2, 768], P('section', 'dp'), may hold values from -3 to 3
- embed_table: float32 [768, 30528], P('dp', 'section'), may hold values from -0.21875 to 0.21875
- logit_grad: bfloat16 [16384, 30528], P('dp', 'section'), may hold values from -1 to 1
Outputs:
- logits: bfloat16 [16384, 30528], P('dp', 'section')
- token_grad: bfloat16 [16384, 768], P('dp', 'section')
- grad_w_qkv: float32 [2, 768, 576], P('section', 'dp')
- grad_b_qv: float32 [2, 1536], P('section', 'dp')
- grad_w_post: float32 [2, 768, 768], P('section', 'dp')
- grad_b_post: float32 [2, 768], P('section', 'dp')
- grad_gain_one: float32 [2, 768], P('section', 'dp')
- grad_shift_one: float32 [2, 768], P('section', 'dp')
- grad_w_inter: float32 [2, 768, 768], P('section', 'dp')
- grad_b_inter: float32 [2, 3072], P('section', 'dp')
- grad_w_out: float32 [2, 3072, 192], P('section', 'dp')
- grad_b_out: float32 [2, 768], P('section', 'dp')
- grad_gain_two: float32 [2, 768], P('section', 'dp')
- grad_shift_two: float32 [2, 768], P('section', 'dp')
- table_grad: float32 [768, 30528], P('dp', 'section')
The draws below stay inside these ranges and needn't reach their ends.
Inputs may be any that keep to these rules, and one draw needn't show every extreme that they name: Each row holds the lengths of 4 sequences packed in order into one micro-batch, summing to 64; the longest is 32.
All inputs are finite; a program needn't handle non-finite values.
Results may differ from the reference program's by a relative error of at most 0.022.
Values may be sent and summed in bfloat16 or wider, within the bound.
No kernel may reach another device: no remote copies, remote signals or barrier semaphores. Data moves between devices by JAX's collectives and lax.ppermute only.
A program may use at most 384 MiB of HBM per device.

```python
import math
import jax
import jax.numpy as jnp
import numpy as np
from jax import lax

D = 768
FF = 3072
V = 30528
GROUPS = 4
LAYERS = 2
DOCS = 4
MB_TOK = 64
TOKENS = 16384
NMB = 256


def block_scale(own_key, extent, split, low, largest):
    def one(dim, parts):
        steps = jax.random.uniform(jax.random.fold_in(jax.random.fold_in(own_key, 6), dim), (parts,), jnp.float32, low / len(split), largest / len(split))
        return jnp.repeat(jnp.exp(steps), extent[dim] // parts).reshape((-1,) + (1,) * (len(extent) - dim - 1))

    level = one(*split[0])
    for cut in split[1:]:
        level = level * one(*cut)
    return level


def split_up(number_of, total, most, slope):
    loads = [(1 << 20) // math.isqrt(standing ** slope) + 1 for standing in range(2, number_of + 1)]
    surplus, counts = total - most - (number_of - 1), [1] * (number_of - 1)
    while surplus > 0:
        candidates = [i for i in range(number_of - 1) if counts[i] < most]
        mass, left = sum([loads[i] for i in candidates]), surplus
        for i in candidates:
            extra = min(most - counts[i], max(1, left * loads[i] // mass), surplus)
            counts[i] = counts[i] + extra
            surplus = surplus - extra
    return np.array([most] + counts)


def uneven_parts(own_key, number_of, total, most, lean):
    if number_of == 2:
        one = jax.random.randint(own_key, (), max(1, total - most), min(most, total - 1) + 1)
        return jnp.stack([one, total - one])
    tallies = jnp.asarray(split_up(number_of, total, most, lean), jnp.int32)
    pairs = (number_of - 1) // 2
    donor, taker = tallies[1:1 + 2 * pairs:2], tallies[2:2 + 2 * pairs:2]
    room = jnp.minimum(donor - 1, most - taker)
    moved = jax.random.randint(jax.random.fold_in(own_key, 1), (pairs,), 0, 1 << 20) % (room + 1)
    tallies = tallies.at[1:1 + 2 * pairs:2].set(donor - moved).at[2:2 + 2 * pairs:2].set(taker + moved)
    return tallies[jax.random.permutation(jax.random.fold_in(own_key, 2), number_of)]


def scatter_about(rng, extent, spread, limit, shards=(), kind=jnp.bfloat16):
    factor_of = block_scale(rng, extent, shards, -0.22, 0.18) if shards else 1.0
    entries = jax.random.normal(rng, extent, jnp.float32) * spread * factor_of
    return jnp.minimum(jnp.maximum(entries, -limit), limit).astype(kind)


def setup_inputs(seed: int = 0) -> dict:
    streams_of = jax.random.split(jax.random.key(seed), 17)
    return {
        "tokens": scatter_about(streams_of[0], (TOKENS, D), 1.0, 6.0, ((0, 64),)),
        "lengths": jax.vmap(lambda own: uneven_parts(own, DOCS, MB_TOK, MB_TOK // 2, 2))(jax.random.split(streams_of[1], NMB)).reshape((NMB, DOCS)).astype(jnp.int32),
        "w_qkv": scatter_about(streams_of[2], (LAYERS, D, 3 * D // GROUPS), (D // GROUPS) ** -0.5, 0.4375, ((0, 2), (1, 64)), jnp.float32),
        "b_qv": scatter_about(streams_of[3], (LAYERS, 2 * D), 0.5, 3.0, ((0, 2), (1, 64)), jnp.float32),
        "w_post": scatter_about(streams_of[4], (LAYERS, D, D), (D // 8) ** -0.5, 0.625, ((0, 2), (1, 64)), jnp.float32),
        "b_post": scatter_about(streams_of[5], (LAYERS, D), 0.5, 3.0, ((0, 2), (1, 64)), jnp.float32),
        "gain_one": jnp.clip(1.0 + 0.15 * jax.random.normal(streams_of[6], (LAYERS, D), jnp.float32), 0.25, 1.75),
        "shift_one": scatter_about(streams_of[7], (LAYERS, D), 0.5, 3.0, ((0, 2), (1, 64)), jnp.float32),
        "w_inter": scatter_about(streams_of[8], (LAYERS, D, FF // GROUPS), (D // GROUPS) ** -0.5, 0.4375, ((0, 2), (1, 64)), jnp.float32),
        "b_inter": scatter_about(streams_of[9], (LAYERS, FF), 0.5, 3.0, ((0, 2), (1, 64)), jnp.float32),
        "w_out": scatter_about(streams_of[10], (LAYERS, FF, D // GROUPS), (FF // GROUPS) ** -0.5, 0.21875, ((0, 2), (1, 64)), jnp.float32),
        "b_out": scatter_about(streams_of[11], (LAYERS, D), 0.5, 3.0, ((0, 2), (1, 64)), jnp.float32),
        "gain_two": jnp.clip(1.0 + 0.15 * jax.random.normal(streams_of[12], (LAYERS, D), jnp.float32), 0.25, 1.75),
        "shift_two": scatter_about(streams_of[13], (LAYERS, D), 0.5, 3.0, ((0, 2), (1, 64)), jnp.float32),
        "embed_table": scatter_about(streams_of[14], (D, V), D ** -0.5, 0.21875, ((0, 64), (1, 2)), jnp.float32),
        "logit_grad": scatter_about(streams_of[15], (TOKENS, V), (V // D) ** -0.5, 1.0, ((0, 64), (1, 2))),
    }


@jax.custom_vjp
def low(v):
    return lax.optimization_barrier(v.astype(jnp.bfloat16)).astype(jnp.float32)

@jax.custom_vjp
def low_back(v):
    return v

def low_keep(v):
    return (low(v), None)

def low_pass(kept, grad):
    return (grad,)

def back_keep(v):
    return (v, None)

def back_low(kept, grad):
    return (low(grad),)
low.defvjp(low_keep, low_pass)
low_back.defvjp(back_keep, back_low)
highest = lax.Precision.HIGHEST

def both_ways(values):
    return low(low_back(values))

def layer_norm(values, gain, shift):
    row_mean = lax.optimization_barrier(jnp.mean(values, axis=-1, keepdims=True))
    centred = values - row_mean
    variance = lax.optimization_barrier(jnp.mean(centred * centred, axis=-1, keepdims=True))
    return centred * lax.rsqrt(variance + 1e-12) * gain + shift

def same_document(length_row, row_count):
    doc_ends = jnp.cumsum(length_row.astype(jnp.int32))
    places = jnp.arange(row_count, dtype=jnp.int32)
    doc_index = lax.optimization_barrier(jnp.sum((places[:, None] >= doc_ends[None, :]).astype(jnp.int32), axis=1))
    return doc_index[:, None] == doc_index[None, :]

def grouped(values, matrix):
    row_count = values.shape[0]
    fan_in = matrix.shape[0] // 4
    inputs = values.reshape(row_count, 4, fan_in)
    weights = matrix.reshape(4, fan_in, matrix.shape[1])
    return jnp.einsum('ngc,gcf->ngf', inputs, weights, precision=highest)

def layer_forward(inputs, doc_mask, weights):
    w_qkv, b_qv, w_post, b_post, gain_one, shift_one, w_inter, b_inter, w_out, b_out, gain_two, shift_two = weights
    row_count, model_width = inputs.shape
    group_width = model_width // 4
    head_count = model_width // 64
    project = grouped(inputs, w_qkv)
    queries = both_ways(project[:, :, :group_width].reshape(row_count, model_width) + b_qv[:model_width])
    keys_part = both_ways(project[:, :, group_width:2 * group_width].reshape(row_count, model_width))
    values_part = both_ways(project[:, :, 2 * group_width:].reshape(row_count, model_width) + b_qv[model_width:])
    query_heads = queries.reshape(row_count, head_count, 64)
    key_heads = keys_part.reshape(row_count, head_count, 64)
    value_heads = values_part.reshape(row_count, head_count, 64)
    scores = low_back(jnp.einsum('qhd,khd->hqk', query_heads, key_heads, precision=highest) * 0.125)
    scores = jnp.where(doc_mask[None], scores, -1e+30)
    row_top = lax.optimization_barrier(jnp.max(scores, axis=-1, keepdims=True))
    exponents = jnp.exp(scores - row_top)
    attention = low(exponents / lax.optimization_barrier(jnp.sum(exponents, axis=-1, keepdims=True)))
    context = both_ways(jnp.einsum('hqk,khd->qhd', attention, value_heads, precision=highest).reshape(row_count, model_width))
    post_out = low_back(jnp.dot(context, w_post, precision=highest) + b_post)
    hidden = both_ways(layer_norm(post_out + inputs, gain_one, shift_one))
    inter_pre = low_back(grouped(hidden, w_inter).reshape(row_count, -1) + b_inter)
    activated = low(jax.nn.gelu(inter_pre, approximate=False))
    output = low_back(grouped(activated, w_out).reshape(row_count, model_width) + b_out)
    return layer_norm(output + hidden, gain_two, shift_two)

def reference(tokens, lengths, w_qkv, b_qv, w_post, b_post, gain_one, shift_one, w_inter, b_inter, w_out, b_out, gain_two, shift_two, embed_table, logit_grad):
    params = (w_qkv, b_qv, w_post, b_post, gain_one, shift_one, w_inter, b_inter, w_out, b_out, gain_two, shift_two)
    params_float = tuple((weight.astype(jnp.float32) for weight in params))

    def forward(token_values, param_values, table_values):
        low_params = tuple((low(weight) for weight in param_values))
        low_table = low(table_values)
        blocks = token_values.reshape(-1, MB_TOK, token_values.shape[1])

        def one_micro(micro_pair):
            block_rows, length_row = micro_pair
            doc_mask = same_document(length_row, MB_TOK)
            layer_zero = layer_forward(block_rows, doc_mask, tuple((weight[0] for weight in low_params)))
            layer_one = layer_forward(low_back(low(layer_zero)), doc_mask, tuple((weight[1] for weight in low_params)))
            return jnp.dot(low(layer_one), low_table, precision=highest)
        logit_blocks = lax.map(jax.checkpoint(one_micro), (blocks, lengths))
        return logit_blocks.reshape(-1, low_table.shape[1])
    logit_values, pullback = jax.vjp(forward, tokens.astype(jnp.float32), params_float, embed_table.astype(jnp.float32))
    token_grad, param_grads, table_grad = pullback(logit_grad.astype(jnp.float32))
    return (logit_values.astype(jnp.bfloat16), token_grad.astype(jnp.bfloat16), param_grads[0], param_grads[1], param_grads[2], param_grads[3], param_grads[4], param_grads[5], param_grads[6], param_grads[7], param_grads[8], param_grads[9], param_grads[10], param_grads[11], table_grad)
```

```python
import functools
import jax
import jax.numpy as jnp
from jax import lax
from jax.experimental import pallas as pl
from jax.experimental.pallas import tpu as pltpu
from jax.sharding import PartitionSpec as P

BF = jnp.bfloat16
F32 = jnp.float32
ROWS, WIDTH, FF_GROUP, GROUP, HEADS = 128, 768, 768, 192, 12
SHARD = {
    "b_qv": (0, 24), "b_inter": (24, 48), "b_post": (72, 12), "gain_one": (84, 12),
    "shift_one": (96, 12), "b_out": (108, 12), "gain_two": (120, 12), "shift_two": (132, 12),
}
PLACE, _at = {}, 0
for _name, (_off, _width) in SHARD.items():
    PLACE[_name] = (_at, 64 * _width)
    _at += 64 * _width
VECTOR = _at


def dot(a, b):
    return lax.dot_general(a, b, (((1,), (0,)), ((), ())), preferred_element_type=F32)


def dot_nt(a, b):
    return lax.dot_general(a, b, (((1,), (1,)), ((), ())), preferred_element_type=F32)


def dot_tn(a, b):
    return lax.dot_general(a, b, (((0,), (0,)), ((), ())), preferred_element_type=F32)


def vector_of(vec_ref, name):
    at, size = PLACE[name]
    return vec_ref[:, at : at + size]


def norm_parts(values):
    mean = jnp.mean(values, axis=-1, keepdims=True)
    centred = values - mean
    scale = lax.rsqrt(jnp.mean(centred * centred, axis=-1, keepdims=True) + 1e-12)
    return centred * scale, scale


def same_doc(lengths_ref, first_row):
    row = lax.broadcasted_iota(jnp.int32, (ROWS, ROWS), 0)
    col = lax.broadcasted_iota(jnp.int32, (ROWS, ROWS), 1)
    row_id = jnp.zeros((ROWS, ROWS), jnp.int32)
    col_id = jnp.zeros((ROWS, ROWS), jnp.int32)
    for micro in range(2):
        end = micro * 64
        for doc in range(4):
            end = end + lengths_ref[first_row + micro, doc]
            row_id = row_id + (row >= end).astype(jnp.int32)
            col_id = col_id + (col >= end).astype(jnp.int32)
    return row_id == col_id


def gelu_parts(x):
    half = 0.5 * (1.0 + lax.erf(x * 0.7071067811865476))
    return half


def layer_forward(u_ref, same, wa, wb, wc, vec_ref, y_ref, q_ref, k_ref, v_ref, p_ref, ctx_ref, xh1_ref, rs1_ref, hid_ref, inter_ref, xh2_ref, rs2_ref):
    u = u_ref[...]
    for g in range(4):
        cols = slice(GROUP * g, GROUP * (g + 1))
        block = dot(u[:, cols], wa(g))
        b_q = vec_ref[:, PLACE["b_qv"][0] + GROUP * g : PLACE["b_qv"][0] + GROUP * (g + 1)]
        b_v = vec_ref[:, PLACE["b_qv"][0] + WIDTH + GROUP * g : PLACE["b_qv"][0] + WIDTH + GROUP * (g + 1)]
        q_ref[:, cols] = (block[:, :GROUP] + b_q).astype(BF)
        k_ref[:, cols] = block[:, GROUP : 2 * GROUP].astype(BF)
        v_ref[:, cols] = (block[:, 2 * GROUP : 3 * GROUP] + b_v).astype(BF)
    lane = lax.broadcasted_iota(jnp.int32, (ROWS, 128), 1)
    for pair in range(HEADS // 2):
        cols = slice(128 * pair, 128 * (pair + 1))
        qt, kt, vt = q_ref[:, cols], k_ref[:, cols], v_ref[:, cols]
        outs = []
        for half in range(2):
            mine = (lane >= 64) if half else (lane < 64)
            qm = jnp.where(mine, qt, jnp.zeros_like(qt))
            scores = jnp.where(same, dot_nt(qm, kt) * 0.125, -1e30)
            top = jnp.max(scores, axis=-1, keepdims=True)
            e = jnp.exp(scores - top)
            p = e / jnp.sum(e, axis=-1, keepdims=True)
            p_ref[2 * pair + half] = p
            outs.append(dot(p.astype(BF), vt))
        ctx_ref[:, cols] = jnp.where(lane < 64, outs[0], outs[1]).astype(BF)
    ctx = ctx_ref[...]
    w_post, _ = wb(None)
    r1 = dot(ctx, w_post) + vector_of(vec_ref, "b_post") + u.astype(F32)
    xh, rs = norm_parts(r1)
    xh1_ref[...] = xh
    rs1_ref[...] = jnp.broadcast_to(rs, (ROWS, 128))
    hidden = (xh * vector_of(vec_ref, "gain_one") + vector_of(vec_ref, "shift_one")).astype(BF)
    hid_ref[...] = hidden
    outs = []
    for g in range(4):
        cols = slice(GROUP * g, GROUP * (g + 1))
        _, w_inter = wb(g)
        at = PLACE["b_inter"][0] + FF_GROUP * g
        inter = dot(hidden[:, cols], w_inter) + vec_ref[:, at : at + FF_GROUP]
        inter_ref[:, FF_GROUP * g : FF_GROUP * (g + 1)] = inter
        act = (inter * gelu_parts(inter)).astype(BF)
        outs.append(dot(act, wc(g)))
    r2 = jnp.concatenate(outs, axis=1) + vector_of(vec_ref, "b_out") + hidden.astype(F32)
    xh, rs = norm_parts(r2)
    xh2_ref[...] = xh
    rs2_ref[...] = jnp.broadcast_to(rs, (ROWS, 128))
    y_ref[...] = (xh * vector_of(vec_ref, "gain_two") + vector_of(vec_ref, "shift_two")).astype(BF)


def norm_back(gy, xh, rs, gain):
    t = gy * gain
    m1 = jnp.mean(t, axis=-1, keepdims=True)
    m2 = jnp.mean(t * xh, axis=-1, keepdims=True)
    return rs[:, :1] * (t - m1 - xh * m2)


def layer_backward(gy, u_ref, wa, wb, wc, vec_ref, q_ref, k_ref, v_ref, p_ref, ctx_ref, xh1_ref, rs1_ref, hid_ref, inter_ref, xh2_ref, rs2_ref,
                   gu_ref, put_a, put_b, put_c, gvec_ref, gq_ref, gk_ref, gv_ref):
    def put_vec(name, row, start=0):
        at = PLACE[name][0] + start
        gvec_ref[:, at : at + row.shape[1]] = row

    def colsum(x):
        return jnp.sum(x.astype(F32), axis=0, keepdims=True)

    xh2 = xh2_ref[...]
    put_vec("gain_two", colsum(gy * xh2))
    put_vec("shift_two", colsum(gy))
    g_r2 = norm_back(gy, xh2, rs2_ref[...], vector_of(vec_ref, "gain_two"))
    g_out = g_r2.astype(BF)
    put_vec("b_out", colsum(g_out))
    hidden = hid_ref[...]
    hidden_t = hidden.T
    parts = []
    for g in range(4):
        cols = slice(GROUP * g, GROUP * (g + 1))
        wide = slice(FF_GROUP * g, FF_GROUP * (g + 1))
        inter = inter_ref[:, wide]
        half = gelu_parts(inter)
        act = (inter * half).astype(BF)
        slope = half + inter * (jnp.exp(-0.5 * inter * inter) * 0.3989422804014327)
        go = g_out[:, cols]
        put_c(g, dot(act.T, go))
        g_inter = (dot_nt(go, wc(g)) * slope).astype(BF)
        put_vec("b_inter", colsum(g_inter), FF_GROUP * g)
        put_b(g, dot(hidden_t[cols], g_inter))
        _, w_inter = wb(g)
        parts.append(dot_nt(g_inter, w_inter))
    g_hidden = (g_r2 + jnp.concatenate(parts, axis=1)).astype(BF).astype(F32)
    xh1 = xh1_ref[...]
    put_vec("gain_one", colsum(g_hidden * xh1))
    put_vec("shift_one", colsum(g_hidden))
    g_r1 = norm_back(g_hidden, xh1, rs1_ref[...], vector_of(vec_ref, "gain_one"))
    g_post = g_r1.astype(BF)
    put_vec("b_post", colsum(g_post))
    put_b(None, dot(ctx_ref[...].T, g_post))
    w_post, _ = wb(None)
    g_ctx = dot_nt(g_post, w_post).astype(BF)
    lane = lax.broadcasted_iota(jnp.int32, (ROWS, 128), 1)
    for pair in range(HEADS // 2):
        cols = slice(128 * pair, 128 * (pair + 1))
        qt, kt, vt, ct = q_ref[:, cols], k_ref[:, cols], v_ref[:, cols], g_ctx[:, cols]
        got = []
        for half in range(2):
            mine = (lane >= 64) if half else (lane < 64)
            cm = jnp.where(mine, ct, jnp.zeros_like(ct))
            p = p_ref[2 * pair + half]
            g_p = dot_nt(cm, vt)
            g_v = dot_tn(p.astype(BF), ct)
            g_s = (p * (g_p - jnp.sum(p * g_p, axis=-1, keepdims=True))).astype(BF)
            got.append((dot(g_s, kt) * 0.125, dot_tn(g_s, qt) * 0.125, g_v))
        gq_ref[:, cols] = jnp.where(lane < 64, got[0][0], got[1][0]).astype(BF)
        gk_ref[:, cols] = jnp.where(lane < 64, got[0][1], got[1][1]).astype(BF)
        gv_ref[:, cols] = jnp.where(lane < 64, got[0][2], got[1][2]).astype(BF)
    put_vec("b_qv", colsum(gq_ref[...]))
    put_vec("b_qv", colsum(gv_ref[...]), WIDTH)
    u_t = u_ref[...].T
    parts = []
    for g in range(4):
        cols = slice(GROUP * g, GROUP * (g + 1))
        gp = jnp.concatenate([gq_ref[:, cols], gk_ref[:, cols], gv_ref[:, cols]], axis=1)
        put_a(g, dot(u_t[cols], gp))
        parts.append(dot_nt(gp, wa(g)))
    gu_ref[...] = g_r1 + jnp.concatenate(parts, axis=1)


SIZE = 4
STRIDE = {"x": 16, "y": 4, "z": 1}
WORD_PART, WORD_STEP = 5120, 1280
ORDERS = (("z", "y", "x"), ("x", "z", "y"), ("y", "x", "z"))
VMEM = pl.BlockSpec(memory_space=pltpu.VMEM)
SMEM = pl.BlockSpec(memory_space=pltpu.SMEM)
HBM = pl.BlockSpec(memory_space=pl.ANY)
PARAMS = pltpu.CompilerParams(vmem_limit_bytes=56 << 20)


def spec_of(shape, dtype):
    return jax.ShapeDtypeStruct(shape, dtype)


def place_on(axis):
    return (lax.axis_index("dp") // STRIDE[axis]) % SIZE


def ring(block, axis, first_step, second_step):
    stride, route = STRIDE[axis], []
    for section, step in enumerate((first_step, second_step)):
        for chip in range(64):
            at = (chip // stride) % SIZE
            to = chip + ((at + step) % SIZE - at) * stride
            route.append((section * 64 + chip, section * 64 + to))
    return lax.ppermute(block, ("section", "dp"), route)


def cis(block, axis):
    return ring(block, axis, 1, -1)


def trans(block, axis):
    return ring(block, axis, -1, 1)


def swap(block):
    return lax.ppermute(block, "section", [(0, 1), (1, 0)])


def gather_stage(block, axis):
    near = cis(block, axis)
    other = trans(block, axis)
    return [block, near, other, cis(near, axis)]


def relative(axis):
    at = place_on(axis)
    sign = 1 - 2 * lax.axis_index("section")
    return [at, (at - sign) % SIZE, (at + sign) % SIZE, (at + 2) % SIZE]


def in_place(blocks, axis):
    which = relative(axis)
    ordered = []
    for spot in range(SIZE):
        picked = blocks[3]
        for number in range(3):
            picked = jnp.where(which[number] == spot, blocks[number], picked)
        ordered.append(picked)
    return ordered


def scatter_stage(blocks, axis):
    own, minus, plus, far = blocks
    first = cis(far, axis)
    third = trans(minus, axis)
    passed = (plus.astype(F32) + first.astype(F32)).astype(BF)
    second = cis(passed, axis)
    return own.astype(F32) + second.astype(F32) + third.astype(F32)


def stack_kernel(*refs):
    rows = refs[0].shape[0]
    for n in range(4):
        refs[4][n * rows : (n + 1) * rows] = refs[n][...]


def stack_rows(blocks):
    rows, columns = blocks[0].shape
    return pl.pallas_call(
        stack_kernel,
        grid=(columns // WORD_STEP,),
        out_shape=spec_of((4 * rows, columns), BF),
        in_specs=[pl.BlockSpec((rows, WORD_STEP), lambda i: (0, i))] * 4,
        out_specs=pl.BlockSpec((4 * rows, WORD_STEP), lambda i: (0, i)),
        name="stack_rows",
    )(*blocks)


def assemble_kernel(where_ref, *refs):
    ins, outs = refs[:12], refs[12:15]
    for n in range(4):
        outs[0][where_ref[0, n]] = ins[n][...]
        outs[1][:, where_ref[1, n]] = ins[4 + n][...]
        outs[2][:, where_ref[2, n]] = ins[8 + n][...]


A_SHAPE, B_SHAPE, C_SHAPE = (4, 192, 640), (4, 4, 48, 1536), (16, 4, 48, 192)


def assemble(blocks_a, blocks_b, blocks_c):
    where = jnp.stack([jnp.stack(relative(axis)) for axis in "xyz"]).astype(jnp.int32)
    return pl.pallas_call(
        assemble_kernel,
        out_shape=[spec_of(shape, BF) for shape in (A_SHAPE, B_SHAPE, C_SHAPE)],
        in_specs=[SMEM] + [VMEM] * 12,
        out_specs=[VMEM] * 3,
        compiler_params=PARAMS,
        name="assemble_weights",
    )(where, *blocks_a, *blocks_b, *blocks_c)


def fetch(layer, sec_ref, mine, other, held, sems):
    def bring(sources):
        copies = [pltpu.make_async_copy(sources[n], held[n], sems.at[n]) for n in range(3)]
        for copy in copies:
            copy.start()
        for copy in copies:
            copy.wait()

    @pl.when(sec_ref[0] == layer)
    def _():
        bring(mine)

    @pl.when(sec_ref[0] != layer)
    def _():
        bring(other)


def views(held):
    held_a, held_b, held_c = held

    def wa(g):
        return held_a[g][:, :576]

    def wb(g):
        if g is None:
            return held_b[...].reshape(WIDTH, 1536)[:, :WIDTH], None
        return None, held_b[g].reshape(GROUP, 1536)[:, WIDTH:]

    def wc(g):
        return held_c[4 * g : 4 * g + 4].reshape(FF_GROUP, GROUP)

    return wa, wb, wc


HELD = [pltpu.VMEM(shape, BF) for shape in (A_SHAPE, B_SHAPE, C_SHAPE)] + [pltpu.SemaphoreType.DMA((3,))]
KEPT = [
    spec_of((ROWS, WIDTH), BF),
    spec_of((ROWS, WIDTH), BF),
    spec_of((ROWS, WIDTH), BF),
    spec_of((HEADS, ROWS, ROWS), F32),
    spec_of((ROWS, WIDTH), BF),
    spec_of((ROWS, WIDTH), F32),
    spec_of((ROWS, 128), F32),
    spec_of((ROWS, WIDTH), BF),
    spec_of((ROWS, 4 * FF_GROUP), F32),
    spec_of((ROWS, WIDTH), F32),
    spec_of((ROWS, 128), F32),
]


def forward_kernel(layer, sec_ref, lengths_ref, u_ref, vec_ref, *refs):
    mine, other, outs, held, sems = refs[:3], refs[3:6], refs[6:18], refs[18:21], refs[21]
    fetch(layer, sec_ref, mine, other, held, sems)
    wa, wb, wc = views(held)
    source = jnp.where(sec_ref[0] == layer, 0, 1)
    layer_forward(u_ref, same_doc(lengths_ref, 2 * sec_ref[0]), wa, wb, wc, vec_ref.at[source], *outs)


def forward(layer, section, lengths, inputs, vectors, mine, other):
    outs = pl.pallas_call(
        functools.partial(forward_kernel, layer),
        out_shape=[spec_of((ROWS, WIDTH), BF)] + KEPT,
        in_specs=[SMEM, SMEM, VMEM, VMEM] + [HBM] * 6,
        out_specs=[VMEM] * 12,
        scratch_shapes=HELD,
        compiler_params=PARAMS,
        name="layer_forward",
    )(section, lengths, inputs, vectors, *mine, *other)
    return outs[0], outs[1:]


def backward_kernel(layer, sec_ref, gy_ref, u_ref, vec_ref, *refs):
    mine, other, kept = refs[:3], refs[3:6], refs[6:17]
    gu_ref, da_ref, db_ref, dc_ref = refs[17:21]
    held, sems, grads, gvec_ref, turned_ref = refs[21:24], refs[24], refs[25:28], refs[28], refs[29]
    fetch(layer, sec_ref, mine, other, held, sems)
    wa, wb, wc = views(held)

    def put_a(g, term):
        da_ref[g, :, :576] = term.astype(BF)

    def put_b(g, term):
        if g is None:
            db_ref[:, :, :, :WIDTH] = term.astype(BF).reshape(4, 4, 48, WIDTH)
        else:
            db_ref[g, :, :, WIDTH:] = term.astype(BF).reshape(4, 48, WIDTH)

    def put_c(g, term):
        dc_ref[4 * g : 4 * g + 4] = term.astype(BF).reshape(4, 4, 48, GROUP)

    source = jnp.where(sec_ref[0] == layer, 0, 1)
    gy = gy_ref[...].astype(BF).astype(F32) if layer == 0 else gy_ref[...]
    layer_backward(gy, u_ref, wa, wb, wc, vec_ref.at[source], *kept, gu_ref, put_a, put_b, put_c, gvec_ref, *grads)
    contract_into(gvec_ref, turned_ref, da_ref)


def backward(layer, section, gy, inputs, vectors, mine, other, kept):
    outs = pl.pallas_call(
        functools.partial(backward_kernel, layer),
        out_shape=[
            spec_of((ROWS, WIDTH), F32),
            spec_of(A_SHAPE, BF),
            spec_of(B_SHAPE, BF),
            spec_of(C_SHAPE, BF),
        ],
        in_specs=[SMEM, VMEM, VMEM, VMEM] + [HBM] * 6 + [VMEM] * 11,
        out_specs=[VMEM] * 4,
        scratch_shapes=HELD
        + [pltpu.VMEM((ROWS, WIDTH), BF)] * 3
        + [pltpu.VMEM((1, VECTOR), F32), pltpu.VMEM((128, WIDTH), F32)],
        compiler_params=PARAMS,
        name="layer_backward",
    )(section, gy, inputs, vectors, *mine, *other, *kept)
    return outs[0], outs[1:4]


def spreads():
    row = lax.broadcasted_iota(jnp.int32, (GROUP, 1), 0)
    device = row // 12
    within = row - 12 * device
    wide = [48 * device + within + 12 * n for n in range(4)]
    lane = lax.broadcasted_iota(jnp.int32, (GROUP, FF_GROUP), 1)
    inter = [(lane == target).astype(F32).astype(BF) for target in wide]
    row = lax.broadcasted_iota(jnp.int32, (96, 1), 0)
    device = row // 12
    within = row - 12 * device
    lane = lax.broadcasted_iota(jnp.int32, (96, GROUP), 1)
    heads = [(lane == 24 * device + within + 12 * n).astype(F32).astype(BF) for n in range(2)]
    return inter, heads


def expand_kernel(mine_ref, other_ref, out_ref):
    inter, heads = spreads()
    for source, ref in enumerate((mine_ref, other_ref)):
        turned = ref[...].reshape(WIDTH, 640)[:, 512:].astype(F32).T
        for name, (offset, width) in SHARD.items():
            at = PLACE[name][0]
            lane = 64 + offset // 12
            if name == "b_inter":
                for g in range(4):
                    rows = turned[lane : lane + 4, GROUP * g : GROUP * (g + 1)].astype(BF)
                    value = sum(dot(rows, inter[n])[n : n + 1] for n in range(4))
                    out_ref[source, :, at + FF_GROUP * g : at + FF_GROUP * (g + 1)] = value
            elif name == "b_qv":
                for e in range(8):
                    rows = turned[lane : lane + 2, 96 * e : 96 * (e + 1)].astype(BF)
                    value = sum(dot(rows, heads[n])[n : n + 1] for n in range(2))
                    out_ref[source, :, at + GROUP * e : at + GROUP * (e + 1)] = value
            else:
                out_ref[source, :, at : at + WIDTH] = turned[lane : lane + 1]


def expand(mine, other):
    return pl.pallas_call(
        expand_kernel,
        out_shape=spec_of((2, 1, VECTOR), F32),
        in_specs=[VMEM] * 2,
        out_specs=VMEM,
        compiler_params=PARAMS,
        name="expand_vectors",
    )(mine, other)


def contract_into(gvec_ref, turned_ref, da_ref):
    inter, heads = spreads()
    turned_ref[...] = jnp.zeros_like(turned_ref)
    for name, (offset, width) in SHARD.items():
        at = PLACE[name][0]
        lane = 64 + offset // 12
        if name == "b_inter":
            for g in range(4):
                value = gvec_ref[:, at + FF_GROUP * g : at + FF_GROUP * (g + 1)].astype(BF)
                for n in range(4):
                    turned_ref[lane + n : lane + n + 1, GROUP * g : GROUP * (g + 1)] = dot_nt(value, inter[n])
        elif name == "b_qv":
            for e in range(8):
                value = gvec_ref[:, at + GROUP * e : at + GROUP * (e + 1)].astype(BF)
                for n in range(2):
                    turned_ref[lane + n : lane + n + 1, 96 * e : 96 * (e + 1)] = dot_nt(value, heads[n])
        else:
            turned_ref[lane : lane + 1] = gvec_ref[:, at : at + WIDTH]
    columns = turned_ref[...].T.astype(BF)
    for g in range(4):
        da_ref[g, :, 576:] = columns[GROUP * g : GROUP * (g + 1), 64:]


def table_kernel(lhs_ref, grad_ref, *outs):
    for n in range(4):
        outs[n][...] = dot_nt(lhs_ref[GROUP * n : GROUP * (n + 1)], grad_ref[...]).astype(BF)


def table_terms(part, turned, logit_grad):
    steps = WORD_PART // WORD_STEP
    return pl.pallas_call(
        table_kernel,
        grid=(steps,),
        out_shape=[spec_of((GROUP, WORD_PART), BF)] * 4,
        in_specs=[
            pl.BlockSpec((WIDTH, 256), lambda i: (part, 0)),
            pl.BlockSpec((WORD_STEP, 256), lambda i: (steps * part + i, 0)),
        ],
        out_specs=[pl.BlockSpec((GROUP, WORD_STEP), lambda i: (0, i))] * 4,
        compiler_params=PARAMS,
        name="table_terms",
    )(turned, logit_grad)


def head_grad_kernel(part, words, grad_ref, *refs):
    ins, out_ref = refs[:4], refs[4]
    step = pl.program_id(0)
    grad = grad_ref[...]
    if (part + 1) * WORD_PART > words:
        column = lax.broadcasted_iota(jnp.int32, grad.shape, 0) + (part * WORD_PART + step * WORD_STEP)
        grad = jnp.where(column < words, grad, jnp.zeros_like(grad))

    @pl.when(step == 0)
    def _():
        out_ref[...] = jnp.zeros_like(out_ref)

    table = jnp.concatenate([block[...] for block in ins], axis=0)
    out_ref[...] += dot(table, grad)


def head_grad(part, logit_grad, blocks):
    steps = WORD_PART // WORD_STEP
    return pl.pallas_call(
        functools.partial(head_grad_kernel, part, logit_grad.shape[0]),
        grid=(steps,),
        out_shape=spec_of((WIDTH, 256), F32),
        in_specs=[pl.BlockSpec((WORD_STEP, 256), lambda i: (steps * part + i, 0))]
        + [pl.BlockSpec((GROUP, WORD_STEP), lambda i: (0, i))] * 4,
        out_specs=pl.BlockSpec((WIDTH, 256), lambda i: (0, 0)),
        compiler_params=PARAMS,
        name="head_grad",
    )(logit_grad, *blocks)


def unpermute_kernel(a_ref, b_ref, c_ref, pick_ref, out_ref):
    total = jnp.zeros((256, WIDTH), F32)
    for part, ref in enumerate((a_ref, b_ref, c_ref)):
        value = ref[...]
        high = value.astype(BF)
        rest = (value - high.astype(F32)).astype(BF)
        pick = pick_ref[WIDTH * part : WIDTH * (part + 1)]
        total = total + dot_tn(high, pick) + dot_tn(rest, pick)
    out_ref[...] = total


def unpermute(terms, pick):
    return pl.pallas_call(
        unpermute_kernel,
        out_shape=spec_of((256, WIDTH), F32),
        in_specs=[VMEM] * 4,
        out_specs=VMEM,
        compiler_params=PARAMS,
        name="unpermute",
    )(*terms, pick)


def logits_kernel(lhs_ref, *refs):
    ins, out_ref = refs[:4], refs[-1]
    table = jnp.concatenate([block[...] for block in ins], axis=0)
    out_ref[...] = dot(lhs_ref[...], table).astype(BF).T


def logits_part(part, straight, blocks, words, before):
    steps = WORD_PART // WORD_STEP
    extra = [] if before is None else [before]
    return pl.pallas_call(
        logits_kernel,
        grid=(steps,),
        out_shape=spec_of((words, 256), BF),
        in_specs=[pl.BlockSpec((256, WIDTH), lambda i: (0, part))]
        + [pl.BlockSpec((GROUP, WORD_STEP), lambda i: (0, i))] * 4
        + [HBM] * len(extra),
        out_specs=pl.BlockSpec((WORD_STEP, 256), lambda i: (steps * part + i, 0)),
        input_output_aliases={5: 0} if extra else {},
        compiler_params=PARAMS,
        name="logits",
    )(straight, *blocks, *extra)


def combine_kernel(sec_ref, where_ref, *refs):
    kept, came, outs = refs[:6], refs[6:12], refs[12:24]
    bufs, sems = refs[24:30], refs[30]

    def bring(layer):
        copies = []
        for n in range(3):
            copies.append(pltpu.make_async_copy(kept[3 * layer + n], bufs[n], sems.at[n]))
            copies.append(pltpu.make_async_copy(came[3 * layer + n], bufs[3 + n], sems.at[3 + n]))
        for copy in copies:
            copy.start()
        for copy in copies:
            copy.wait()

    @pl.when(sec_ref[0] == 0)
    def _():
        bring(0)

    @pl.when(sec_ref[0] != 0)
    def _():
        bring(1)

    def added(first, second):
        return (first.astype(F32) + second.astype(F32)).astype(BF)

    for n in range(4):
        a, b, c = where_ref[0, n], where_ref[1, n], where_ref[2, n]
        outs[n][...] = added(bufs[0][a], bufs[3][a])
        outs[4 + n][...] = added(bufs[1][:, b], bufs[4][:, b])
        outs[8 + n][...] = added(bufs[2][:, c], bufs[5][:, c])


def combine(section, kept, came):
    where = jnp.stack([jnp.stack(relative(axis)) for axis in "xyz"]).astype(jnp.int32)
    shapes = [(192, 640)] * 4 + [(4, 48, 1536)] * 4 + [(16, 48, 192)] * 4
    outs = pl.pallas_call(
        combine_kernel,
        out_shape=[spec_of(shape, BF) for shape in shapes],
        in_specs=[SMEM, SMEM] + [HBM] * 12,
        out_specs=[VMEM] * 12,
        scratch_shapes=[pltpu.VMEM(shape, BF) for shape in (A_SHAPE, B_SHAPE, C_SHAPE) * 2]
        + [pltpu.SemaphoreType.DMA((6,))],
        compiler_params=PARAMS,
        name="combine_grads",
    )(section, where, *kept, *came)
    return outs[:4], outs[4:8], outs[8:]


def feature_picks():
    picks = []
    for order in ORDERS:
        steps = [jnp.stack(relative(axis)) * (12 * STRIDE[axis]) for axis in order[::-1]]
        feature = (
            steps[0][:, None, None, None]
            + steps[1][None, :, None, None]
            + steps[2][None, None, :, None]
            + jnp.arange(12)[None, None, None, :]
        ).reshape(WIDTH)
        picks.append(feature)
    feature = jnp.concatenate(picks)
    return (feature[:, None] == jnp.arange(WIDTH)[None, :]).astype(BF)


def per_device(
    tokens, lengths, w_qkv, b_qv, w_post, b_post, gain_one, shift_one, w_inter, b_inter, w_out, b_out, gain_two, shift_two,
    embed_table, logit_grad,
):
    section_index = lax.axis_index("section")
    section = section_index.astype(jnp.int32)[None]
    is_first = section_index == 0
    words = embed_table.shape[1]
    given = dict(b_qv=b_qv, b_inter=b_inter, b_post=b_post, gain_one=gain_one, shift_one=shift_one, b_out=b_out, gain_two=gain_two, shift_two=shift_two)
    shard = jnp.concatenate([given[name][0].astype(BF) for name in SHARD]).reshape(12, 12).T

    both = jnp.concatenate([w_qkv[0].astype(BF), shard, jnp.zeros((12, 52), BF), w_post[0].astype(BF), w_inter[0].astype(BF)], axis=1)
    both = jnp.concatenate(in_place(gather_stage(both, "z"), "z"), axis=0)
    part_a = jnp.concatenate(in_place(gather_stage(both[:, :640], "y"), "y"), axis=0)
    part_b = jnp.stack(in_place(gather_stage(both[:, 640:], "x"), "x"), axis=0)
    part_c = jnp.stack(in_place(gather_stage(w_out[0].astype(BF), "y"), "y"), axis=0)
    part_c = jnp.concatenate(in_place(gather_stage(part_c, "x"), "x"), axis=0)
    mine = assemble(gather_stage(part_a, "x"), gather_stage(part_b, "y"), gather_stage(part_c, "z"))
    other = [swap(piece) for piece in mine]
    vectors = expand(mine[0], other[0])

    table_low = jnp.pad(embed_table.astype(BF), ((0, 0), (0, 3 * WORD_PART - words)))
    table = []
    for part, order in enumerate(ORDERS):
        rows = table_low[:, WORD_PART * part : WORD_PART * (part + 1)]
        rows = jnp.concatenate(gather_stage(rows, order[0]), axis=0)
        rows = stack_rows(gather_stage(rows, order[1]))
        table.append(gather_stage(rows, order[2]))

    inputs = lax.dynamic_slice_in_dim(tokens, section_index * ROWS, ROWS, 0)
    middle, kept_zero = forward(0, section, lengths, inputs, vectors, mine, other)
    top, kept_one = forward(1, section, lengths, middle, vectors, mine, other)

    pick = feature_picks()
    grad_turned = logit_grad.T
    top_other = swap(top)
    top_rows = jnp.concatenate([jnp.where(is_first, top, top_other), jnp.where(is_first, top_other, top)], axis=0)
    turned = dot_nt(pick, top_rows).astype(BF)
    straight = dot_nt(top_rows, pick).astype(BF)
    table_sums = []
    for part, order in enumerate(ORDERS):
        total = scatter_stage(table_terms(part, turned, grad_turned), order[2]).astype(BF)
        total = scatter_stage([total[48 * n : 48 * (n + 1)] for n in range(4)], order[1]).astype(BF)
        total = scatter_stage([total[12 * n : 12 * (n + 1)] for n in range(4)], order[0])
        table_sums.append(total)
    table_grad = jnp.concatenate(table_sums, axis=1)[:, :words]

    grad_rows = unpermute([head_grad(part, grad_turned, table[part]) for part in range(3)], pick)
    came = swap(lax.dynamic_slice_in_dim(grad_rows, (1 - section_index) * ROWS, ROWS, 0))
    grad_top = lax.dynamic_slice_in_dim(grad_rows, section_index * ROWS, ROWS, 0) + came
    grad_middle, terms_one = backward(1, section, grad_top, middle, vectors, mine, other, kept_one)
    came_one = [lax.ppermute(term, "section", [(0, 1)]) for term in terms_one]
    grad_inputs, terms_zero = backward(0, section, grad_middle, inputs, vectors, mine, other, kept_zero)
    came_zero = [lax.ppermute(term, "section", [(1, 0)]) for term in terms_zero]

    token_low = grad_inputs.astype(BF)
    half = WIDTH // 2
    own_half = lax.dynamic_slice_in_dim(token_low, section_index * half, half, 1)
    came_half = swap(lax.dynamic_slice_in_dim(token_low, (1 - section_index) * half, half, 1))
    token_out = jnp.concatenate([jnp.where(is_first, own_half, came_half), jnp.where(is_first, came_half, own_half)], axis=0)

    parts_a, parts_b, parts_c = combine(section, [*terms_zero, *terms_one], [*came_zero, *came_one])

    def picked(pieces, axis):
        return [lax.dynamic_index_in_dim(pieces, at, 0, keepdims=False) for at in relative(axis)]

    sum_a = scatter_stage(parts_a, "x").astype(BF)
    sum_b = scatter_stage(parts_b, "y").astype(BF)
    sum_c = scatter_stage(parts_c, "z").astype(BF)
    sum_a = scatter_stage(picked(sum_a.reshape(4, 48, 640), "y"), "y").astype(BF)
    sum_b = scatter_stage(picked(sum_b, "x"), "x").astype(BF)
    sum_c = scatter_stage(picked(sum_c.reshape(4, 4, 48, 192), "x"), "x").astype(BF)
    sum_c = scatter_stage(picked(sum_c, "y"), "y")
    sum_ab = jnp.concatenate([sum_a, sum_b], axis=1).reshape(4, 12, 640 + 1536)
    sum_ab = scatter_stage(picked(sum_ab, "z"), "z")

    sums = {"w_qkv": sum_ab[:, :576], "w_post": sum_ab[:, 640 : 640 + WIDTH], "w_inter": sum_ab[:, 640 + WIDTH :], "w_out": sum_c}
    vec_sums = sum_ab[:, 576:588].T
    for name, (offset, width) in SHARD.items():
        sums[name] = vec_sums[offset // 12 : (offset + width) // 12].reshape(width)
    names = ("w_qkv", "b_qv", "w_post", "b_post", "gain_one", "shift_one", "w_inter", "b_inter", "w_out", "b_out", "gain_two", "shift_two")
    logits = None
    for part in range(3):
        logits = logits_part(part, straight, table[part], words, logits)
    return (logits.T, token_out) + tuple(sums[name][None] for name in names) + (table_grad,)


def solution(mesh):
    matrix, vector = P("section", "dp", None), P("section", "dp")
    weights = (matrix, vector, matrix, vector, vector, vector, matrix, vector, matrix, vector, vector, vector)
    return jax.shard_map(
        per_device,
        mesh=mesh,
        in_specs=(P("dp", None), P("dp", None)) + weights + (P("dp", "section"), P("dp", "section")),
        out_specs=(P("dp", "section"), P("dp", "section")) + weights + (P("dp", "section"),),
        check_vma=False,
    )
```

```python
import functools
import jax
import jax.numpy as jnp
from jax import lax
from jax.experimental import pallas as pl
from jax.experimental.pallas import tpu as pltpu
from jax.sharding import PartitionSpec as P

BF = jnp.bfloat16
F32 = jnp.float32
ROWS, WIDTH, FF_GROUP, GROUP, HEADS = 128, 768, 768, 192, 12
SHARD = {
    "b_qv": (0, 24), "b_inter": (24, 48), "b_post": (72, 12), "gain_one": (84, 12),
    "shift_one": (96, 12), "b_out": (108, 12), "gain_two": (120, 12), "shift_two": (132, 12),
}
PLACE, _at = {}, 0
for _name, (_off, _width) in SHARD.items():
    PLACE[_name] = (_at, 64 * _width)
    _at += 64 * _width
VECTOR = _at


def dot(a, b):
    return lax.dot_general(a, b, (((1,), (0,)), ((), ())), preferred_element_type=F32)


def dot_nt(a, b):
    return lax.dot_general(a, b, (((1,), (1,)), ((), ())), preferred_element_type=F32)


def dot_tn(a, b):
    return lax.dot_general(a, b, (((0,), (0,)), ((), ())), preferred_element_type=F32)


def vector_of(vec_ref, name):
    at, size = PLACE[name]
    return vec_ref[:, at : at + size]


def norm_parts(values):
    mean = jnp.mean(values, axis=-1, keepdims=True)
    centred = values - mean
    scale = lax.rsqrt(jnp.mean(centred * centred, axis=-1, keepdims=True) + 1e-12)
    return centred * scale, scale


def same_doc(lengths_ref, first_row):
    row = lax.broadcasted_iota(jnp.int32, (ROWS, ROWS), 0)
    col = lax.broadcasted_iota(jnp.int32, (ROWS, ROWS), 1)
    row_id = jnp.zeros((ROWS, ROWS), jnp.int32)
    col_id = jnp.zeros((ROWS, ROWS), jnp.int32)
    for micro in range(2):
        end = micro * 64
        for doc in range(4):
            end = end + lengths_ref[first_row + micro, doc]
            row_id = row_id + (row >= end).astype(jnp.int32)
            col_id = col_id + (col >= end).astype(jnp.int32)
    return row_id == col_id


def gelu_parts(x):
    half = 0.5 * (1.0 + lax.erf(x * 0.7071067811865476))
    return half


def layer_forward(u_ref, same, wa, wb, wc, vec_ref, y_ref, q_ref, k_ref, v_ref, p_ref, ctx_ref, xh1_ref, rs1_ref, hid_ref, inter_ref, xh2_ref, rs2_ref):
    u = u_ref[...]
    for g in range(4):
        cols = slice(GROUP * g, GROUP * (g + 1))
        block = dot(u[:, cols], wa(g))
        b_q = vec_ref[:, PLACE["b_qv"][0] + GROUP * g : PLACE["b_qv"][0] + GROUP * (g + 1)]
        b_v = vec_ref[:, PLACE["b_qv"][0] + WIDTH + GROUP * g : PLACE["b_qv"][0] + WIDTH + GROUP * (g + 1)]
        q_ref[:, cols] = (block[:, :GROUP] + b_q).astype(BF)
        k_ref[:, cols] = block[:, GROUP : 2 * GROUP].astype(BF)
        v_ref[:, cols] = (block[:, 2 * GROUP : 3 * GROUP] + b_v).astype(BF)
    lane = lax.broadcasted_iota(jnp.int32, (ROWS, 128), 1)
    for pair in range(HEADS // 2):
        cols = slice(128 * pair, 128 * (pair + 1))
        qt, kt, vt = q_ref[:, cols], k_ref[:, cols], v_ref[:, cols]
        outs = []
        for half in range(2):
            mine = (lane >= 64) if half else (lane < 64)
            qm = jnp.where(mine, qt, jnp.zeros_like(qt))
            scores = jnp.where(same, dot_nt(qm, kt) * 0.125, -1e30)
            top = jnp.max(scores, axis=-1, keepdims=True)
            e = jnp.exp(scores - top)
            p = e / jnp.sum(e, axis=-1, keepdims=True)
            p_ref[2 * pair + half] = p
            outs.append(dot(p.astype(BF), vt))
        ctx_ref[:, cols] = jnp.where(lane < 64, outs[0], outs[1]).astype(BF)
    ctx = ctx_ref[...]
    w_post, _ = wb(None)
    r1 = dot(ctx, w_post) + vector_of(vec_ref, "b_post") + u.astype(F32)
    xh, rs = norm_parts(r1)
    xh1_ref[...] = xh
    rs1_ref[...] = jnp.broadcast_to(rs, (ROWS, 128))
    hidden = (xh * vector_of(vec_ref, "gain_one") + vector_of(vec_ref, "shift_one")).astype(BF)
    hid_ref[...] = hidden
    outs = []
    for g in range(4):
        cols = slice(GROUP * g, GROUP * (g + 1))
        _, w_inter = wb(g)
        at = PLACE["b_inter"][0] + FF_GROUP * g
        inter = dot(hidden[:, cols], w_inter) + vec_ref[:, at : at + FF_GROUP]
        inter_ref[:, FF_GROUP * g : FF_GROUP * (g + 1)] = inter
        act = (inter * gelu_parts(inter)).astype(BF)
        outs.append(dot(act, wc(g)))
    r2 = jnp.concatenate(outs, axis=1) + vector_of(vec_ref, "b_out") + hidden.astype(F32)
    xh, rs = norm_parts(r2)
    xh2_ref[...] = xh
    rs2_ref[...] = jnp.broadcast_to(rs, (ROWS, 128))
    y_ref[...] = (xh * vector_of(vec_ref, "gain_two") + vector_of(vec_ref, "shift_two")).astype(BF)


def norm_back(gy, xh, rs, gain):
    t = gy * gain
    m1 = jnp.mean(t, axis=-1, keepdims=True)
    m2 = jnp.mean(t * xh, axis=-1, keepdims=True)
    return rs[:, :1] * (t - m1 - xh * m2)


def layer_backward(gy, u_ref, wa, wb, wc, vec_ref, q_ref, k_ref, v_ref, p_ref, ctx_ref, xh1_ref, rs1_ref, hid_ref, inter_ref, xh2_ref, rs2_ref,
                   gu_ref, put_a, put_b, put_c, gvec_ref, gq_ref, gk_ref, gv_ref):
    def put_vec(name, row, start=0):
        at = PLACE[name][0] + start
        gvec_ref[:, at : at + row.shape[1]] = row

    def colsum(x):
        return jnp.sum(x.astype(F32), axis=0, keepdims=True)

    xh2 = xh2_ref[...]
    put_vec("gain_two", colsum(gy * xh2))
    put_vec("shift_two", colsum(gy))
    g_r2 = norm_back(gy, xh2, rs2_ref[...], vector_of(vec_ref, "gain_two"))
    g_out = g_r2.astype(BF)
    put_vec("b_out", colsum(g_out))
    hidden = hid_ref[...]
    hidden_t = hidden.T
    parts = []
    for g in range(4):
        cols = slice(GROUP * g, GROUP * (g + 1))
        wide = slice(FF_GROUP * g, FF_GROUP * (g + 1))
        inter = inter_ref[:, wide]
        half = gelu_parts(inter)
        act = (inter * half).astype(BF)
        slope = half + inter * (jnp.exp(-0.5 * inter * inter) * 0.3989422804014327)
        go = g_out[:, cols]
        put_c(g, dot(act.T, go))
        g_inter = (dot_nt(go, wc(g)) * slope).astype(BF)
        put_vec("b_inter", colsum(g_inter), FF_GROUP * g)
        put_b(g, dot(hidden_t[cols], g_inter))
        _, w_inter = wb(g)
        parts.append(dot_nt(g_inter, w_inter))
    g_hidden = (g_r2 + jnp.concatenate(parts, axis=1)).astype(BF).astype(F32)
    xh1 = xh1_ref[...]
    put_vec("gain_one", colsum(g_hidden * xh1))
    put_vec("shift_one", colsum(g_hidden))
    g_r1 = norm_back(g_hidden, xh1, rs1_ref[...], vector_of(vec_ref, "gain_one"))
    g_post = g_r1.astype(BF)
    put_vec("b_post", colsum(g_post))
    put_b(None, dot(ctx_ref[...].T, g_post))
    w_post, _ = wb(None)
    g_ctx = dot_nt(g_post, w_post).astype(BF)
    lane = lax.broadcasted_iota(jnp.int32, (ROWS, 128), 1)
    for pair in range(HEADS // 2):
        cols = slice(128 * pair, 128 * (pair + 1))
        qt, kt, vt, ct = q_ref[:, cols], k_ref[:, cols], v_ref[:, cols], g_ctx[:, cols]
        got = []
        for half in range(2):
            mine = (lane >= 64) if half else (lane < 64)
            cm = jnp.where(mine, ct, jnp.zeros_like(ct))
            p = p_ref[2 * pair + half]
            g_p = dot_nt(cm, vt)
            g_v = dot_tn(p.astype(BF), ct)
            g_s = (p * (g_p - jnp.sum(p * g_p, axis=-1, keepdims=True))).astype(BF)
            got.append((dot(g_s, kt) * 0.125, dot_tn(g_s, qt) * 0.125, g_v))
        gq_ref[:, cols] = jnp.where(lane < 64, got[0][0], got[1][0]).astype(BF)
        gk_ref[:, cols] = jnp.where(lane < 64, got[0][1], got[1][1]).astype(BF)
        gv_ref[:, cols] = jnp.where(lane < 64, got[0][2], got[1][2]).astype(BF)
    put_vec("b_qv", colsum(gq_ref[...]))
    put_vec("b_qv", colsum(gv_ref[...]), WIDTH)
    u_t = u_ref[...].T
    parts = []
    for g in range(4):
        cols = slice(GROUP * g, GROUP * (g + 1))
        gp = jnp.concatenate([gq_ref[:, cols], gk_ref[:, cols], gv_ref[:, cols]], axis=1)
        put_a(g, dot(u_t[cols], gp))
        parts.append(dot_nt(gp, wa(g)))
    gu_ref[...] = g_r1 + jnp.concatenate(parts, axis=1)


SIZE = 4
STRIDE = {"x": 16, "y": 4, "z": 1}
WORD_PART, WORD_STEP = 5120, 1280
STEPS = WORD_PART // WORD_STEP
ORDERS = (("z", "y", "x"), ("x", "z", "y"), ("y", "x", "z"))
VMEM = pl.BlockSpec(memory_space=pltpu.VMEM)
SMEM = pl.BlockSpec(memory_space=pltpu.SMEM)
HBM = pl.BlockSpec(memory_space=pl.ANY)
PARAMS = pltpu.CompilerParams(vmem_limit_bytes=56 << 20)
A_WIDTH, B_WIDTH = 1408, 1536
A_SHAPE, B_SHAPE = (4, GROUP, A_WIDTH), (4, 4, 48, B_WIDTH)


def cost(us):
    return pl.CostEstimate(flops=int(us * 1e8), bytes_accessed=int(us * 3.2e6), transcendentals=0)


def spec_of(shape, dtype):
    return jax.ShapeDtypeStruct(shape, dtype)


def place_on(axis):
    return (lax.axis_index("dp") // STRIDE[axis]) % SIZE


def exchange(block, axis, pairs):
    stride, route = STRIDE[axis], []
    for section in range(2):
        for chip in range(64):
            at = (chip // stride) % SIZE
            mate = at ^ 1 if section == pairs else SIZE - 1 - at
            route.append((section * 64 + chip, section * 64 + chip + (mate - at) * stride))
    return lax.ppermute(block, ("section", "dp"), route)


def near(block, axis):
    return exchange(block, axis, 0)


def next_near(block, axis):
    return exchange(block, axis, 1)


def swap(block):
    return lax.ppermute(block, "section", [(0, 1), (1, 0)])


def start_all(copies):
    for copy in copies:
        copy.start()


def wait_all(copies):
    for copy in copies:
        copy.wait()


def gather_pairs(block, axis, name, join):
    with jax.named_scope(name + "_" + axis + "_first"):
        first = near(block, axis)
    pair = join([block, first])
    with jax.named_scope(name + "_" + axis + "_second"):
        second = next_near(pair, axis)
    return pair, second


def scatter_pairs(kept, sent, axis, name):
    with jax.named_scope(name + "_" + axis + "_second"):
        came = next_near(sent, axis)
    half = kept.shape[0] // 2
    with jax.named_scope(name + "_" + axis + "_add"):
        passed = (kept[half:].astype(F32) + came[half:].astype(F32)).astype(BF)
    with jax.named_scope(name + "_" + axis + "_first"):
        last = near(passed, axis)
    return kept[:half], came[:half], last


def summed(blocks):
    return sum(block.astype(F32) for block in blocks)


def gather_stage(block, axis, name):
    with jax.named_scope(name + "_" + axis + "_first"):
        first = near(block, axis)
    with jax.named_scope(name + "_" + axis + "_second"):
        second = next_near(block, axis)
    with jax.named_scope(name + "_" + axis + "_across"):
        across = next_near(first, axis)
    return [block, first, second, across]


def relative(axis):
    at = place_on(axis)
    one, two = at ^ 1, SIZE - 1 - at
    is_first = lax.axis_index("section") == 0
    return [at, jnp.where(is_first, one, two), jnp.where(is_first, two, one), (at + 2) % SIZE]


def wheres():
    return jnp.stack([jnp.stack(relative(axis)) for axis in "xyz"]).astype(jnp.int32)


def in_place(blocks, axis):
    which = relative(axis)
    ordered = []
    for spot in range(SIZE):
        picked = blocks[3]
        for number in range(3):
            picked = jnp.where(which[number] == spot, blocks[number], picked)
        ordered.append(picked)
    return ordered


def picked(pieces, axis):
    return [lax.dynamic_index_in_dim(pieces, at, 0, keepdims=False) for at in relative(axis)]


def pair_kernel(first_ref, second_ref, out_ref, held_ref, in_sems, out_sems):
    rows, columns = first_ref.shape
    half = columns // 256 * 128
    lanes = [pl.ds(0, half), pl.ds(half, columns - half)]
    spots = [(n // 2, lanes[n % 2]) for n in range(4)]
    held = [held_ref.at[pl.ds(n * rows, rows), lane] for n, lane in spots]
    arrive = [pltpu.make_async_copy((first_ref, second_ref)[spots[n][0]].at[:, spots[n][1]], held[n], in_sems.at[n]) for n in range(4)]
    leave = [pltpu.make_async_copy(held[n], out_ref.at[pl.ds(spots[n][0] * rows, rows), spots[n][1]], out_sems.at[n]) for n in range(4)]
    start_all(arrive)
    for copy_in, copy_out in zip(arrive, leave, strict=True):
        copy_in.wait()
        copy_out.start()
    wait_all(leave)


def pair_rows(blocks):
    rows, columns = blocks[0].shape
    shape = (2 * rows, columns)
    return pl.pallas_call(
        pair_kernel,
        out_shape=spec_of(shape, BF),
        in_specs=[HBM] * 2,
        out_specs=HBM,
        scratch_shapes=[pltpu.VMEM(shape, BF), pltpu.SemaphoreType.DMA((4,)), pltpu.SemaphoreType.DMA((4,))],
        compiler_params=PARAMS,
        cost_estimate=cost(1.0),
        name="pair_rows",
    )(*blocks)


def stack_kernel(extra, where_ref, *refs):
    ins, outs, refs = refs[:2], refs[2 : 3 + (extra > 0)], refs[3 + (extra > 0) :]
    held_ref, in_sems, out_sems = refs[:3]
    spots = [pl.ds(n * 48, 48) for n in range(4)]
    sources = [ref.at[pl.ds(n * 48, 48)] for ref in ins for n in range(2)]
    arrive = [pltpu.make_async_copy(sources[n].at[:, pl.ds(0, WORD_PART)], held_ref.at[spots[n]], in_sems.at[n]) for n in range(4)]
    leave = [pltpu.make_async_copy(held_ref.at[spots[n]], outs[0].at[spots[n]], out_sems.at[n]) for n in range(4)]
    if extra:
        side_ref, side_in, side_out = refs[3:]
        for n in range(4):
            arrive.append(pltpu.make_async_copy(sources[n].at[:, pl.ds(WORD_PART, extra)], side_ref.at[n], side_in.at[n]))
            leave.append(pltpu.make_async_copy(side_ref.at[n], outs[1].at[where_ref[n]], side_out.at[n]))
    start_all(arrive)
    for copy_in, copy_out in zip(arrive, leave, strict=True):
        copy_in.wait()
        copy_out.start()
    wait_all(leave)


def stack_rows(blocks, axis):
    extra = blocks[0].shape[1] - WORD_PART
    sems = [pltpu.SemaphoreType.DMA((4,))] * 2
    more = [pltpu.VMEM((4, 48, extra), BF), *sems] if extra else []
    return pl.pallas_call(
        functools.partial(stack_kernel, extra),
        out_shape=[spec_of((GROUP, WORD_PART), BF)] + ([spec_of((4, 48, extra), BF)] if extra else []),
        in_specs=[SMEM] + [HBM] * 2,
        out_specs=[HBM] * (2 if extra else 1),
        scratch_shapes=[pltpu.VMEM((GROUP, WORD_PART), BF), *sems, *more],
        compiler_params=PARAMS,
        cost_estimate=cost(1.5),
        name="stack_rows",
    )(jnp.stack(relative(axis)).astype(jnp.int32), *blocks)


def unit_order():
    spot = lax.broadcasted_iota(jnp.int32, (1, FF_GROUP), 1)
    quarter = spot // GROUP
    rest = spot - GROUP * quarter
    device = rest // 12
    unit = 48 * device + 12 * quarter + (rest - 12 * device)
    row = lax.broadcasted_iota(jnp.int32, (FF_GROUP, FF_GROUP), 0)
    return (row == unit).astype(F32).astype(BF)


def pack_kernel(qkv_ref, post_ref, inter_ref, out_ref, *refs):
    vectors, packed_ref, held_ref, turned_ref = refs[:8], refs[8], refs[9], refs[10]
    held_ref[...] = jnp.zeros_like(held_ref)
    turned_ref[...] = jnp.zeros_like(turned_ref)
    for row in range(12):
        held_ref[row : row + 1, :576] = qkv_ref[row]
        held_ref[row : row + 1, 640:A_WIDTH] = post_ref[row]
        held_ref[row : row + 1, A_WIDTH : A_WIDTH + FF_GROUP] = inter_ref[row]
    for ref, (offset, width) in zip(vectors, SHARD.values(), strict=True):
        for n in range(width // 12):
            lane = 64 + offset // 12 + n
            turned_ref[lane : lane + 1, :12] = ref[:, 12 * n : 12 * (n + 1)]
    columns = turned_ref[...].T
    inter = dot(held_ref[:, A_WIDTH : A_WIDTH + FF_GROUP].astype(BF), unit_order())
    packed_ref[:, :576] = held_ref[:12, :576].astype(BF)
    packed_ref[:, 576:640] = columns[:12, 64:].astype(BF)
    packed_ref[:, 640:A_WIDTH] = held_ref[:12, 640:A_WIDTH].astype(BF)
    packed_ref[:, A_WIDTH : A_WIDTH + FF_GROUP] = inter[:12].astype(BF)
    for n in range(4):
        at = A_WIDTH + FF_GROUP + GROUP * n
        packed_ref[:, at : at + GROUP] = out_ref[12 * n : 12 * (n + 1)].astype(BF)


def pack(qkv, post, inter, out, vectors):
    return pl.pallas_call(
        pack_kernel,
        out_shape=spec_of((12, A_WIDTH + B_WIDTH), BF),
        in_specs=[VMEM] * 12,
        out_specs=VMEM,
        scratch_shapes=[pltpu.VMEM((16, A_WIDTH + FF_GROUP), F32), pltpu.VMEM((128, 128), F32)],
        compiler_params=PARAMS,
        cost_estimate=cost(2.0),
        name="pack_weights",
    )(qkv, post, inter, out, *vectors)


def unpack_kernel(own_ref, second_ref, third_ref, qkv_ref, post_ref, inter_ref, out_ref, *refs):
    vectors, turned_ref = refs[:8], refs[8]
    total = summed([own_ref[...], second_ref[...], third_ref[...]])
    units = total[:, A_WIDTH : A_WIDTH + FF_GROUP]
    order = unit_order()
    high = units.astype(BF)
    rest = units - high.astype(F32)
    middle = rest.astype(BF)
    last = (rest - middle.astype(F32)).astype(BF)
    inter = dot_nt(high, order) + dot_nt(middle, order) + dot_nt(last, order)
    for row in range(12):
        qkv_ref[row] = total[row : row + 1, :576]
        post_ref[row] = total[row : row + 1, 640:A_WIDTH]
        inter_ref[row] = inter[row : row + 1]
    for n in range(4):
        at = A_WIDTH + FF_GROUP + GROUP * n
        out_ref[12 * n : 12 * (n + 1)] = total[:, at : at + GROUP]
    turned_ref[...] = jnp.zeros_like(turned_ref)
    turned_ref[:12] = total[:, 512:640]
    columns = turned_ref[...].T
    for ref, (offset, width) in zip(vectors, SHARD.values(), strict=True):
        for n in range(width // 12):
            lane = 64 + offset // 12 + n
            ref[:, 12 * n : 12 * (n + 1)] = columns[lane : lane + 1, :12]


def unpack(blocks):
    shapes = [(12, 1, 576), (12, 1, WIDTH), (12, 1, WIDTH), (48, GROUP)] + [(1, width) for _, width in SHARD.values()]
    return pl.pallas_call(
        unpack_kernel,
        out_shape=[spec_of(shape, F32) for shape in shapes],
        in_specs=[VMEM] * 3,
        out_specs=[VMEM] * 12,
        scratch_shapes=[pltpu.VMEM((128, 128), F32)],
        compiler_params=PARAMS,
        cost_estimate=cost(2.0),
        name="unpack_grads",
    )(*blocks)


def assemble_kernel(where_ref, *refs):
    ins, outs = refs[:8], refs[8:]
    for n in range(4):
        outs[0][where_ref[0, n]] = ins[n][...]
        outs[1][:, where_ref[1, n]] = ins[4 + n][...]


def assemble(where, blocks_a, blocks_b):
    return pl.pallas_call(
        assemble_kernel,
        out_shape=[spec_of(shape, BF) for shape in (A_SHAPE, B_SHAPE)],
        in_specs=[SMEM] + [VMEM] * 8,
        out_specs=[VMEM] * 2,
        compiler_params=PARAMS,
        cost_estimate=cost(5.0),
        name="assemble_weights",
    )(where, *blocks_a, *blocks_b)


def fetch(layer, sec_ref, mine, other, held, sems):
    def bring(sources):
        copies = [pltpu.make_async_copy(sources[n], held[n], sems.at[n]) for n in range(2)]
        for copy in copies:
            copy.start()
        for copy in copies:
            copy.wait()

    @pl.when(sec_ref[0] == layer)
    def _():
        bring(mine)

    @pl.when(sec_ref[0] != layer)
    def _():
        bring(other)


def views(held):
    held_a, held_b = held

    def wa(g):
        return held_a[g][:, :576]

    def wb(g):
        if g is None:
            return held_a[...].reshape(WIDTH, A_WIDTH)[:, 640:], None
        return None, held_b[g].reshape(GROUP, B_WIDTH)[:, :FF_GROUP]

    def wc(g):
        block = held_b[g].reshape(GROUP, B_WIDTH)
        return jnp.concatenate([block[:, FF_GROUP + GROUP * q : FF_GROUP + GROUP * (q + 1)] for q in range(4)], axis=0)

    return wa, wb, wc


HELD = [pltpu.VMEM(shape, BF) for shape in (A_SHAPE, B_SHAPE)] + [pltpu.SemaphoreType.DMA((2,))]
KEPT = [
    spec_of((ROWS, WIDTH), BF),
    spec_of((ROWS, WIDTH), BF),
    spec_of((ROWS, WIDTH), BF),
    spec_of((HEADS, ROWS, ROWS), F32),
    spec_of((ROWS, WIDTH), BF),
    spec_of((ROWS, WIDTH), F32),
    spec_of((ROWS, 128), F32),
    spec_of((ROWS, WIDTH), BF),
    spec_of((ROWS, 4 * FF_GROUP), F32),
    spec_of((ROWS, WIDTH), F32),
    spec_of((ROWS, 128), F32),
]


def forward_kernel(layer, sec_ref, lengths_ref, u_ref, vec_ref, *refs):
    mine, other, outs, held, sems = refs[:2], refs[2:4], refs[4:16], refs[16:18], refs[18]
    fetch(layer, sec_ref, mine, other, held, sems)
    wa, wb, wc = views(held)
    source = jnp.where(sec_ref[0] == layer, 0, 1)
    layer_forward(u_ref, same_doc(lengths_ref, 2 * sec_ref[0]), wa, wb, wc, vec_ref.at[source], *outs)


def forward(layer, section, lengths, inputs, vectors, mine, other):
    outs = pl.pallas_call(
        functools.partial(forward_kernel, layer),
        out_shape=[spec_of((ROWS, WIDTH), BF)] + KEPT,
        in_specs=[SMEM, SMEM, VMEM, VMEM] + [HBM] * 4,
        out_specs=[VMEM] * 12,
        scratch_shapes=HELD,
        compiler_params=PARAMS,
        cost_estimate=cost(10.0),
        name="layer_forward",
    )(section, lengths, inputs, vectors, *mine, *other)
    return outs[0], outs[1:]


def backward_kernel(layer, sec_ref, gy_ref, u_ref, vec_ref, *refs):
    mine, other, kept = refs[:2], refs[2:4], refs[4:15]
    gu_ref, da_ref, db_ref = refs[15:18]
    held, sems, grads, gvec_ref, turned_ref = refs[18:20], refs[20], refs[21:24], refs[24], refs[25]
    fetch(layer, sec_ref, mine, other, held, sems)
    wa, wb, wc = views(held)

    def put_a(g, term):
        da_ref[g, :, :576] = term.astype(BF)

    def put_b(g, term):
        if g is None:
            da_ref[:, :, 640:] = term.astype(BF).reshape(4, GROUP, WIDTH)
        else:
            db_ref[g, :, :, :FF_GROUP] = term.astype(BF).reshape(4, 48, FF_GROUP)

    def put_c(g, term):
        low = term.astype(BF)
        for q in range(4):
            lanes = slice(FF_GROUP + GROUP * q, FF_GROUP + GROUP * (q + 1))
            db_ref[g, :, :, lanes] = low[GROUP * q : GROUP * (q + 1)].reshape(4, 48, GROUP)

    source = jnp.where(sec_ref[0] == layer, 0, 1)
    gy = gy_ref[...].astype(BF).astype(F32) if layer == 0 else gy_ref[...]
    layer_backward(gy, u_ref, wa, wb, wc, vec_ref.at[source], *kept, gu_ref, put_a, put_b, put_c, gvec_ref, *grads)
    contract_into(gvec_ref, turned_ref, da_ref)


def backward(layer, section, gy, inputs, vectors, mine, other, kept):
    outs = pl.pallas_call(
        functools.partial(backward_kernel, layer),
        out_shape=[spec_of((ROWS, WIDTH), F32), spec_of(A_SHAPE, BF), spec_of(B_SHAPE, BF)],
        in_specs=[SMEM, VMEM, VMEM, VMEM] + [HBM] * 4 + [VMEM] * 11,
        out_specs=[VMEM] * 3,
        scratch_shapes=HELD
        + [pltpu.VMEM((ROWS, WIDTH), BF)] * 3
        + [pltpu.VMEM((1, VECTOR), F32), pltpu.VMEM((128, WIDTH), F32)],
        compiler_params=PARAMS,
        cost_estimate=cost(15.0),
        name="layer_backward",
    )(section, gy, inputs, vectors, *mine, *other, *kept)
    return outs[0], outs[1:]


def spreads():
    row = lax.broadcasted_iota(jnp.int32, (96, 1), 0)
    device = row // 12
    within = row - 12 * device
    lane = lax.broadcasted_iota(jnp.int32, (96, GROUP), 1)
    return [(lane == 24 * device + within + 12 * n).astype(F32).astype(BF) for n in range(2)]


def expand_kernel(mine_ref, other_ref, out_ref):
    heads = spreads()
    for source, ref in enumerate((mine_ref, other_ref)):
        turned = ref[...].reshape(WIDTH, 128).astype(F32).T
        for name, (offset, width) in SHARD.items():
            at = PLACE[name][0]
            lane = 64 + offset // 12
            if name == "b_inter":
                for g in range(4):
                    for q in range(4):
                        spot = at + FF_GROUP * g + GROUP * q
                        out_ref[source, :, spot : spot + GROUP] = turned[lane + q : lane + q + 1, GROUP * g : GROUP * (g + 1)]
            elif name == "b_qv":
                for e in range(8):
                    rows = turned[lane : lane + 2, 96 * e : 96 * (e + 1)].astype(BF)
                    value = sum(dot(rows, heads[n])[n : n + 1] for n in range(2))
                    out_ref[source, :, at + GROUP * e : at + GROUP * (e + 1)] = value
            else:
                out_ref[source, :, at : at + WIDTH] = turned[lane : lane + 1]


def expand(mine, other):
    return pl.pallas_call(
        expand_kernel,
        grid=(1,),
        out_shape=spec_of((2, 1, VECTOR), F32),
        in_specs=[pl.BlockSpec((4, GROUP, 128), lambda i: (0, 0, 4))] * 2,
        out_specs=pl.BlockSpec((2, 1, VECTOR), lambda i: (0, 0, 0)),
        compiler_params=PARAMS,
        cost_estimate=cost(3.0),
        name="expand_vectors",
    )(mine, other)


def contract_into(gvec_ref, turned_ref, da_ref):
    heads = spreads()
    turned_ref[...] = jnp.zeros_like(turned_ref)
    for name, (offset, width) in SHARD.items():
        at = PLACE[name][0]
        lane = 64 + offset // 12
        if name == "b_inter":
            for g in range(4):
                for q in range(4):
                    spot = at + FF_GROUP * g + GROUP * q
                    turned_ref[lane + q : lane + q + 1, GROUP * g : GROUP * (g + 1)] = gvec_ref[:, spot : spot + GROUP]
        elif name == "b_qv":
            for e in range(8):
                value = gvec_ref[:, at + GROUP * e : at + GROUP * (e + 1)].astype(BF)
                for n in range(2):
                    turned_ref[lane + n : lane + n + 1, 96 * e : 96 * (e + 1)] = dot_nt(value, heads[n])
        else:
            turned_ref[lane : lane + 1] = gvec_ref[:, at : at + WIDTH]
    columns = turned_ref[...].T.astype(BF)
    for g in range(4):
        da_ref[g, :, 576:640] = columns[GROUP * g : GROUP * (g + 1), 64:]


def spread_kernel(sec_ref, mine_ref, other_ref, pick_ref, turned_ref, straight_ref, held_ref):
    mine, other = mine_ref[...].T, other_ref[...].T
    first = sec_ref[0] == 0
    held_ref[:, :ROWS] = jnp.where(first, mine, other)
    held_ref[:, ROWS:] = jnp.where(first, other, mine)
    turned_ref[...] = dot(pick_ref[...], held_ref[...]).astype(BF)
    straight_ref[...] = turned_ref[...].T


def spread_rows(section, mine, other, pick):
    return pl.pallas_call(
        spread_kernel,
        out_shape=[spec_of((3 * WIDTH, 256), BF), spec_of((256, 3 * WIDTH), BF)],
        in_specs=[SMEM] + [VMEM] * 3,
        out_specs=[VMEM] * 2,
        scratch_shapes=[pltpu.VMEM((WIDTH, 256), BF)],
        compiler_params=PARAMS,
        cost_estimate=cost(4.0),
        name="spread_rows",
    )(section, mine, other, pick)


def word_chunks(words):
    starts = [[part * WORD_PART + step * WORD_STEP for step in range(STEPS)] for part in range(3)]
    return [[(start, min(WORD_STEP, words - start)) for start in part] for part in starts]


def grad_copies(grad_ref, held_ref, sems, words):
    copies = []
    for part, chunks in enumerate(word_chunks(words)):
        copies.append(
            [
                pltpu.make_async_copy(
                    grad_ref.at[pl.ds(start, size)],
                    held_ref.at[part % 2, pl.ds(step * WORD_STEP, size)],
                    sems.at[part % 2, step],
                )
                for step, (start, size) in enumerate(chunks)
            ]
        )
    return copies


def clear_rest(held_ref, part, words):
    used = min(WORD_PART, words - part * WORD_PART)
    if used < WORD_PART:
        held_ref[part % 2, used:] = jnp.zeros((WORD_PART - used, 256), BF)


def send_kernel(lhs_ref, grad_ref, *refs):
    outs, grad_buf, out_buf, grad_sems, out_sems = refs[:6], refs[6], refs[7], refs[8], refs[9]
    words = grad_ref.shape[0]
    arrive = grad_copies(grad_ref, grad_buf, grad_sems, words)
    leave = []
    start_all(arrive[0])
    start_all(arrive[1])
    for part in range(3):
        for step in range(STEPS):
            at = part * STEPS + step
            slot = at % 3
            columns = pl.ds(step * WORD_STEP, WORD_STEP)
            arrive[part][step].wait()
            if step == STEPS - 1:
                clear_rest(grad_buf, part, words)
            if at >= 3:
                wait_all(leave[at - 3])
            spot = slice(WIDTH * part + 2 * GROUP, WIDTH * (part + 1))
            term = dot_nt(lhs_ref[spot], grad_buf[part % 2, columns])
            for n in range(2):
                out_buf[slot, n] = term[GROUP * n : GROUP * (n + 1)].astype(BF)
            leave.append(
                [
                    pltpu.make_async_copy(out_buf.at[slot, n], outs[2 * part + n].at[:, columns], out_sems.at[slot, n])
                    for n in range(2)
                ]
            )
            start_all(leave[at])
        if part == 0:
            start_all(arrive[2])
    for copies in leave[-3:]:
        wait_all(copies)


def table_send(turned, logit_grad):
    return pl.pallas_call(
        send_kernel,
        out_shape=[spec_of((GROUP, WORD_PART), BF)] * 6,
        in_specs=[VMEM, HBM],
        out_specs=[HBM] * 6,
        scratch_shapes=[
            pltpu.VMEM((2, WORD_PART, 256), BF),
            pltpu.VMEM((3, 2, GROUP, WORD_STEP), BF),
            pltpu.SemaphoreType.DMA((2, STEPS)),
            pltpu.SemaphoreType.DMA((3, 2)),
        ],
        compiler_params=PARAMS,
        cost_estimate=cost(8.0),
        name="table_send",
    )(turned, logit_grad)


def term_kernel(part, extra, pieces, lhs_ref, grad_ref, *refs):
    added, outs = refs[:extra], refs[extra : extra + pieces]
    grad_buf, add_buf, out_buf, grad_sems, add_sems, out_sems = refs[extra + pieces :]
    words = grad_ref.shape[0]
    chunks = word_chunks(words)[part]
    rows = GROUP // pieces
    grads, adds, leave = [], [], []
    for step, (start, size) in enumerate(chunks):
        columns = pl.ds(step * WORD_STEP, WORD_STEP)
        grads.append(pltpu.make_async_copy(grad_ref.at[pl.ds(start, size)], grad_buf.at[step, pl.ds(0, size)], grad_sems.at[step]))
        adds.append([pltpu.make_async_copy(added[n].at[:, columns], add_buf.at[step, n], add_sems.at[step, n]) for n in range(extra)])
        leave.append(
            [
                pltpu.make_async_copy(out_buf.at[step, pl.ds(n * rows, rows)], outs[n].at[:, columns], out_sems.at[step, n])
                for n in range(pieces)
            ]
        )
        grads[step].start()
        start_all(adds[step])
    for step, (start, size) in enumerate(chunks):
        grads[step].wait()
        if size < WORD_STEP:
            grad_buf[step, size:] = jnp.zeros((WORD_STEP - size, 256), BF)
        total = dot_nt(lhs_ref[...], grad_buf[step])
        wait_all(adds[step])
        for n in range(extra):
            total = total + add_buf[step, n].astype(F32)
        out_buf[step] = total.astype(BF)
        start_all(leave[step])
    for copies in leave:
        wait_all(copies)


def table_term(part, block, turned, logit_grad, added, pieces):
    extra = len(added)
    rows = GROUP // pieces
    return pl.pallas_call(
        functools.partial(term_kernel, part, extra, pieces),
        grid=(1,),
        out_shape=[spec_of((rows, WORD_PART), BF)] * pieces,
        in_specs=[pl.BlockSpec((GROUP, 256), lambda i: (4 * part + block, 0))] + [HBM] * (1 + extra),
        out_specs=[HBM] * pieces,
        scratch_shapes=[
            pltpu.VMEM((STEPS, WORD_STEP, 256), BF),
            pltpu.VMEM((STEPS, extra, GROUP, WORD_STEP), BF),
            pltpu.VMEM((STEPS, GROUP, WORD_STEP), BF),
            pltpu.SemaphoreType.DMA((STEPS,)),
            pltpu.SemaphoreType.DMA((STEPS, extra)),
            pltpu.SemaphoreType.DMA((STEPS, pieces)),
        ],
        compiler_params=PARAMS,
        cost_estimate=cost(4.0),
        name="table_term",
    )(turned, logit_grad, *added)


def table_copies(ins, held_ref, sems):
    return [
        [
            pltpu.make_async_copy(ins[4 * part + n], held_ref.at[part % 2, pl.ds(GROUP * n, GROUP)], sems.at[part % 2, n])
            for n in range(4)
        ]
        for part in range(3)
    ]


def head_grad_kernel(grad_ref, pick_ref, *refs):
    ins, out_ref, total_ref, table_buf, grad_buf, table_sems, grad_sems = refs[:12], *refs[12:]
    words = grad_ref.shape[0]
    rows = [
        [
            pltpu.make_async_copy(ins[4 * part + n], table_buf.at[part, pl.ds(GROUP * n, GROUP)], table_sems.at[part, n])
            for n in range(4)
        ]
        for part in range(3)
    ]
    grads = grad_copies(grad_ref, grad_buf, grad_sems, words)
    for part in range(3):
        if part < 2:
            start_all(grads[part])
        start_all(rows[part])
    for part in range(3):
        wait_all(grads[part])
        clear_rest(grad_buf, part, words)
        wait_all(rows[part])
        term = dot(table_buf[part], grad_buf[part % 2])
        if part == 0:
            start_all(grads[2])
        placed = dot(pick_ref[:, WIDTH * part : WIDTH * (part + 1)], term.astype(BF))
        if part == 0:
            total_ref[...] = placed
        else:
            total_ref[...] += placed
    out_ref[...] = total_ref[...].T


def head_grad(logit_grad, pick, table):
    return pl.pallas_call(
        head_grad_kernel,
        out_shape=spec_of((256, WIDTH), F32),
        in_specs=[HBM, VMEM] + [HBM] * 12,
        out_specs=VMEM,
        scratch_shapes=[
            pltpu.VMEM((WIDTH, 256), F32),
            pltpu.VMEM((3, WIDTH, WORD_PART), BF),
            pltpu.VMEM((2, WORD_PART, 256), BF),
            pltpu.SemaphoreType.DMA((3, 4)),
            pltpu.SemaphoreType.DMA((2, STEPS)),
        ],
        compiler_params=PARAMS,
        cost_estimate=cost(16.0),
        name="head_grad",
    )(logit_grad, pick, *[block for blocks in table for block in blocks])


def logits_kernel(lhs_ref, *refs):
    ins, out_ref, table_buf, out_buf, table_sems, out_sems = refs[:12], *refs[12:]
    chunks = word_chunks(out_ref.shape[0])
    rows = table_copies(ins, table_buf, table_sems)
    leave = []
    start_all(rows[0])
    start_all(rows[1])
    for part in range(3):
        wait_all(rows[part])
        for step, (start, size) in enumerate(chunks[part]):
            at = part * STEPS + step
            slot = at % 3
            if at >= 3:
                leave[at - 3].wait()
            columns = slice(step * WORD_STEP, (step + 1) * WORD_STEP)
            lhs = lhs_ref[:, WIDTH * part : WIDTH * (part + 1)]
            out_buf[slot] = dot(lhs, table_buf[part % 2, :, columns]).astype(BF).T
            leave.append(pltpu.make_async_copy(out_buf.at[slot, pl.ds(0, size)], out_ref.at[pl.ds(start, size)], out_sems.at[slot]))
            leave[at].start()
        if part == 0:
            start_all(rows[2])
    wait_all(leave[-3:])


def logits_of(straight, table, words):
    return pl.pallas_call(
        logits_kernel,
        out_shape=spec_of((words, 256), BF),
        in_specs=[VMEM] + [HBM] * 12,
        out_specs=HBM,
        scratch_shapes=[
            pltpu.VMEM((2, WIDTH, WORD_PART), BF),
            pltpu.VMEM((3, WORD_STEP, 256), BF),
            pltpu.SemaphoreType.DMA((2, 4)),
            pltpu.SemaphoreType.DMA((3,)),
        ],
        compiler_params=PARAMS,
        cost_estimate=cost(14.0),
        name="logits",
    )(straight, *[block for blocks in table for block in blocks])


def combine_kernel(sec_ref, where_ref, *refs):
    kept, came, outs = refs[:4], refs[4:8], refs[8:12]
    bufs, sems = refs[12:16], refs[16]

    def bring(layer):
        copies = []
        for n in range(2):
            copies.append(pltpu.make_async_copy(kept[2 * layer + n], bufs[n], sems.at[n]))
            copies.append(pltpu.make_async_copy(came[2 * layer + n], bufs[2 + n], sems.at[2 + n]))
        for copy in copies:
            copy.start()
        for copy in copies:
            copy.wait()

    @pl.when(sec_ref[0] == 0)
    def _():
        bring(0)

    @pl.when(sec_ref[0] != 0)
    def _():
        bring(1)

    def added(first, second):
        return (first.astype(F32) + second.astype(F32)).astype(BF)

    for n in range(4):
        a, b = where_ref[0, n], where_ref[1, n]
        outs[n // 2][n % 2] = added(bufs[0][a], bufs[2][a])
        outs[2 + n // 2][n % 2] = added(bufs[1][:, b], bufs[3][:, b])


def combine(section, where, kept, came):
    shapes = [(2, GROUP, A_WIDTH)] * 2 + [(2, 4, 48, B_WIDTH)] * 2
    outs = pl.pallas_call(
        combine_kernel,
        out_shape=[spec_of(shape, BF) for shape in shapes],
        in_specs=[SMEM, SMEM] + [HBM] * 8,
        out_specs=[VMEM] * 4,
        scratch_shapes=[pltpu.VMEM(shape, BF) for shape in (A_SHAPE, B_SHAPE) * 2] + [pltpu.SemaphoreType.DMA((4,))],
        compiler_params=PARAMS,
        cost_estimate=cost(8.0),
        name="combine_grads",
    )(section, where, *kept, *came)
    return outs


def feature_picks():
    picks = []
    for order in ORDERS:
        steps = [jnp.stack(relative(axis)) * (12 * STRIDE[axis]) for axis in order[::-1]]
        feature = (
            steps[0][:, None, None, None]
            + steps[1][None, :, None, None]
            + steps[2][None, None, :, None]
            + jnp.arange(12)[None, None, None, :]
        ).reshape(WIDTH)
        picks.append(feature)
    feature = jnp.concatenate(picks)
    row = jnp.arange(WIDTH)
    return (feature[:, None] == row[None, :]).astype(BF), (row[:, None] == feature[None, :]).astype(BF)


def tied(values, *others):
    return lax.optimization_barrier((values, *others))[0]


def per_device(
    tokens, lengths, w_qkv, b_qv, w_post, b_post, gain_one, shift_one, w_inter, b_inter, w_out, b_out, gain_two, shift_two,
    embed_table, logit_grad,
):
    section_index = lax.axis_index("section")
    section = section_index.astype(jnp.int32)[None]
    is_first = section_index == 0
    words = embed_table.shape[1]
    where = wheres()
    given = dict(b_qv=b_qv, b_inter=b_inter, b_post=b_post, gain_one=gain_one, shift_one=shift_one, b_out=b_out, gain_two=gain_two, shift_two=shift_two)

    grad_turned = logit_grad.T
    turn = (1, 0, 2)

    packed = pack(
        w_qkv.transpose(turn), w_post.transpose(turn), w_inter.transpose(turn), w_out[0], [given[name] for name in SHARD]
    )
    table_low = jnp.pad(embed_table.astype(BF), ((0, 0), (0, 3 * WORD_PART - words)))
    names = ["table_a", "table_b", "table_c"]
    rows = [table_low[:, WORD_PART * part : WORD_PART * (part + 1)] for part in range(3)]

    def low_join(blocks):
        return jnp.concatenate(blocks, axis=0)

    rows[0] = jnp.concatenate([rows[0], packed], axis=1)
    names[0] = "table_weights"
    for part in range(3):
        pairs = gather_pairs(rows[part], ORDERS[part][0], names[part], low_join)
        if part == 0:
            quarters = [pair[12 * n : 12 * (n + 1), WORD_PART:] for pair in pairs for n in range(2)]
            weights = low_join(in_place(quarters, "z"))
            pairs = [pair[:, :WORD_PART] for pair in pairs]
        rows[part] = low_join(pairs)
    rows[0] = jnp.concatenate([rows[0], weights[:, :A_WIDTH]], axis=1)
    rows[2] = jnp.concatenate([rows[2], weights[:, A_WIDTH:]], axis=1)
    names = ["table_a", "table_b", "table_c"]
    stacked = [
        stack_rows(gather_pairs(rows[part], ORDERS[part][1], names[part], pair_rows), ORDERS[part][1]) for part in (0, 2, 1)
    ]
    blocks_a = gather_stage(stacked[0][1].reshape(GROUP, A_WIDTH), "x", "weights_a")
    blocks_b = gather_stage(stacked[1][1], "y", "weights_b")
    mine = assemble(where, blocks_a, blocks_b)
    with jax.named_scope("weights_swap"):
        other = [swap(piece) for piece in mine]
    vectors = expand(mine[0], other[0])
    rows = [stacked[0][0], stacked[2][0], stacked[1][0]]
    rows[0] = tied(rows[0], blocks_a[1], blocks_a[2])
    rows[1] = tied(rows[1], blocks_b[1], blocks_b[2])
    table = [gather_stage(rows[part], ORDERS[part][2], names[part]) for part in range(3)]
    pick, pick_turned = feature_picks()

    inputs = lax.dynamic_slice_in_dim(tokens, section_index * ROWS, ROWS, 0)
    inputs = tied(inputs, *[blocks[1] for blocks in table])
    middle, kept_zero = forward(0, section, lengths, inputs, vectors, mine, other)
    top, kept_one = forward(1, section, lengths, middle, vectors, mine, other)

    with jax.named_scope("top_swap"):
        top_other = swap(top)
    turned, straight = spread_rows(section, top, top_other, pick)
    leaving = table_send(turned, grad_turned)
    names = ["grad_a", "grad_b", "grad_c"]
    passed, direct = [], []
    for part in range(3):
        axis = ORDERS[part][2]
        with jax.named_scope(names[part] + "_" + axis + "_across"):
            came = next_near(leaving[2 * part + 1], axis)
        with jax.named_scope(names[part] + "_" + axis + "_second"):
            direct.append(next_near(leaving[2 * part], axis))
        passed.append(table_term(part, 1, turned, grad_turned, [came], 1)[0])
    sums = []
    for part in range(3):
        axis = ORDERS[part][2]
        with jax.named_scope(names[part] + "_" + axis + "_first"):
            onward = near(passed[part], axis)
        pieces = table_term(part, 0, turned, grad_turned, [onward, direct[part]], 2)
        whole = summed(scatter_pairs(*pieces, ORDERS[part][1], names[part])).astype(BF)
        sums.append(summed(scatter_pairs(whole[:24], whole[24:], ORDERS[part][0], names[part])))
    table_grad = jnp.concatenate(sums, axis=1)[:, :words]

    grad_rows = head_grad(tied(grad_turned, *leaving), pick_turned, table)
    with jax.named_scope("head_swap"):
        came = swap(lax.dynamic_slice_in_dim(grad_rows, (1 - section_index) * ROWS, ROWS, 0))
    grad_top = lax.dynamic_slice_in_dim(grad_rows, section_index * ROWS, ROWS, 0) + came
    grad_middle, terms_one = backward(1, section, grad_top, middle, vectors, mine, other, kept_one)
    with jax.named_scope("one_swap"):
        came_one = [swap(term) for term in terms_one]
    grad_middle = tied(grad_middle, *passed)
    grad_inputs, terms_zero = backward(0, section, grad_middle, inputs, vectors, mine, other, kept_zero)
    with jax.named_scope("zero_swap"):
        came_zero = [swap(term) for term in terms_zero]

    token_low = grad_inputs.astype(BF)
    half = WIDTH // 2
    own_half = lax.dynamic_slice_in_dim(token_low, section_index * half, half, 1)
    with jax.named_scope("token_swap"):
        came_half = swap(lax.dynamic_slice_in_dim(token_low, (1 - section_index) * half, half, 1))
    token_out = jnp.concatenate([jnp.where(is_first, own_half, came_half), jnp.where(is_first, came_half, own_half)], axis=0)

    kept_a, sent_a, kept_b, sent_b = combine(section, where, [*terms_zero, *terms_one], [*came_zero, *came_one])

    def again(whole, axis):
        places = picked(whole, axis)
        return jnp.stack(places[:2]), jnp.stack(places[2:])

    sum_a = summed(scatter_pairs(kept_a, sent_a, "x", "sum_a")).astype(BF).reshape(4, 48, A_WIDTH)
    sum_b = summed(scatter_pairs(kept_b, sent_b, "y", "sum_b")).astype(BF)[0]
    sum_a = summed(scatter_pairs(*again(sum_a, "y"), "y", "sum_a")).astype(BF)
    sum_b = summed(scatter_pairs(*again(sum_b, "x"), "x", "sum_b")).astype(BF)
    both = jnp.concatenate([sum_a, sum_b], axis=2).reshape(4, 12, A_WIDTH + B_WIDTH)
    pieces = scatter_pairs(*again(both, "z"), "z", "sum")
    g_qkv, g_post, g_inter, g_out, *g_vectors = unpack([piece[0] for piece in pieces])
    sums = dict(zip(SHARD, g_vectors, strict=True))
    sums.update(w_qkv=g_qkv.transpose(turn), w_post=g_post.transpose(turn), w_inter=g_inter.transpose(turn), w_out=g_out[None])
    names = ("w_qkv", "b_qv", "w_post", "b_post", "gain_one", "shift_one", "w_inter", "b_inter", "w_out", "b_out", "gain_two", "shift_two")
    logits = logits_of(tied(straight, kept_a), table, words)
    return (logits.T, token_out) + tuple(sums[name] for name in names) + (table_grad,)


def solution(mesh):
    matrix, vector = P("section", "dp", None), P("section", "dp")
    weights = (matrix, vector, matrix, vector, vector, vector, matrix, vector, matrix, vector, vector, vector)
    return jax.shard_map(
        per_device,
        mesh=mesh,
        in_specs=(P("dp", None), P("dp", None)) + weights + (P("dp", "section"), P("dp", "section")),
        out_specs=(P("dp", "section"), P("dp", "section")) + weights + (P("dp", "section"),),
        check_vma=False,
    )
```

```python
import functools
import jax
import jax.numpy as jnp
from jax import lax
from jax.experimental import pallas as pl
from jax.experimental.pallas import tpu as pltpu
from jax.sharding import PartitionSpec as P

BF = jnp.bfloat16
F32 = jnp.float32
ROWS, WIDTH, FF_GROUP, GROUP, HEADS = 128, 768, 768, 192, 12
SHARD = {
    "b_qv": (0, 24), "b_inter": (24, 48), "b_post": (72, 12), "gain_one": (84, 12),
    "shift_one": (96, 12), "b_out": (108, 12), "gain_two": (120, 12), "shift_two": (132, 12),
}
PLACE, _at = {}, 0
for _name, (_off, _width) in SHARD.items():
    PLACE[_name] = (_at, 64 * _width)
    _at += 64 * _width
VECTOR = _at


def dot(a, b):
    return lax.dot_general(a, b, (((1,), (0,)), ((), ())), preferred_element_type=F32)


def dot_nt(a, b):
    return lax.dot_general(a, b, (((1,), (1,)), ((), ())), preferred_element_type=F32)


def dot_tn(a, b):
    return lax.dot_general(a, b, (((0,), (0,)), ((), ())), preferred_element_type=F32)


def vector_of(vec_ref, name):
    at, size = PLACE[name]
    return vec_ref[:, at : at + size]


def norm_parts(values):
    mean = jnp.mean(values, axis=-1, keepdims=True)
    centred = values - mean
    scale = lax.rsqrt(jnp.mean(centred * centred, axis=-1, keepdims=True) + 1e-12)
    return centred * scale, scale


def same_doc(lengths_ref, first_row):
    row = lax.broadcasted_iota(jnp.int32, (ROWS, ROWS), 0)
    col = lax.broadcasted_iota(jnp.int32, (ROWS, ROWS), 1)
    row_id = jnp.zeros((ROWS, ROWS), jnp.int32)
    col_id = jnp.zeros((ROWS, ROWS), jnp.int32)
    for micro in range(2):
        end = micro * 64
        for doc in range(4):
            end = end + lengths_ref[first_row + micro, doc]
            row_id = row_id + (row >= end).astype(jnp.int32)
            col_id = col_id + (col >= end).astype(jnp.int32)
    return row_id == col_id


def gelu_parts(x):
    half = 0.5 * (1.0 + lax.erf(x * 0.7071067811865476))
    return half


def layer_forward(u_ref, same, wa, wb, wc, vec_ref, y_ref, q_ref, k_ref, v_ref, p_ref, ctx_ref, xh1_ref, rs1_ref, hid_ref, inter_ref, xh2_ref, rs2_ref):
    u = u_ref[...]
    for g in range(4):
        cols = slice(GROUP * g, GROUP * (g + 1))
        block = dot(u[:, cols], wa(g))
        b_q = vec_ref[:, PLACE["b_qv"][0] + GROUP * g : PLACE["b_qv"][0] + GROUP * (g + 1)]
        b_v = vec_ref[:, PLACE["b_qv"][0] + WIDTH + GROUP * g : PLACE["b_qv"][0] + WIDTH + GROUP * (g + 1)]
        q_ref[:, cols] = (block[:, :GROUP] + b_q).astype(BF)
        k_ref[:, cols] = block[:, GROUP : 2 * GROUP].astype(BF)
        v_ref[:, cols] = (block[:, 2 * GROUP : 3 * GROUP] + b_v).astype(BF)
    lane = lax.broadcasted_iota(jnp.int32, (ROWS, 128), 1)
    for pair in range(HEADS // 2):
        cols = slice(128 * pair, 128 * (pair + 1))
        qt, kt, vt = q_ref[:, cols], k_ref[:, cols], v_ref[:, cols]
        outs = []
        for half in range(2):
            mine = (lane >= 64) if half else (lane < 64)
            qm = jnp.where(mine, qt, jnp.zeros_like(qt))
            scores = jnp.where(same, dot_nt(qm, kt) * 0.125, -1e30)
            top = jnp.max(scores, axis=-1, keepdims=True)
            e = jnp.exp(scores - top)
            p = e / jnp.sum(e, axis=-1, keepdims=True)
            p_ref[2 * pair + half] = p
            outs.append(dot(p.astype(BF), vt))
        ctx_ref[:, cols] = jnp.where(lane < 64, outs[0], outs[1]).astype(BF)
    ctx = ctx_ref[...]
    w_post, _ = wb(None)
    r1 = dot(ctx, w_post) + vector_of(vec_ref, "b_post") + u.astype(F32)
    xh, rs = norm_parts(r1)
    xh1_ref[...] = xh
    rs1_ref[...] = jnp.broadcast_to(rs, (ROWS, 128))
    hidden = (xh * vector_of(vec_ref, "gain_one") + vector_of(vec_ref, "shift_one")).astype(BF)
    hid_ref[...] = hidden
    outs = []
    for g in range(4):
        cols = slice(GROUP * g, GROUP * (g + 1))
        _, w_inter = wb(g)
        at = PLACE["b_inter"][0] + FF_GROUP * g
        inter = dot(hidden[:, cols], w_inter) + vec_ref[:, at : at + FF_GROUP]
        inter_ref[:, FF_GROUP * g : FF_GROUP * (g + 1)] = inter
        act = (inter * gelu_parts(inter)).astype(BF)
        outs.append(dot(act, wc(g)))
    r2 = jnp.concatenate(outs, axis=1) + vector_of(vec_ref, "b_out") + hidden.astype(F32)
    xh, rs = norm_parts(r2)
    xh2_ref[...] = xh
    rs2_ref[...] = jnp.broadcast_to(rs, (ROWS, 128))
    y_ref[...] = (xh * vector_of(vec_ref, "gain_two") + vector_of(vec_ref, "shift_two")).astype(BF)


def norm_back(gy, xh, rs, gain):
    t = gy * gain
    m1 = jnp.mean(t, axis=-1, keepdims=True)
    m2 = jnp.mean(t * xh, axis=-1, keepdims=True)
    return rs[:, :1] * (t - m1 - xh * m2)


def layer_backward(gy, u_ref, wa, wb, wc, vec_ref, q_ref, k_ref, v_ref, p_ref, ctx_ref, xh1_ref, rs1_ref, hid_ref, inter_ref, xh2_ref, rs2_ref,
                   gu_ref, put_a, put_b, put_c, gvec_ref, gq_ref, gk_ref, gv_ref):
    def put_vec(name, row, start=0):
        at = PLACE[name][0] + start
        gvec_ref[:, at : at + row.shape[1]] = row

    def colsum(x):
        return jnp.sum(x.astype(F32), axis=0, keepdims=True)

    xh2 = xh2_ref[...]
    put_vec("gain_two", colsum(gy * xh2))
    put_vec("shift_two", colsum(gy))
    g_r2 = norm_back(gy, xh2, rs2_ref[...], vector_of(vec_ref, "gain_two"))
    g_out = g_r2.astype(BF)
    put_vec("b_out", colsum(g_out))
    hidden = hid_ref[...]
    hidden_t = hidden.T
    parts = []
    for g in range(4):
        cols = slice(GROUP * g, GROUP * (g + 1))
        wide = slice(FF_GROUP * g, FF_GROUP * (g + 1))
        inter = inter_ref[:, wide]
        half = gelu_parts(inter)
        act = (inter * half).astype(BF)
        slope = half + inter * (jnp.exp(-0.5 * inter * inter) * 0.3989422804014327)
        go = g_out[:, cols]
        put_c(g, dot(act.T, go))
        g_inter = (dot_nt(go, wc(g)) * slope).astype(BF)
        put_vec("b_inter", colsum(g_inter), FF_GROUP * g)
        put_b(g, dot(hidden_t[cols], g_inter))
        _, w_inter = wb(g)
        parts.append(dot_nt(g_inter, w_inter))
    g_hidden = (g_r2 + jnp.concatenate(parts, axis=1)).astype(BF).astype(F32)
    xh1 = xh1_ref[...]
    put_vec("gain_one", colsum(g_hidden * xh1))
    put_vec("shift_one", colsum(g_hidden))
    g_r1 = norm_back(g_hidden, xh1, rs1_ref[...], vector_of(vec_ref, "gain_one"))
    g_post = g_r1.astype(BF)
    put_vec("b_post", colsum(g_post))
    put_b(None, dot(ctx_ref[...].T, g_post))
    w_post, _ = wb(None)
    g_ctx = dot_nt(g_post, w_post).astype(BF)
    lane = lax.broadcasted_iota(jnp.int32, (ROWS, 128), 1)
    for pair in range(HEADS // 2):
        cols = slice(128 * pair, 128 * (pair + 1))
        qt, kt, vt, ct = q_ref[:, cols], k_ref[:, cols], v_ref[:, cols], g_ctx[:, cols]
        got = []
        for half in range(2):
            mine = (lane >= 64) if half else (lane < 64)
            cm = jnp.where(mine, ct, jnp.zeros_like(ct))
            p = p_ref[2 * pair + half]
            g_p = dot_nt(cm, vt)
            g_v = dot_tn(p.astype(BF), ct)
            g_s = (p * (g_p - jnp.sum(p * g_p, axis=-1, keepdims=True))).astype(BF)
            got.append((dot(g_s, kt) * 0.125, dot_tn(g_s, qt) * 0.125, g_v))
        gq_ref[:, cols] = jnp.where(lane < 64, got[0][0], got[1][0]).astype(BF)
        gk_ref[:, cols] = jnp.where(lane < 64, got[0][1], got[1][1]).astype(BF)
        gv_ref[:, cols] = jnp.where(lane < 64, got[0][2], got[1][2]).astype(BF)
    put_vec("b_qv", colsum(gq_ref[...]))
    put_vec("b_qv", colsum(gv_ref[...]), WIDTH)
    u_t = u_ref[...].T
    parts = []
    for g in range(4):
        cols = slice(GROUP * g, GROUP * (g + 1))
        gp = jnp.concatenate([gq_ref[:, cols], gk_ref[:, cols], gv_ref[:, cols]], axis=1)
        put_a(g, dot(u_t[cols], gp))
        parts.append(dot_nt(gp, wa(g)))
    gu_ref[...] = g_r1 + jnp.concatenate(parts, axis=1)


SIZE = 4
STRIDE = {"x": 16, "y": 4, "z": 1}
WORD_PART, WORD_STEP = 5120, 1280
STEPS = WORD_PART // WORD_STEP
DEPTH = 4
ORDERS = (("z", "y", "x"), ("x", "z", "y"), ("y", "x", "z"))
VMEM = pl.BlockSpec(memory_space=pltpu.VMEM)
SMEM = pl.BlockSpec(memory_space=pltpu.SMEM)
HBM = pl.BlockSpec(memory_space=pl.ANY)
PARAMS = pltpu.CompilerParams(vmem_limit_bytes=56 << 20)
A_WIDTH, B_WIDTH = 1408, 1536
A_SHAPE, B_SHAPE = (4, GROUP, A_WIDTH), (4, 4, 48, B_WIDTH)


def cost(us):
    return pl.CostEstimate(flops=int(us * 1e8), bytes_accessed=int(us * 3.2e6), transcendentals=0)


def spec_of(shape, dtype):
    return jax.ShapeDtypeStruct(shape, dtype)


def place_on(axis):
    return (lax.axis_index("dp") // STRIDE[axis]) % SIZE


def exchange(block, axis, pairs):
    stride, route = STRIDE[axis], []
    for section in range(2):
        for chip in range(64):
            at = (chip // stride) % SIZE
            mate = at ^ 1 if section == pairs else SIZE - 1 - at
            route.append((section * 64 + chip, section * 64 + chip + (mate - at) * stride))
    return lax.ppermute(block, ("section", "dp"), route)


def near(block, axis):
    return exchange(block, axis, 0)


def next_near(block, axis):
    return exchange(block, axis, 1)


def swap(block):
    return lax.ppermute(block, "section", [(0, 1), (1, 0)])


def start_all(copies):
    for copy in copies:
        copy.start()


def wait_all(copies):
    for copy in copies:
        copy.wait()


def gather_pairs(block, axis, name, join):
    with jax.named_scope(name + "_" + axis + "_first"):
        first = near(block, axis)
    pair = join([block, first])
    with jax.named_scope(name + "_" + axis + "_second"):
        second = next_near(pair, axis)
    return pair, second


def scatter_pairs(kept, sent, axis, name, after=()):
    with jax.named_scope(name + "_" + axis + "_second"):
        came = next_near(sent, axis)
    half = kept.shape[0] // 2
    with jax.named_scope(name + "_" + axis + "_add"):
        passed = (kept[half:].astype(F32) + came[half:].astype(F32)).astype(BF)
        passed = tied(passed, *after) if after else passed
    with jax.named_scope(name + "_" + axis + "_first"):
        last = near(passed, axis)
    return kept[:half], came[:half], last, passed


def summed(blocks):
    return sum(block.astype(F32) for block in blocks)


def gather_stage(block, axis, name):
    with jax.named_scope(name + "_" + axis + "_first"):
        first = near(block, axis)
    with jax.named_scope(name + "_" + axis + "_second"):
        second = next_near(block, axis)
    with jax.named_scope(name + "_" + axis + "_across"):
        across = next_near(first, axis)
    return [block, first, second, across]


def relative(axis):
    at = place_on(axis)
    one, two = at ^ 1, SIZE - 1 - at
    is_first = lax.axis_index("section") == 0
    return [at, jnp.where(is_first, one, two), jnp.where(is_first, two, one), (at + 2) % SIZE]


def wheres():
    return jnp.stack([jnp.stack(relative(axis)) for axis in "xyz"]).astype(jnp.int32)


def in_place(blocks, axis):
    which = relative(axis)
    ordered = []
    for spot in range(SIZE):
        picked = blocks[3]
        for number in range(3):
            picked = jnp.where(which[number] == spot, blocks[number], picked)
        ordered.append(picked)
    return ordered


def picked(pieces, axis):
    return [lax.dynamic_index_in_dim(pieces, at, 0, keepdims=False) for at in relative(axis)]


def pair_kernel(first_ref, second_ref, out_ref, held_ref, in_sems, out_sems):
    rows, columns = first_ref.shape
    half = columns // 256 * 128
    lanes = [pl.ds(0, half), pl.ds(half, columns - half)]
    spots = [(n // 2, lanes[n % 2]) for n in range(4)]
    held = [held_ref.at[pl.ds(n * rows, rows), lane] for n, lane in spots]
    arrive = [pltpu.make_async_copy((first_ref, second_ref)[spots[n][0]].at[:, spots[n][1]], held[n], in_sems.at[n]) for n in range(4)]
    leave = [pltpu.make_async_copy(held[n], out_ref.at[pl.ds(spots[n][0] * rows, rows), spots[n][1]], out_sems.at[n]) for n in range(4)]
    start_all(arrive)
    for copy_in, copy_out in zip(arrive, leave, strict=True):
        copy_in.wait()
        copy_out.start()
    wait_all(leave)


def pair_rows(blocks):
    rows, columns = blocks[0].shape
    shape = (2 * rows, columns)
    return pl.pallas_call(
        pair_kernel,
        out_shape=spec_of(shape, BF),
        in_specs=[HBM] * 2,
        out_specs=HBM,
        scratch_shapes=[pltpu.VMEM(shape, BF), pltpu.SemaphoreType.DMA((4,)), pltpu.SemaphoreType.DMA((4,))],
        compiler_params=PARAMS,
        cost_estimate=cost(1.0),
        name="pair_rows",
    )(*blocks)


def stack_kernel(extra, where_ref, *refs):
    ins, outs, refs = refs[:2], refs[2 : 3 + (extra > 0)], refs[3 + (extra > 0) :]
    held_ref, in_sems, out_sems = refs[:3]
    spots = [pl.ds(n * 48, 48) for n in range(4)]
    sources = [ref.at[pl.ds(n * 48, 48)] for ref in ins for n in range(2)]
    arrive = [pltpu.make_async_copy(sources[n].at[:, pl.ds(0, WORD_PART)], held_ref.at[spots[n]], in_sems.at[n]) for n in range(4)]
    leave = [pltpu.make_async_copy(held_ref.at[spots[n]], outs[0].at[spots[n]], out_sems.at[n]) for n in range(4)]
    if extra:
        side_ref, side_in, side_out = refs[3:]
        for n in range(4):
            arrive.append(pltpu.make_async_copy(sources[n].at[:, pl.ds(WORD_PART, extra)], side_ref.at[n], side_in.at[n]))
            leave.append(pltpu.make_async_copy(side_ref.at[n], outs[1].at[where_ref[n]], side_out.at[n]))
    start_all(arrive)
    for copy_in, copy_out in zip(arrive, leave, strict=True):
        copy_in.wait()
        copy_out.start()
    wait_all(leave)


def stack_rows(blocks, axis):
    extra = blocks[0].shape[1] - WORD_PART
    sems = [pltpu.SemaphoreType.DMA((4,))] * 2
    more = [pltpu.VMEM((4, 48, extra), BF), *sems] if extra else []
    return pl.pallas_call(
        functools.partial(stack_kernel, extra),
        out_shape=[spec_of((GROUP, WORD_PART), BF)] + ([spec_of((4, 48, extra), BF)] if extra else []),
        in_specs=[SMEM] + [HBM] * 2,
        out_specs=[HBM] * (2 if extra else 1),
        scratch_shapes=[pltpu.VMEM((GROUP, WORD_PART), BF), *sems, *more],
        compiler_params=PARAMS,
        cost_estimate=cost(1.5),
        name="stack_rows",
    )(jnp.stack(relative(axis)).astype(jnp.int32), *blocks)


def unit_order():
    spot = lax.broadcasted_iota(jnp.int32, (1, FF_GROUP), 1)
    quarter = spot // GROUP
    rest = spot - GROUP * quarter
    device = rest // 12
    unit = 48 * device + 12 * quarter + (rest - 12 * device)
    row = lax.broadcasted_iota(jnp.int32, (FF_GROUP, FF_GROUP), 0)
    return (row == unit).astype(F32).astype(BF)


def pack_kernel(qkv_ref, post_ref, inter_ref, out_ref, *refs):
    vectors, packed_ref, held_ref, turned_ref = refs[:8], refs[8], refs[9], refs[10]
    held_ref[...] = jnp.zeros_like(held_ref)
    turned_ref[...] = jnp.zeros_like(turned_ref)
    for row in range(12):
        held_ref[row : row + 1, :576] = qkv_ref[row]
        held_ref[row : row + 1, 640:A_WIDTH] = post_ref[row]
        held_ref[row : row + 1, A_WIDTH : A_WIDTH + FF_GROUP] = inter_ref[row]
    for ref, (offset, width) in zip(vectors, SHARD.values(), strict=True):
        for n in range(width // 12):
            lane = 64 + offset // 12 + n
            turned_ref[lane : lane + 1, :12] = ref[:, 12 * n : 12 * (n + 1)]
    columns = turned_ref[...].T
    inter = dot(held_ref[:, A_WIDTH : A_WIDTH + FF_GROUP].astype(BF), unit_order())
    packed_ref[:, :576] = held_ref[:12, :576].astype(BF)
    packed_ref[:, 576:640] = columns[:12, 64:].astype(BF)
    packed_ref[:, 640:A_WIDTH] = held_ref[:12, 640:A_WIDTH].astype(BF)
    packed_ref[:, A_WIDTH : A_WIDTH + FF_GROUP] = inter[:12].astype(BF)
    for n in range(4):
        at = A_WIDTH + FF_GROUP + GROUP * n
        packed_ref[:, at : at + GROUP] = out_ref[12 * n : 12 * (n + 1)].astype(BF)


def pack(qkv, post, inter, out, vectors):
    return pl.pallas_call(
        pack_kernel,
        out_shape=spec_of((12, A_WIDTH + B_WIDTH), BF),
        in_specs=[VMEM] * 12,
        out_specs=VMEM,
        scratch_shapes=[pltpu.VMEM((16, A_WIDTH + FF_GROUP), F32), pltpu.VMEM((128, 128), F32)],
        compiler_params=PARAMS,
        cost_estimate=cost(2.0),
        name="pack_weights",
    )(qkv, post, inter, out, *vectors)


def unpack_kernel(own_ref, second_ref, third_ref, qkv_ref, post_ref, inter_ref, out_ref, *refs):
    vectors, turned_ref = refs[:8], refs[8]
    total = summed([own_ref[...], second_ref[...], third_ref[...]])
    units = total[:, A_WIDTH : A_WIDTH + FF_GROUP]
    order = unit_order()
    high = units.astype(BF)
    rest = units - high.astype(F32)
    middle = rest.astype(BF)
    last = (rest - middle.astype(F32)).astype(BF)
    inter = dot_nt(high, order) + dot_nt(middle, order) + dot_nt(last, order)
    for row in range(12):
        qkv_ref[row] = total[row : row + 1, :576]
        post_ref[row] = total[row : row + 1, 640:A_WIDTH]
        inter_ref[row] = inter[row : row + 1]
    for n in range(4):
        at = A_WIDTH + FF_GROUP + GROUP * n
        out_ref[12 * n : 12 * (n + 1)] = total[:, at : at + GROUP]
    turned_ref[...] = jnp.zeros_like(turned_ref)
    turned_ref[:12] = total[:, 512:640]
    columns = turned_ref[...].T
    for ref, (offset, width) in zip(vectors, SHARD.values(), strict=True):
        for n in range(width // 12):
            lane = 64 + offset // 12 + n
            ref[:, 12 * n : 12 * (n + 1)] = columns[lane : lane + 1, :12]


def unpack(blocks):
    shapes = [(12, 1, 576), (12, 1, WIDTH), (12, 1, WIDTH), (48, GROUP)] + [(1, width) for _, width in SHARD.values()]
    return pl.pallas_call(
        unpack_kernel,
        out_shape=[spec_of(shape, F32) for shape in shapes],
        in_specs=[VMEM] * 3,
        out_specs=[VMEM] * 12,
        scratch_shapes=[pltpu.VMEM((128, 128), F32)],
        compiler_params=PARAMS,
        cost_estimate=cost(2.0),
        name="unpack_grads",
    )(*blocks)


def assemble_kernel(where_ref, *refs):
    ins, outs = refs[:8], refs[8:]
    for n in range(4):
        outs[0][where_ref[0, n]] = ins[n][...]
        outs[1][:, where_ref[1, n]] = ins[4 + n][...]


def assemble(where, blocks_a, blocks_b):
    return pl.pallas_call(
        assemble_kernel,
        out_shape=[spec_of(shape, BF) for shape in (A_SHAPE, B_SHAPE)],
        in_specs=[SMEM] + [VMEM] * 8,
        out_specs=[VMEM] * 2,
        compiler_params=PARAMS,
        cost_estimate=cost(5.0),
        name="assemble_weights",
    )(where, *blocks_a, *blocks_b)


def fetch(layer, sec_ref, mine, other, held, sems):
    def bring(sources):
        copies = [pltpu.make_async_copy(sources[n], held[n], sems.at[n]) for n in range(2)]
        for copy in copies:
            copy.start()
        for copy in copies:
            copy.wait()

    @pl.when(sec_ref[0] == layer)
    def _():
        bring(mine)

    @pl.when(sec_ref[0] != layer)
    def _():
        bring(other)


def views(held):
    held_a, held_b = held

    def wa(g):
        return held_a[g][:, :576]

    def wb(g):
        if g is None:
            return held_a[...].reshape(WIDTH, A_WIDTH)[:, 640:], None
        return None, held_b[g].reshape(GROUP, B_WIDTH)[:, :FF_GROUP]

    def wc(g):
        block = held_b[g].reshape(GROUP, B_WIDTH)
        return jnp.concatenate([block[:, FF_GROUP + GROUP * q : FF_GROUP + GROUP * (q + 1)] for q in range(4)], axis=0)

    return wa, wb, wc


HELD = [pltpu.VMEM(shape, BF) for shape in (A_SHAPE, B_SHAPE)] + [pltpu.SemaphoreType.DMA((2,))]
KEPT = [
    spec_of((ROWS, WIDTH), BF),
    spec_of((ROWS, WIDTH), BF),
    spec_of((ROWS, WIDTH), BF),
    spec_of((HEADS, ROWS, ROWS), F32),
    spec_of((ROWS, WIDTH), BF),
    spec_of((ROWS, WIDTH), F32),
    spec_of((ROWS, 128), F32),
    spec_of((ROWS, WIDTH), BF),
    spec_of((ROWS, 4 * FF_GROUP), F32),
    spec_of((ROWS, WIDTH), F32),
    spec_of((ROWS, 128), F32),
]


def forward_kernel(layer, sec_ref, lengths_ref, u_ref, vec_ref, *refs):
    mine, other, outs, held, sems = refs[:2], refs[2:4], refs[4:16], refs[16:18], refs[18]
    fetch(layer, sec_ref, mine, other, held, sems)
    wa, wb, wc = views(held)
    source = jnp.where(sec_ref[0] == layer, 0, 1)
    layer_forward(u_ref, same_doc(lengths_ref, 2 * sec_ref[0]), wa, wb, wc, vec_ref.at[source], *outs)


def forward(layer, section, lengths, inputs, vectors, mine, other):
    outs = pl.pallas_call(
        functools.partial(forward_kernel, layer),
        out_shape=[spec_of((ROWS, WIDTH), BF)] + KEPT,
        in_specs=[SMEM, SMEM, VMEM, VMEM] + [HBM] * 4,
        out_specs=[VMEM] * 12,
        scratch_shapes=HELD,
        compiler_params=PARAMS,
        cost_estimate=cost(10.0),
        name="layer_forward",
    )(section, lengths, inputs, vectors, *mine, *other)
    return outs[0], outs[1:]


def backward_kernel(layer, sec_ref, gy_ref, u_ref, vec_ref, *refs):
    mine, other, kept = refs[:2], refs[2:4], refs[4:15]
    gu_ref, da_ref, db_ref = refs[15:18]
    held, sems, grads, gvec_ref, turned_ref = refs[18:20], refs[20], refs[21:24], refs[24], refs[25]
    fetch(layer, sec_ref, mine, other, held, sems)
    wa, wb, wc = views(held)

    def put_a(g, term):
        da_ref[g, :, :576] = term.astype(BF)

    def put_b(g, term):
        if g is None:
            da_ref[:, :, 640:] = term.astype(BF).reshape(4, GROUP, WIDTH)
        else:
            db_ref[g, :, :, :FF_GROUP] = term.astype(BF).reshape(4, 48, FF_GROUP)

    def put_c(g, term):
        low = term.astype(BF)
        for q in range(4):
            lanes = slice(FF_GROUP + GROUP * q, FF_GROUP + GROUP * (q + 1))
            db_ref[g, :, :, lanes] = low[GROUP * q : GROUP * (q + 1)].reshape(4, 48, GROUP)

    source = jnp.where(sec_ref[0] == layer, 0, 1)
    gy = gy_ref[...].astype(BF).astype(F32) if layer == 0 else gy_ref[...]
    layer_backward(gy, u_ref, wa, wb, wc, vec_ref.at[source], *kept, gu_ref, put_a, put_b, put_c, gvec_ref, *grads)
    contract_into(gvec_ref, turned_ref, da_ref)


def backward(layer, section, gy, inputs, vectors, mine, other, kept):
    outs = pl.pallas_call(
        functools.partial(backward_kernel, layer),
        out_shape=[spec_of((ROWS, WIDTH), F32), spec_of(A_SHAPE, BF), spec_of(B_SHAPE, BF)],
        in_specs=[SMEM, VMEM, VMEM, VMEM] + [HBM] * 4 + [VMEM] * 11,
        out_specs=[VMEM] * 3,
        scratch_shapes=HELD
        + [pltpu.VMEM((ROWS, WIDTH), BF)] * 3
        + [pltpu.VMEM((1, VECTOR), F32), pltpu.VMEM((128, WIDTH), F32)],
        compiler_params=PARAMS,
        cost_estimate=cost(15.0),
        name="layer_backward",
    )(section, gy, inputs, vectors, *mine, *other, *kept)
    return outs[0], outs[1:]


def spreads():
    row = lax.broadcasted_iota(jnp.int32, (96, 1), 0)
    device = row // 12
    within = row - 12 * device
    lane = lax.broadcasted_iota(jnp.int32, (96, GROUP), 1)
    return [(lane == 24 * device + within + 12 * n).astype(F32).astype(BF) for n in range(2)]


def expand_kernel(mine_ref, other_ref, out_ref):
    heads = spreads()
    for source, ref in enumerate((mine_ref, other_ref)):
        turned = ref[...].reshape(WIDTH, 128).astype(F32).T
        for name, (offset, width) in SHARD.items():
            at = PLACE[name][0]
            lane = 64 + offset // 12
            if name == "b_inter":
                for g in range(4):
                    for q in range(4):
                        spot = at + FF_GROUP * g + GROUP * q
                        out_ref[source, :, spot : spot + GROUP] = turned[lane + q : lane + q + 1, GROUP * g : GROUP * (g + 1)]
            elif name == "b_qv":
                for e in range(8):
                    rows = turned[lane : lane + 2, 96 * e : 96 * (e + 1)].astype(BF)
                    value = sum(dot(rows, heads[n])[n : n + 1] for n in range(2))
                    out_ref[source, :, at + GROUP * e : at + GROUP * (e + 1)] = value
            else:
                out_ref[source, :, at : at + WIDTH] = turned[lane : lane + 1]


def expand(mine, other):
    return pl.pallas_call(
        expand_kernel,
        grid=(1,),
        out_shape=spec_of((2, 1, VECTOR), F32),
        in_specs=[pl.BlockSpec((4, GROUP, 128), lambda i: (0, 0, 4))] * 2,
        out_specs=pl.BlockSpec((2, 1, VECTOR), lambda i: (0, 0, 0)),
        compiler_params=PARAMS,
        cost_estimate=cost(3.0),
        name="expand_vectors",
    )(mine, other)


def contract_into(gvec_ref, turned_ref, da_ref):
    heads = spreads()
    turned_ref[...] = jnp.zeros_like(turned_ref)
    for name, (offset, width) in SHARD.items():
        at = PLACE[name][0]
        lane = 64 + offset // 12
        if name == "b_inter":
            for g in range(4):
                for q in range(4):
                    spot = at + FF_GROUP * g + GROUP * q
                    turned_ref[lane + q : lane + q + 1, GROUP * g : GROUP * (g + 1)] = gvec_ref[:, spot : spot + GROUP]
        elif name == "b_qv":
            for e in range(8):
                value = gvec_ref[:, at + GROUP * e : at + GROUP * (e + 1)].astype(BF)
                for n in range(2):
                    turned_ref[lane + n : lane + n + 1, 96 * e : 96 * (e + 1)] = dot_nt(value, heads[n])
        else:
            turned_ref[lane : lane + 1] = gvec_ref[:, at : at + WIDTH]
    columns = turned_ref[...].T.astype(BF)
    for g in range(4):
        da_ref[g, :, 576:640] = columns[GROUP * g : GROUP * (g + 1), 64:]


def picks_of(feature_ref, part):
    row = lax.broadcasted_iota(jnp.int32, (WIDTH, WIDTH), 0)
    return (row == feature_ref[:, WIDTH * part : WIDTH * (part + 1)]).astype(F32).astype(BF)


def spread_kernel(sec_ref, feature_ref, mine_ref, other_ref, *refs):
    turned_ref, straight_ref, held_ref = refs[-3:]
    first = sec_ref[0] == 0
    held_ref[:ROWS] = jnp.where(first, mine_ref[...], other_ref[...])
    held_ref[ROWS:] = jnp.where(first, other_ref[...], mine_ref[...])
    for part in range(3):
        spot = slice(WIDTH * part, WIDTH * (part + 1))
        spread = dot(held_ref[...], picks_of(feature_ref, part)).astype(BF)
        straight_ref[:, spot] = spread
        turned_ref[spot] = spread.T


def spread_rows(section, feature, mine, other, after):
    return pl.pallas_call(
        spread_kernel,
        out_shape=[spec_of((3 * WIDTH, 256), BF), spec_of((256, 3 * WIDTH), BF)],
        in_specs=[SMEM] + [VMEM] * 3 + [HBM] * len(after),
        out_specs=[VMEM] * 2,
        scratch_shapes=[pltpu.VMEM((256, WIDTH), BF)],
        compiler_params=PARAMS,
        cost_estimate=cost(4.0),
        name="spread_rows",
    )(section, feature, mine, other, *after)


def word_chunks(words):
    starts = [[part * WORD_PART + step * WORD_STEP for step in range(STEPS)] for part in range(3)]
    return [[(start, min(WORD_STEP, words - start)) for start in part] for part in starts]


def grad_copies(grad_ref, held_ref, sems, words):
    copies = []
    for part, chunks in enumerate(word_chunks(words)):
        copies.append(
            [
                pltpu.make_async_copy(
                    grad_ref.at[pl.ds(start, size)],
                    held_ref.at[part % 2, pl.ds(step * WORD_STEP, size)],
                    sems.at[part % 2, step],
                )
                for step, (start, size) in enumerate(chunks)
            ]
        )
    return copies


def clear_rest(held_ref, part, words):
    used = min(WORD_PART, words - part * WORD_PART)
    if used < WORD_PART:
        held_ref[part % 2, used:] = jnp.zeros((WORD_PART - used, 256), BF)


def send_kernel(lhs_ref, grad_ref, *refs):
    outs, grad_buf, out_buf, grad_sems, out_sems = refs[:6], refs[6], refs[7], refs[8], refs[9]
    words = grad_ref.shape[0]
    arrive = grad_copies(grad_ref, grad_buf, grad_sems, words)
    leave = []
    start_all(arrive[0])
    start_all(arrive[1])
    for part in range(3):
        for step in range(STEPS):
            at = part * STEPS + step
            slot = at % 3
            columns = pl.ds(step * WORD_STEP, WORD_STEP)
            arrive[part][step].wait()
            if step == STEPS - 1:
                clear_rest(grad_buf, part, words)
            if at >= 3:
                wait_all(leave[at - 3])
            spot = slice(WIDTH * part + 2 * GROUP, WIDTH * (part + 1))
            term = dot_nt(lhs_ref[spot], grad_buf[part % 2, columns])
            for n in range(2):
                out_buf[slot, n] = term[GROUP * n : GROUP * (n + 1)].astype(BF)
            leave.append(
                [
                    pltpu.make_async_copy(out_buf.at[slot, n], outs[2 * part + n].at[:, columns], out_sems.at[slot, n])
                    for n in range(2)
                ]
            )
            start_all(leave[at])
        if part == 0:
            start_all(arrive[2])
    for copies in leave[-3:]:
        wait_all(copies)


def table_send(turned, logit_grad):
    return pl.pallas_call(
        send_kernel,
        out_shape=[spec_of((GROUP, WORD_PART), BF)] * 6,
        in_specs=[VMEM, HBM],
        out_specs=[HBM] * 6,
        scratch_shapes=[
            pltpu.VMEM((2, WORD_PART, 256), BF),
            pltpu.VMEM((3, 2, GROUP, WORD_STEP), BF),
            pltpu.SemaphoreType.DMA((2, STEPS)),
            pltpu.SemaphoreType.DMA((3, 2)),
        ],
        compiler_params=PARAMS,
        cost_estimate=cost(8.0),
        name="table_send",
    )(turned, logit_grad)


def term_kernel(part, extra, pieces, lhs_ref, grad_ref, *refs):
    added, outs = refs[:extra], refs[extra : extra + pieces]
    grad_buf, add_buf, out_buf, grad_sems, add_sems, out_sems = refs[extra + pieces :]
    words = grad_ref.shape[0]
    chunks = word_chunks(words)[part]
    rows = GROUP // pieces
    grads, adds, leave = [], [], []
    for step, (start, size) in enumerate(chunks):
        columns = pl.ds(step * WORD_STEP, WORD_STEP)
        grads.append(pltpu.make_async_copy(grad_ref.at[pl.ds(start, size)], grad_buf.at[step, pl.ds(0, size)], grad_sems.at[step]))
        adds.append([pltpu.make_async_copy(added[n].at[:, columns], add_buf.at[step, n], add_sems.at[step, n]) for n in range(extra)])
        leave.append(
            [
                pltpu.make_async_copy(out_buf.at[step, pl.ds(n * rows, rows)], outs[n].at[:, columns], out_sems.at[step, n])
                for n in range(pieces)
            ]
        )
        grads[step].start()
        start_all(adds[step])
    for step, (start, size) in enumerate(chunks):
        grads[step].wait()
        if size < WORD_STEP:
            grad_buf[step, size:] = jnp.zeros((WORD_STEP - size, 256), BF)
        total = dot_nt(lhs_ref[...], grad_buf[step])
        wait_all(adds[step])
        for n in range(extra):
            total = total + add_buf[step, n].astype(F32)
        out_buf[step] = total.astype(BF)
        start_all(leave[step])
    for copies in leave:
        wait_all(copies)


def table_term(part, block, turned, logit_grad, added, pieces):
    extra = len(added)
    rows = GROUP // pieces
    return pl.pallas_call(
        functools.partial(term_kernel, part, extra, pieces),
        grid=(1,),
        out_shape=[spec_of((rows, WORD_PART), BF)] * pieces,
        in_specs=[pl.BlockSpec((GROUP, 256), lambda i: (4 * part + block, 0))] + [HBM] * (1 + extra),
        out_specs=[HBM] * pieces,
        scratch_shapes=[
            pltpu.VMEM((STEPS, WORD_STEP, 256), BF),
            pltpu.VMEM((STEPS, extra, GROUP, WORD_STEP), BF),
            pltpu.VMEM((STEPS, GROUP, WORD_STEP), BF),
            pltpu.SemaphoreType.DMA((STEPS,)),
            pltpu.SemaphoreType.DMA((STEPS, extra)),
            pltpu.SemaphoreType.DMA((STEPS, pieces)),
        ],
        compiler_params=PARAMS,
        cost_estimate=cost(4.0),
        name="table_term",
    )(turned, logit_grad, *added)


def terms_kernel(parts, block, extra, pieces, lhs_ref, grad_ref, *refs):
    count = len(parts)
    added, outs = refs[: count * extra], refs[-6 - count * pieces : -6]
    grad_buf, add_buf, out_buf, grad_sems, add_sems, out_sems = refs[-6:]
    rows = GROUP // pieces
    words = word_chunks(grad_ref.shape[0])
    chunks = [(n, step, *chunk) for n, part in enumerate(parts) for step, chunk in enumerate(words[part])]
    arrive, leave = [], []
    for at, (part, step, start, size) in enumerate(chunks):
        slot = at % DEPTH
        columns = pl.ds(step * WORD_STEP, WORD_STEP)
        arrive.append(
            [pltpu.make_async_copy(grad_ref.at[pl.ds(start, size)], grad_buf.at[slot, pl.ds(0, size)], grad_sems.at[slot])]
            + [
                pltpu.make_async_copy(added[extra * part + n].at[:, columns], add_buf.at[slot, n], add_sems.at[slot, n])
                for n in range(extra)
            ]
        )
        leave.append(
            [
                pltpu.make_async_copy(out_buf.at[slot, pl.ds(n * rows, rows)], outs[pieces * part + n].at[:, columns], out_sems.at[slot, n])
                for n in range(pieces)
            ]
        )
    for at in range(DEPTH - 1):
        start_all(arrive[at])
    for at, (part, step, start, size) in enumerate(chunks):
        slot = at % DEPTH
        wait_all(arrive[at])
        if at + DEPTH - 1 < len(chunks):
            start_all(arrive[at + DEPTH - 1])
        if at >= DEPTH:
            wait_all(leave[at - DEPTH])
        if size < WORD_STEP:
            grad_buf[slot, size:] = jnp.zeros((WORD_STEP - size, 256), BF)
        spot = WIDTH * parts[part] + GROUP * block
        total = dot_nt(lhs_ref[spot : spot + GROUP], grad_buf[slot])
        for n in range(extra):
            total = total + add_buf[slot, n].astype(F32)
        out_buf[slot] = total.astype(BF)
        start_all(leave[at])
    for copies in leave[-DEPTH:]:
        wait_all(copies)


def table_terms(parts, block, turned, logit_grad, added, pieces, after=()):
    count = len(parts)
    extra = len(added) // count
    rows = GROUP // pieces
    return pl.pallas_call(
        functools.partial(terms_kernel, parts, block, extra, pieces),
        out_shape=[spec_of((rows, WORD_PART), BF)] * (count * pieces),
        in_specs=[VMEM] + [HBM] * (1 + count * extra + len(after)),
        out_specs=[HBM] * (count * pieces),
        scratch_shapes=[
            pltpu.VMEM((DEPTH, WORD_STEP, 256), BF),
            pltpu.VMEM((DEPTH, extra, GROUP, WORD_STEP), BF),
            pltpu.VMEM((DEPTH, GROUP, WORD_STEP), BF),
            pltpu.SemaphoreType.DMA((DEPTH,)),
            pltpu.SemaphoreType.DMA((DEPTH, extra)),
            pltpu.SemaphoreType.DMA((DEPTH, pieces)),
        ],
        compiler_params=PARAMS,
        cost_estimate=cost(1.5 + 3.0 * count),
        name="table_terms",
    )(turned, logit_grad, *added, *after)


def table_stream(ins, held_ref, sems, parts):
    copies = []
    for at in range(len(parts) * STEPS):
        columns = pl.ds(at % STEPS * WORD_STEP, WORD_STEP)
        copies.append(
            [
                pltpu.make_async_copy(
                    ins[4 * (at // STEPS) + n].at[:, columns], held_ref.at[at % DEPTH, pl.ds(GROUP * n, GROUP)], sems.at[at % DEPTH, n]
                )
                for n in range(4)
            ]
        )
    return copies


def head_grad_kernel(feature_ref, grad_ref, *refs):
    ins, (out_ref, total_ref, term_ref, table_buf, grad_buf, table_sems, grad_sems) = refs[:12], refs[-7:]
    chunks = [chunk for part in word_chunks(grad_ref.shape[0]) for chunk in part]
    arrive = table_stream(ins, table_buf, table_sems, range(3))
    for at, (start, size) in enumerate(chunks):
        slot = at % DEPTH
        arrive[at].append(pltpu.make_async_copy(grad_ref.at[pl.ds(start, size)], grad_buf.at[slot, pl.ds(0, size)], grad_sems.at[slot]))
    for at in range(DEPTH - 1):
        start_all(arrive[at])
    for at, (start, size) in enumerate(chunks):
        slot = at % DEPTH
        wait_all(arrive[at])
        if at + DEPTH - 1 < len(chunks):
            start_all(arrive[at + DEPTH - 1])
        if size < WORD_STEP:
            grad_buf[slot, size:] = jnp.zeros((WORD_STEP - size, 256), BF)
        term = dot(table_buf[slot], grad_buf[slot])
        if at % STEPS == 0:
            term_ref[...] = term
        else:
            term_ref[...] += term
        if at % STEPS == STEPS - 1:
            part = at // STEPS
            placed = dot(picks_of(feature_ref, part), term_ref[...].astype(BF))
            if part == 0:
                total_ref[...] = placed
            else:
                total_ref[...] += placed
    out_ref[...] = total_ref[...].T


def head_grad(feature, logit_grad, table, after):
    return pl.pallas_call(
        head_grad_kernel,
        out_shape=spec_of((256, WIDTH), F32),
        in_specs=[VMEM] + [HBM] * (13 + len(after)),
        out_specs=VMEM,
        scratch_shapes=[
            pltpu.VMEM((WIDTH, 256), F32),
            pltpu.VMEM((WIDTH, 256), F32),
            pltpu.VMEM((DEPTH, WIDTH, WORD_STEP), BF),
            pltpu.VMEM((DEPTH, WORD_STEP, 256), BF),
            pltpu.SemaphoreType.DMA((DEPTH, 4)),
            pltpu.SemaphoreType.DMA((DEPTH,)),
        ],
        compiler_params=PARAMS,
        cost_estimate=cost(14.0),
        name="head_grad",
    )(feature, logit_grad, *[block for blocks in table for block in blocks], *after)


def logits_kernel(parts, lhs_ref, *refs):
    ins, (out_ref, table_buf, out_buf, table_sems, out_sems) = refs[: 4 * len(parts)], refs[-5:]
    words = word_chunks(out_ref.shape[0])
    chunks = [chunk for part in parts for chunk in words[part]]
    arrive = table_stream(ins, table_buf, table_sems, parts)
    leave = []
    for at in range(DEPTH - 1):
        start_all(arrive[at])
    for at, (start, size) in enumerate(chunks):
        slot = at % DEPTH
        wait_all(arrive[at])
        if at + DEPTH - 1 < len(chunks):
            start_all(arrive[at + DEPTH - 1])
        if at >= DEPTH:
            leave[at - DEPTH].wait()
        part = parts[at // STEPS]
        lhs = lhs_ref[:, WIDTH * part : WIDTH * (part + 1)]
        out_buf[slot] = dot(lhs, table_buf[slot]).astype(BF).T
        leave.append(pltpu.make_async_copy(out_buf.at[slot, pl.ds(0, size)], out_ref.at[pl.ds(start, size)], out_sems.at[slot]))
        leave[at].start()
    wait_all(leave[-DEPTH:])


def logits_of(parts, straight, table, words, before, after):
    blocks = [block for part in parts for block in table[part]]
    extra = [] if before is None else [before]
    return pl.pallas_call(
        functools.partial(logits_kernel, parts),
        out_shape=spec_of((words, 256), BF),
        in_specs=[VMEM] + [HBM] * (len(blocks) + len(extra) + len(after)),
        out_specs=HBM,
        scratch_shapes=[
            pltpu.VMEM((DEPTH, WIDTH, WORD_STEP), BF),
            pltpu.VMEM((DEPTH, WORD_STEP, 256), BF),
            pltpu.SemaphoreType.DMA((DEPTH, 4)),
            pltpu.SemaphoreType.DMA((DEPTH,)),
        ],
        compiler_params=PARAMS,
        input_output_aliases={1 + len(blocks): 0} if extra else {},
        cost_estimate=cost(1.0 + 4.5 * len(parts)),
        name="logits",
    )(straight, *blocks, *extra, *after)


def combine_kernel(sec_ref, where_ref, *refs):
    kept, came, outs = refs[:4], refs[4:8], refs[8:12]
    bufs, sems = refs[12:16], refs[16]

    def bring(layer):
        copies = []
        for n in range(2):
            copies.append(pltpu.make_async_copy(kept[2 * layer + n], bufs[n], sems.at[n]))
            copies.append(pltpu.make_async_copy(came[2 * layer + n], bufs[2 + n], sems.at[2 + n]))
        for copy in copies:
            copy.start()
        for copy in copies:
            copy.wait()

    @pl.when(sec_ref[0] == 0)
    def _():
        bring(0)

    @pl.when(sec_ref[0] != 0)
    def _():
        bring(1)

    def added(first, second):
        return (first.astype(F32) + second.astype(F32)).astype(BF)

    for n in range(4):
        a, b = where_ref[0, n], where_ref[1, n]
        outs[n // 2][n % 2] = added(bufs[0][a], bufs[2][a])
        outs[2 + n // 2][n % 2] = added(bufs[1][:, b], bufs[3][:, b])


def combine(section, where, kept, came):
    shapes = [(2, GROUP, A_WIDTH)] * 2 + [(2, 4, 48, B_WIDTH)] * 2
    outs = pl.pallas_call(
        combine_kernel,
        out_shape=[spec_of(shape, BF) for shape in shapes],
        in_specs=[SMEM, SMEM] + [HBM] * 8,
        out_specs=[VMEM] * 4,
        scratch_shapes=[pltpu.VMEM(shape, BF) for shape in (A_SHAPE, B_SHAPE) * 2] + [pltpu.SemaphoreType.DMA((4,))],
        compiler_params=PARAMS,
        cost_estimate=cost(8.0),
        name="combine_grads",
    )(section, where, *kept, *came)
    return outs


def features():
    rows = []
    for order in ORDERS:
        steps = [jnp.stack(relative(axis)) * (12 * STRIDE[axis]) for axis in order[::-1]]
        feature = (
            steps[0][:, None, None, None]
            + steps[1][None, :, None, None]
            + steps[2][None, None, :, None]
            + jnp.arange(12)[None, None, None, :]
        )
        rows.append(feature.reshape(1, WIDTH))
    return jnp.concatenate(rows, axis=1).astype(jnp.int32)


def tied(values, *others):
    return lax.optimization_barrier((values, *others))[0]


def per_device(
    tokens, lengths, w_qkv, b_qv, w_post, b_post, gain_one, shift_one, w_inter, b_inter, w_out, b_out, gain_two, shift_two,
    embed_table, logit_grad,
):
    section_index = lax.axis_index("section")
    section = section_index.astype(jnp.int32)[None]
    is_first = section_index == 0
    words = embed_table.shape[1]
    where = wheres()
    given = dict(b_qv=b_qv, b_inter=b_inter, b_post=b_post, gain_one=gain_one, shift_one=shift_one, b_out=b_out, gain_two=gain_two, shift_two=shift_two)

    grad_turned = logit_grad.T
    turn = (1, 0, 2)

    packed = pack(
        w_qkv.transpose(turn), w_post.transpose(turn), w_inter.transpose(turn), w_out[0], [given[name] for name in SHARD]
    )
    table_low = jnp.pad(embed_table.astype(BF), ((0, 0), (0, 3 * WORD_PART - words)))
    names = ["table_a", "table_b", "table_c"]
    rows = [table_low[:, WORD_PART * part : WORD_PART * (part + 1)] for part in range(3)]

    def low_join(blocks):
        return jnp.concatenate(blocks, axis=0)

    rows[0] = jnp.concatenate([rows[0], packed], axis=1)
    names[0] = "table_weights"
    for part in range(3):
        pairs = gather_pairs(rows[part], ORDERS[part][0], names[part], low_join)
        if part == 0:
            quarters = [pair[12 * n : 12 * (n + 1), WORD_PART:] for pair in pairs for n in range(2)]
            weights = low_join(in_place(quarters, "z"))
            pairs = [pair[:, :WORD_PART] for pair in pairs]
        rows[part] = low_join(pairs)
    rows[0] = jnp.concatenate([rows[0], weights[:, :A_WIDTH]], axis=1)
    rows[2] = jnp.concatenate([rows[2], weights[:, A_WIDTH:]], axis=1)
    names = ["table_a", "table_b", "table_c"]
    paired = [gather_pairs(rows[part], ORDERS[part][1], names[part], pair_rows) for part in range(3)]
    stacked = [stack_rows(paired[part], ORDERS[part][1]) for part in (0, 2, 1)]
    blocks_a = gather_stage(tied(stacked[0][1].reshape(GROUP, A_WIDTH), paired[1][0]), "x", "weights_a")
    blocks_b = gather_stage(tied(stacked[1][1], paired[1][0]), "y", "weights_b")
    blocks_b[0] = tied(blocks_b[0], stacked[2][0])
    mine = assemble(where, blocks_a, blocks_b)
    with jax.named_scope("weights_swap"):
        other = [swap(piece) for piece in mine]
    vectors = expand(mine[0], other[0])
    rows = [stacked[0][0], stacked[2][0], stacked[1][0]]
    rows[0] = tied(rows[0], blocks_a[1], blocks_a[2])
    rows[1] = tied(rows[1], blocks_b[1], blocks_b[2])
    last_axes = [order[2] for order in ORDERS]

    def sent(exchanged, part, block, label):
        with jax.named_scope(names[part] + "_" + last_axes[part] + "_" + label):
            return exchanged(block, last_axes[part])

    table_first = [sent(near, part, rows[part], "first") for part in range(3)]
    feature = features()

    inputs = lax.dynamic_slice_in_dim(tokens, section_index * ROWS, ROWS, 0)
    middle, kept_zero = forward(0, section, lengths, inputs, vectors, mine, other)
    held = tied(tuple(rows), middle)
    table_second = [sent(next_near, part, held[part], "second") for part in range(3)]
    top, kept_one = forward(1, section, lengths, middle, vectors, mine, other)
    with jax.named_scope("top_swap"):
        top_other = swap(top)
    turned, straight = spread_rows(section, feature, top, top_other, [])
    held = (*tied(tuple(table_first[:2]), top), tied(table_first[2], turned))
    table_across = [sent(next_near, part, held[part], "across") for part in range(3)]
    table = list(zip(rows, table_first, table_second, table_across, strict=True))
    leaving = table_send(turned, grad_turned)
    names = ["grad_a", "grad_b", "grad_c"]
    grad_rows = head_grad(feature, tied(grad_turned, *leaving), table, [])
    with jax.named_scope("head_swap"):
        head_came = swap(lax.dynamic_slice_in_dim(grad_rows, (1 - section_index) * ROWS, ROWS, 0))
    later = tied(turned, grad_rows)
    passed, direct = [], []
    for part in range(3):
        axis = ORDERS[part][2]
        with jax.named_scope(names[part] + "_" + axis + "_across"):
            came = next_near(leaving[2 * part + 1], axis)
        with jax.named_scope(names[part] + "_" + axis + "_second"):
            direct.append(next_near(leaving[2 * part], axis))
        passed.append(table_term(part, 1, later, grad_turned, [came], 1)[0])
    onward = []
    for part in range(3):
        axis = ORDERS[part][2]
        with jax.named_scope(names[part] + "_" + axis + "_first"):
            onward.append(near(passed[part], axis))
    pieces = [table_term(0, 0, turned, grad_turned, [onward[0], direct[0]], 2)]
    both = table_terms((1, 2), 0, turned, grad_turned, [onward[1], direct[1], onward[2], direct[2]], 2)
    pieces += [both[:2], both[2:]]

    grad_top = lax.dynamic_slice_in_dim(grad_rows, section_index * ROWS, ROWS, 0) + head_came
    grad_middle, terms_one = backward(1, section, grad_top, middle, vectors, mine, other, kept_one)
    with jax.named_scope("one_swap"):
        came_one = [swap(term) for term in terms_one]
    grad_middle = tied(grad_middle, *passed)
    grad_inputs, terms_zero = backward(0, section, grad_middle, inputs, vectors, mine, other, kept_zero)
    with jax.named_scope("zero_swap"):
        came_zero = [swap(term) for term in terms_zero]

    token_low = grad_inputs.astype(BF)
    half = WIDTH // 2
    own_half = lax.dynamic_slice_in_dim(token_low, section_index * half, half, 1)
    with jax.named_scope("token_swap"):
        came_half = swap(lax.dynamic_slice_in_dim(token_low, (1 - section_index) * half, half, 1))
    token_out = jnp.concatenate([jnp.where(is_first, own_half, came_half), jnp.where(is_first, came_half, own_half)], axis=0)

    combined = combine(section, where, [*terms_zero, *terms_one], [*came_zero, *came_one])

    kept_a, sent_a, kept_b, sent_b = combined

    def again(whole, axis):
        places = picked(whole, axis)
        return jnp.stack(places[:2]), jnp.stack(places[2:])

    parts_a = scatter_pairs(kept_a, sent_a, "x", "sum_a")
    parts_b = scatter_pairs(kept_b, sent_b, "y", "sum_b")
    whole = []
    for part in range(3):
        total = summed(scatter_pairs(*pieces[part], ORDERS[part][1], names[part], [parts_a[3], parts_b[3]])[:3])
        whole.append(total.astype(BF))
    kept_a, sent_a = again(summed(parts_a[:3]).astype(BF).reshape(4, 48, A_WIDTH), "y")
    kept_b, sent_b = again(summed(parts_b[:3]).astype(BF)[0], "x")
    sum_a = summed(scatter_pairs(kept_a, sent_a, "y", "sum_a")[:3]).astype(BF)
    sum_b = summed(scatter_pairs(kept_b, sent_b, "x", "sum_b")[:3]).astype(BF)
    whole = tied(whole, sent_a, sent_b)
    table_sums = []
    for part in range(3):
        table_sums.append(summed(scatter_pairs(whole[part][:24], whole[part][24:], ORDERS[part][0], names[part])[:3]))
    table_grad = jnp.concatenate(table_sums, axis=1)[:, :words]
    both = jnp.concatenate([sum_a, sum_b], axis=2).reshape(4, 12, A_WIDTH + B_WIDTH)
    pieces = scatter_pairs(*again(both, "z"), "z", "sum")[:3]
    g_qkv, g_post, g_inter, g_out, *g_vectors = unpack([piece[0] for piece in pieces])
    sums = dict(zip(SHARD, g_vectors, strict=True))
    sums.update(w_qkv=g_qkv.transpose(turn), w_post=g_post.transpose(turn), w_inter=g_inter.transpose(turn), w_out=g_out[None])
    names = ("w_qkv", "b_qv", "w_post", "b_post", "gain_one", "shift_one", "w_inter", "b_inter", "w_out", "b_out", "gain_two", "shift_two")
    logits = logits_of((0, 1, 2), tied(straight, combined[0]), table, words, None, [])
    return (logits.T, token_out) + tuple(sums[name] for name in names) + (table_grad,)


def solution(mesh):
    matrix, vector = P("section", "dp", None), P("section", "dp")
    weights = (matrix, vector, matrix, vector, vector, vector, matrix, vector, matrix, vector, vector, vector)
    return jax.shard_map(
        per_device,
        mesh=mesh,
        in_specs=(P("dp", None), P("dp", None)) + weights + (P("dp", "section"), P("dp", "section")),
        out_specs=(P("dp", "section"), P("dp", "section")) + weights + (P("dp", "section"),),
        check_vma=False,
    )
```

```python
import functools
import jax
import jax.numpy as jnp
from jax import lax
from jax.experimental import pallas as pl
from jax.experimental.pallas import tpu as pltpu
from jax.sharding import PartitionSpec as P

BF = jnp.bfloat16
F32 = jnp.float32
ROWS, WIDTH, FF_GROUP, GROUP, HEADS = 128, 768, 768, 192, 12
SHARD = {
    "b_qv": (0, 24), "b_inter": (24, 48), "b_post": (72, 12), "gain_one": (84, 12),
    "shift_one": (96, 12), "b_out": (108, 12), "gain_two": (120, 12), "shift_two": (132, 12),
}
PLACE, _at = {}, 0
for _name, (_off, _width) in SHARD.items():
    PLACE[_name] = (_at, 64 * _width)
    _at += 64 * _width
VECTOR = _at


def dot(a, b):
    return lax.dot_general(a, b, (((1,), (0,)), ((), ())), preferred_element_type=F32)


def dot_nt(a, b):
    return lax.dot_general(a, b, (((1,), (1,)), ((), ())), preferred_element_type=F32)


def dot_tn(a, b):
    return lax.dot_general(a, b, (((0,), (0,)), ((), ())), preferred_element_type=F32)


def vector_of(vec_ref, name):
    at, size = PLACE[name]
    return vec_ref[:, at : at + size]


def norm_parts(values):
    mean = jnp.mean(values, axis=-1, keepdims=True)
    centred = values - mean
    scale = lax.rsqrt(jnp.mean(centred * centred, axis=-1, keepdims=True) + 1e-12)
    return centred * scale, scale


def same_doc(lengths_ref, first_row):
    row = lax.broadcasted_iota(jnp.int32, (ROWS, ROWS), 0)
    col = lax.broadcasted_iota(jnp.int32, (ROWS, ROWS), 1)
    row_id = jnp.zeros((ROWS, ROWS), jnp.int32)
    col_id = jnp.zeros((ROWS, ROWS), jnp.int32)
    for micro in range(2):
        end = micro * 64
        for doc in range(4):
            end = end + lengths_ref[first_row + micro, doc]
            row_id = row_id + (row >= end).astype(jnp.int32)
            col_id = col_id + (col >= end).astype(jnp.int32)
    return row_id == col_id


def gelu_parts(x):
    half = 0.5 * (1.0 + lax.erf(x * 0.7071067811865476))
    return half


def layer_forward(u_ref, same, wa, wb, wc, vec_ref, y_ref, q_ref, k_ref, v_ref, p_ref, ctx_ref, xh1_ref, rs1_ref, hid_ref, inter_ref, xh2_ref, rs2_ref):
    u = u_ref[...]
    for g in range(4):
        cols = slice(GROUP * g, GROUP * (g + 1))
        block = dot(u[:, cols], wa(g))
        b_q = vec_ref[:, PLACE["b_qv"][0] + GROUP * g : PLACE["b_qv"][0] + GROUP * (g + 1)]
        b_v = vec_ref[:, PLACE["b_qv"][0] + WIDTH + GROUP * g : PLACE["b_qv"][0] + WIDTH + GROUP * (g + 1)]
        q_ref[:, cols] = (block[:, :GROUP] + b_q).astype(BF)
        k_ref[:, cols] = block[:, GROUP : 2 * GROUP].astype(BF)
        v_ref[:, cols] = (block[:, 2 * GROUP : 3 * GROUP] + b_v).astype(BF)
    lane = lax.broadcasted_iota(jnp.int32, (ROWS, 128), 1)
    for pair in range(HEADS // 2):
        cols = slice(128 * pair, 128 * (pair + 1))
        qt, kt, vt = q_ref[:, cols], k_ref[:, cols], v_ref[:, cols]
        outs = []
        for half in range(2):
            mine = (lane >= 64) if half else (lane < 64)
            qm = jnp.where(mine, qt, jnp.zeros_like(qt))
            scores = jnp.where(same, dot_nt(qm, kt) * 0.125, -1e30)
            top = jnp.max(scores, axis=-1, keepdims=True)
            e = jnp.exp(scores - top)
            p = e / jnp.sum(e, axis=-1, keepdims=True)
            p_ref[2 * pair + half] = p
            outs.append(dot(p.astype(BF), vt))
        ctx_ref[:, cols] = jnp.where(lane < 64, outs[0], outs[1]).astype(BF)
    ctx = ctx_ref[...]
    w_post, _ = wb(None)
    r1 = dot(ctx, w_post) + vector_of(vec_ref, "b_post") + u.astype(F32)
    xh, rs = norm_parts(r1)
    xh1_ref[...] = xh
    rs1_ref[...] = jnp.broadcast_to(rs, (ROWS, 128))
    hidden = (xh * vector_of(vec_ref, "gain_one") + vector_of(vec_ref, "shift_one")).astype(BF)
    hid_ref[...] = hidden
    outs = []
    for g in range(4):
        cols = slice(GROUP * g, GROUP * (g + 1))
        _, w_inter = wb(g)
        at = PLACE["b_inter"][0] + FF_GROUP * g
        inter = dot(hidden[:, cols], w_inter) + vec_ref[:, at : at + FF_GROUP]
        inter_ref[:, FF_GROUP * g : FF_GROUP * (g + 1)] = inter
        act = (inter * gelu_parts(inter)).astype(BF)
        outs.append(dot(act, wc(g)))
    r2 = jnp.concatenate(outs, axis=1) + vector_of(vec_ref, "b_out") + hidden.astype(F32)
    xh, rs = norm_parts(r2)
    xh2_ref[...] = xh
    rs2_ref[...] = jnp.broadcast_to(rs, (ROWS, 128))
    y_ref[...] = (xh * vector_of(vec_ref, "gain_two") + vector_of(vec_ref, "shift_two")).astype(BF)


def norm_back(gy, xh, rs, gain):
    t = gy * gain
    m1 = jnp.mean(t, axis=-1, keepdims=True)
    m2 = jnp.mean(t * xh, axis=-1, keepdims=True)
    return rs[:, :1] * (t - m1 - xh * m2)


def layer_backward(gy, u_ref, wa, wb, wc, vec_ref, q_ref, k_ref, v_ref, p_ref, ctx_ref, xh1_ref, rs1_ref, hid_ref, inter_ref, xh2_ref, rs2_ref,
                   gu_ref, put_a, put_b, put_c, gvec_ref, gq_ref, gk_ref, gv_ref):
    def put_vec(name, row, start=0):
        at = PLACE[name][0] + start
        gvec_ref[:, at : at + row.shape[1]] = row

    def colsum(x):
        return jnp.sum(x.astype(F32), axis=0, keepdims=True)

    xh2 = xh2_ref[...]
    put_vec("gain_two", colsum(gy * xh2))
    put_vec("shift_two", colsum(gy))
    g_r2 = norm_back(gy, xh2, rs2_ref[...], vector_of(vec_ref, "gain_two"))
    g_out = g_r2.astype(BF)
    put_vec("b_out", colsum(g_out))
    hidden = hid_ref[...]
    hidden_t = hidden.T
    parts = []
    for g in range(4):
        cols = slice(GROUP * g, GROUP * (g + 1))
        wide = slice(FF_GROUP * g, FF_GROUP * (g + 1))
        inter = inter_ref[:, wide]
        half = gelu_parts(inter)
        act = (inter * half).astype(BF)
        slope = half + inter * (jnp.exp(-0.5 * inter * inter) * 0.3989422804014327)
        go = g_out[:, cols]
        put_c(g, dot(act.T, go))
        g_inter = (dot_nt(go, wc(g)) * slope).astype(BF)
        put_vec("b_inter", colsum(g_inter), FF_GROUP * g)
        put_b(g, dot(hidden_t[cols], g_inter))
        _, w_inter = wb(g)
        parts.append(dot_nt(g_inter, w_inter))
    g_hidden = (g_r2 + jnp.concatenate(parts, axis=1)).astype(BF).astype(F32)
    xh1 = xh1_ref[...]
    put_vec("gain_one", colsum(g_hidden * xh1))
    put_vec("shift_one", colsum(g_hidden))
    g_r1 = norm_back(g_hidden, xh1, rs1_ref[...], vector_of(vec_ref, "gain_one"))
    g_post = g_r1.astype(BF)
    put_vec("b_post", colsum(g_post))
    put_b(None, dot(ctx_ref[...].T, g_post))
    w_post, _ = wb(None)
    g_ctx = dot_nt(g_post, w_post).astype(BF)
    lane = lax.broadcasted_iota(jnp.int32, (ROWS, 128), 1)
    for pair in range(HEADS // 2):
        cols = slice(128 * pair, 128 * (pair + 1))
        qt, kt, vt, ct = q_ref[:, cols], k_ref[:, cols], v_ref[:, cols], g_ctx[:, cols]
        got = []
        for half in range(2):
            mine = (lane >= 64) if half else (lane < 64)
            cm = jnp.where(mine, ct, jnp.zeros_like(ct))
            p = p_ref[2 * pair + half]
            g_p = dot_nt(cm, vt)
            g_v = dot_tn(p.astype(BF), ct)
            g_s = (p * (g_p - jnp.sum(p * g_p, axis=-1, keepdims=True))).astype(BF)
            got.append((dot(g_s, kt) * 0.125, dot_tn(g_s, qt) * 0.125, g_v))
        gq_ref[:, cols] = jnp.where(lane < 64, got[0][0], got[1][0]).astype(BF)
        gk_ref[:, cols] = jnp.where(lane < 64, got[0][1], got[1][1]).astype(BF)
        gv_ref[:, cols] = jnp.where(lane < 64, got[0][2], got[1][2]).astype(BF)
    put_vec("b_qv", colsum(gq_ref[...]))
    put_vec("b_qv", colsum(gv_ref[...]), WIDTH)
    u_t = u_ref[...].T
    parts = []
    for g in range(4):
        cols = slice(GROUP * g, GROUP * (g + 1))
        gp = jnp.concatenate([gq_ref[:, cols], gk_ref[:, cols], gv_ref[:, cols]], axis=1)
        put_a(g, dot(u_t[cols], gp))
        parts.append(dot_nt(gp, wa(g)))
    gu_ref[...] = g_r1 + jnp.concatenate(parts, axis=1)


SIZE = 4
STRIDE = {"x": 16, "y": 4, "z": 1}
WORD_PART, WORD_STEP = 5120, 1280
STEPS = WORD_PART // WORD_STEP
DEPTH = 4
ORDERS = (("z", "y", "x"), ("x", "z", "y"), ("y", "x", "z"))
VMEM = pl.BlockSpec(memory_space=pltpu.VMEM)
SMEM = pl.BlockSpec(memory_space=pltpu.SMEM)
HBM = pl.BlockSpec(memory_space=pl.ANY)
PARAMS = pltpu.CompilerParams(vmem_limit_bytes=56 << 20)
A_WIDTH, B_WIDTH = 1408, 1536
A_SHAPE, B_SHAPE = (4, GROUP, A_WIDTH), (4, 4, 48, B_WIDTH)


def cost(us):
    return pl.CostEstimate(flops=int(us * 1e8), bytes_accessed=int(us * 3.2e6), transcendentals=0)


def spec_of(shape, dtype):
    return jax.ShapeDtypeStruct(shape, dtype)


def place_on(axis):
    return (lax.axis_index("dp") // STRIDE[axis]) % SIZE


def exchange(block, axis, pairs):
    stride, route = STRIDE[axis], []
    for section in range(2):
        for chip in range(64):
            at = (chip // stride) % SIZE
            mate = at ^ 1 if section == pairs else SIZE - 1 - at
            route.append((section * 64 + chip, section * 64 + chip + (mate - at) * stride))
    return lax.ppermute(block, ("section", "dp"), route)


def near(block, axis):
    return exchange(block, axis, 0)


def next_near(block, axis):
    return exchange(block, axis, 1)


def swap(block):
    return lax.ppermute(block, "section", [(0, 1), (1, 0)])


def opposite(block, axis):
    stride, route = STRIDE[axis], []
    for device in range(128):
        at = (device // stride) % SIZE
        route.append((device, device + ((at + 2) % SIZE - at) * stride))
    return lax.ppermute(block, ("section", "dp"), route)


def start_all(copies):
    for copy in copies:
        copy.start()


def wait_all(copies):
    for copy in copies:
        copy.wait()


def gather_pairs(block, axis, name, join):
    with jax.named_scope(name + "_" + axis + "_first"):
        first = near(block, axis)
    pair = join([block, first])
    with jax.named_scope(name + "_" + axis + "_second"):
        second = next_near(pair, axis)
    return pair, second


def scatter_pairs(kept, sent, axis, name, after=()):
    with jax.named_scope(name + "_" + axis + "_second"):
        came = next_near(sent, axis)
    half = kept.shape[0] // 2
    with jax.named_scope(name + "_" + axis + "_add"):
        passed = (kept[half:].astype(F32) + came[half:].astype(F32)).astype(BF)
        passed = tied(passed, *after) if after else passed
    with jax.named_scope(name + "_" + axis + "_first"):
        last = near(passed, axis)
    return kept[:half], came[:half], last, passed


def summed(blocks):
    return sum(block.astype(F32) for block in blocks)


def gather_stage(block, axis, name):
    with jax.named_scope(name + "_" + axis + "_first"):
        first = near(block, axis)
    with jax.named_scope(name + "_" + axis + "_second"):
        second = next_near(block, axis)
    with jax.named_scope(name + "_" + axis + "_across"):
        across = next_near(first, axis)
    return [block, first, second, across]


def relative(axis):
    at = place_on(axis)
    one, two = at ^ 1, SIZE - 1 - at
    is_first = lax.axis_index("section") == 0
    return [at, jnp.where(is_first, one, two), jnp.where(is_first, two, one), (at + 2) % SIZE]


def wheres():
    return jnp.stack([jnp.stack(relative(axis)) for axis in "xyz"]).astype(jnp.int32)


def in_place(blocks, axis):
    which = relative(axis)
    ordered = []
    for spot in range(SIZE):
        picked = blocks[3]
        for number in range(3):
            picked = jnp.where(which[number] == spot, blocks[number], picked)
        ordered.append(picked)
    return ordered


def picked(pieces, axis):
    return [lax.dynamic_index_in_dim(pieces, at, 0, keepdims=False) for at in relative(axis)]


def pair_kernel(first_ref, second_ref, out_ref, held_ref, in_sems, out_sems):
    rows, columns = first_ref.shape
    half = columns // 256 * 128
    lanes = [pl.ds(0, half), pl.ds(half, columns - half)]
    spots = [(n // 2, lanes[n % 2]) for n in range(4)]
    held = [held_ref.at[pl.ds(n * rows, rows), lane] for n, lane in spots]
    arrive = [pltpu.make_async_copy((first_ref, second_ref)[spots[n][0]].at[:, spots[n][1]], held[n], in_sems.at[n]) for n in range(4)]
    leave = [pltpu.make_async_copy(held[n], out_ref.at[pl.ds(spots[n][0] * rows, rows), spots[n][1]], out_sems.at[n]) for n in range(4)]
    start_all(arrive)
    for copy_in, copy_out in zip(arrive, leave, strict=True):
        copy_in.wait()
        copy_out.start()
    wait_all(leave)


def pair_rows(blocks):
    rows, columns = blocks[0].shape
    shape = (2 * rows, columns)
    return pl.pallas_call(
        pair_kernel,
        out_shape=spec_of(shape, BF),
        in_specs=[HBM] * 2,
        out_specs=HBM,
        scratch_shapes=[pltpu.VMEM(shape, BF), pltpu.SemaphoreType.DMA((4,)), pltpu.SemaphoreType.DMA((4,))],
        compiler_params=PARAMS,
        cost_estimate=cost(1.0),
        name="pair_rows",
    )(*blocks)


def stack_kernel(extra, where_ref, *refs):
    ins, outs, refs = refs[:2], refs[2 : 3 + (extra > 0)], refs[3 + (extra > 0) :]
    held_ref, in_sems, out_sems = refs[:3]
    spots = [pl.ds(n * 48, 48) for n in range(4)]
    sources = [ref.at[pl.ds(n * 48, 48)] for ref in ins for n in range(2)]
    arrive = [pltpu.make_async_copy(sources[n].at[:, pl.ds(0, WORD_PART)], held_ref.at[spots[n]], in_sems.at[n]) for n in range(4)]
    leave = [pltpu.make_async_copy(held_ref.at[spots[n]], outs[0].at[spots[n]], out_sems.at[n]) for n in range(4)]
    if extra:
        side_ref, side_in, side_out = refs[3:]
        for n in range(4):
            arrive.append(pltpu.make_async_copy(sources[n].at[:, pl.ds(WORD_PART, extra)], side_ref.at[n], side_in.at[n]))
            leave.append(pltpu.make_async_copy(side_ref.at[n], outs[1].at[where_ref[n]], side_out.at[n]))
    start_all(arrive)
    for copy_in, copy_out in zip(arrive, leave, strict=True):
        copy_in.wait()
        copy_out.start()
    wait_all(leave)


def stack_rows(blocks, axis):
    extra = blocks[0].shape[1] - WORD_PART
    sems = [pltpu.SemaphoreType.DMA((4,))] * 2
    more = [pltpu.VMEM((4, 48, extra), BF), *sems] if extra else []
    return pl.pallas_call(
        functools.partial(stack_kernel, extra),
        out_shape=[spec_of((GROUP, WORD_PART), BF)] + ([spec_of((4, 48, extra), BF)] if extra else []),
        in_specs=[SMEM] + [HBM] * 2,
        out_specs=[HBM] * (2 if extra else 1),
        scratch_shapes=[pltpu.VMEM((GROUP, WORD_PART), BF), *sems, *more],
        compiler_params=PARAMS,
        cost_estimate=cost(1.5),
        name="stack_rows",
    )(jnp.stack(relative(axis)).astype(jnp.int32), *blocks)


def unit_order():
    spot = lax.broadcasted_iota(jnp.int32, (1, FF_GROUP), 1)
    quarter = spot // GROUP
    rest = spot - GROUP * quarter
    device = rest // 12
    unit = 48 * device + 12 * quarter + (rest - 12 * device)
    row = lax.broadcasted_iota(jnp.int32, (FF_GROUP, FF_GROUP), 0)
    return (row == unit).astype(F32).astype(BF)


def pack_kernel(qkv_ref, post_ref, inter_ref, out_ref, table_ref, *refs):
    vectors, (first_ref, second_ref, third_ref, held_ref, turned_ref) = refs[:8], refs[8:]
    words = table_ref.shape[1]
    for part, ref in enumerate((first_ref, second_ref, third_ref)):
        size = min(WORD_PART, words - part * WORD_PART)
        ref[:, :size] = table_ref[:, part * WORD_PART : part * WORD_PART + size].astype(BF)
        if size < WORD_PART:
            ref[:, size:] = jnp.zeros((12, WORD_PART - size), BF)
    packed_ref = first_ref.at[:, pl.ds(WORD_PART, A_WIDTH + B_WIDTH)]
    held_ref[...] = jnp.zeros_like(held_ref)
    turned_ref[...] = jnp.zeros_like(turned_ref)
    for row in range(12):
        held_ref[row : row + 1, :576] = qkv_ref[row]
        held_ref[row : row + 1, 640:A_WIDTH] = post_ref[row]
        held_ref[row : row + 1, A_WIDTH : A_WIDTH + FF_GROUP] = inter_ref[row]
    for ref, (offset, width) in zip(vectors, SHARD.values(), strict=True):
        for n in range(width // 12):
            lane = 64 + offset // 12 + n
            turned_ref[lane : lane + 1, :12] = ref[:, 12 * n : 12 * (n + 1)]
    columns = turned_ref[...].T
    inter = dot(held_ref[:, A_WIDTH : A_WIDTH + FF_GROUP].astype(BF), unit_order())
    packed_ref[:, :576] = held_ref[:12, :576].astype(BF)
    packed_ref[:, 576:640] = columns[:12, 64:].astype(BF)
    packed_ref[:, 640:A_WIDTH] = held_ref[:12, 640:A_WIDTH].astype(BF)
    packed_ref[:, A_WIDTH : A_WIDTH + FF_GROUP] = inter[:12].astype(BF)
    for n in range(4):
        at = A_WIDTH + FF_GROUP + GROUP * n
        packed_ref[:, at : at + GROUP] = out_ref[12 * n : 12 * (n + 1)].astype(BF)


def pack(qkv, post, inter, out, table, vectors):
    return pl.pallas_call(
        pack_kernel,
        out_shape=[spec_of((12, width), BF) for width in (WORD_PART + A_WIDTH + B_WIDTH, WORD_PART, WORD_PART)],
        in_specs=[VMEM] * 13,
        out_specs=[VMEM] * 3,
        scratch_shapes=[pltpu.VMEM((16, A_WIDTH + FF_GROUP), F32), pltpu.VMEM((128, 128), F32)],
        compiler_params=PARAMS,
        cost_estimate=cost(2.0),
        name="pack_weights",
    )(qkv, post, inter, out, table, *vectors)


def unpack_kernel(own_ref, first_ref, second_ref, across_ref, qkv_ref, post_ref, inter_ref, out_ref, *refs):
    vectors, turned_ref = refs[:8], refs[8]
    total = summed([own_ref[...], first_ref[...], second_ref[...], across_ref[...]])
    units = total[:, A_WIDTH : A_WIDTH + FF_GROUP]
    order = unit_order()
    high = units.astype(BF)
    rest = units - high.astype(F32)
    middle = rest.astype(BF)
    last = (rest - middle.astype(F32)).astype(BF)
    inter = dot_nt(high, order) + dot_nt(middle, order) + dot_nt(last, order)
    for row in range(12):
        qkv_ref[row] = total[row : row + 1, :576]
        post_ref[row] = total[row : row + 1, 640:A_WIDTH]
        inter_ref[row] = inter[row : row + 1]
    for n in range(4):
        at = A_WIDTH + FF_GROUP + GROUP * n
        out_ref[12 * n : 12 * (n + 1)] = total[:, at : at + GROUP]
    turned_ref[...] = jnp.zeros_like(turned_ref)
    turned_ref[:12] = total[:, 512:640]
    columns = turned_ref[...].T
    for ref, (offset, width) in zip(vectors, SHARD.values(), strict=True):
        for n in range(width // 12):
            lane = 64 + offset // 12 + n
            ref[:, 12 * n : 12 * (n + 1)] = columns[lane : lane + 1, :12]


def unpack(blocks):
    shapes = [(12, 1, 576), (12, 1, WIDTH), (12, 1, WIDTH), (48, GROUP)] + [(1, width) for _, width in SHARD.values()]
    return pl.pallas_call(
        unpack_kernel,
        out_shape=[spec_of(shape, F32) for shape in shapes],
        in_specs=[VMEM] * 4,
        out_specs=[VMEM] * 12,
        scratch_shapes=[pltpu.VMEM((128, 128), F32)],
        compiler_params=PARAMS,
        cost_estimate=cost(2.0),
        name="unpack_grads",
    )(*blocks)


def assemble_kernel(where_ref, *refs):
    ins, outs = refs[:8], refs[8:]
    for n in range(4):
        outs[0][where_ref[0, n]] = ins[n][...]
        outs[1][:, where_ref[1, n]] = ins[4 + n][...]


def assemble(where, blocks_a, blocks_b):
    return pl.pallas_call(
        assemble_kernel,
        out_shape=[spec_of(shape, BF) for shape in (A_SHAPE, B_SHAPE)],
        in_specs=[SMEM] + [VMEM] * 8,
        out_specs=[VMEM] * 2,
        compiler_params=PARAMS,
        cost_estimate=cost(5.0),
        name="assemble_weights",
    )(where, *blocks_a, *blocks_b)


def fetch(layer, sec_ref, mine, other, held, sems):
    def bring(sources):
        copies = [pltpu.make_async_copy(sources[n], held[n], sems.at[n]) for n in range(2)]
        for copy in copies:
            copy.start()
        for copy in copies:
            copy.wait()

    @pl.when(sec_ref[0] == layer)
    def _():
        bring(mine)

    @pl.when(sec_ref[0] != layer)
    def _():
        bring(other)


def views(held):
    held_a, held_b = held

    def wa(g):
        return held_a[g][:, :576]

    def wb(g):
        if g is None:
            return held_a[...].reshape(WIDTH, A_WIDTH)[:, 640:], None
        return None, held_b[g].reshape(GROUP, B_WIDTH)[:, :FF_GROUP]

    def wc(g):
        block = held_b[g].reshape(GROUP, B_WIDTH)
        return jnp.concatenate([block[:, FF_GROUP + GROUP * q : FF_GROUP + GROUP * (q + 1)] for q in range(4)], axis=0)

    return wa, wb, wc


HELD = [pltpu.VMEM(shape, BF) for shape in (A_SHAPE, B_SHAPE)] + [pltpu.SemaphoreType.DMA((2,))]
KEPT = [
    spec_of((ROWS, WIDTH), BF),
    spec_of((ROWS, WIDTH), BF),
    spec_of((ROWS, WIDTH), BF),
    spec_of((HEADS, ROWS, ROWS), F32),
    spec_of((ROWS, WIDTH), BF),
    spec_of((ROWS, WIDTH), F32),
    spec_of((ROWS, 128), F32),
    spec_of((ROWS, WIDTH), BF),
    spec_of((ROWS, 4 * FF_GROUP), F32),
    spec_of((ROWS, WIDTH), F32),
    spec_of((ROWS, 128), F32),
]


def forward_kernel(layer, sec_ref, lengths_ref, u_ref, vec_ref, *refs):
    mine, other, outs, held, sems = refs[:2], refs[2:4], refs[4:16], refs[16:18], refs[18]
    fetch(layer, sec_ref, mine, other, held, sems)
    wa, wb, wc = views(held)
    source = jnp.where(sec_ref[0] == layer, 0, 1)
    layer_forward(u_ref, same_doc(lengths_ref, 2 * sec_ref[0]), wa, wb, wc, vec_ref.at[source], *outs)


def forward(layer, section, lengths, inputs, vectors, mine, other):
    outs = pl.pallas_call(
        functools.partial(forward_kernel, layer),
        out_shape=[spec_of((ROWS, WIDTH), BF)] + KEPT,
        in_specs=[SMEM, SMEM, VMEM, VMEM] + [HBM] * 4,
        out_specs=[VMEM] * 12,
        scratch_shapes=HELD,
        compiler_params=PARAMS,
        cost_estimate=cost(10.0),
        name="layer_forward",
    )(section, lengths, inputs, vectors, *mine, *other)
    return outs[0], outs[1:]


def backward_kernel(layer, sec_ref, gy_ref, u_ref, vec_ref, *refs):
    mine, other, kept = refs[:2], refs[2:4], refs[4:15]
    gu_ref, da_ref, db_ref = refs[15:18]
    held, sems, grads, gvec_ref, turned_ref = refs[18:20], refs[20], refs[21:24], refs[24], refs[25]
    fetch(layer, sec_ref, mine, other, held, sems)
    wa, wb, wc = views(held)

    def put_a(g, term):
        da_ref[g, :, :576] = term.astype(BF)

    def put_b(g, term):
        if g is None:
            da_ref[:, :, 640:] = term.astype(BF).reshape(4, GROUP, WIDTH)
        else:
            db_ref[g, :, :, :FF_GROUP] = term.astype(BF).reshape(4, 48, FF_GROUP)

    def put_c(g, term):
        low = term.astype(BF)
        for q in range(4):
            lanes = slice(FF_GROUP + GROUP * q, FF_GROUP + GROUP * (q + 1))
            db_ref[g, :, :, lanes] = low[GROUP * q : GROUP * (q + 1)].reshape(4, 48, GROUP)

    source = jnp.where(sec_ref[0] == layer, 0, 1)
    gy = gy_ref[...].astype(BF).astype(F32) if layer == 0 else gy_ref[...]
    layer_backward(gy, u_ref, wa, wb, wc, vec_ref.at[source], *kept, gu_ref, put_a, put_b, put_c, gvec_ref, *grads)
    contract_into(gvec_ref, turned_ref, da_ref)


def backward(layer, section, gy, inputs, vectors, mine, other, kept):
    outs = pl.pallas_call(
        functools.partial(backward_kernel, layer),
        out_shape=[spec_of((ROWS, WIDTH), F32), spec_of(A_SHAPE, BF), spec_of(B_SHAPE, BF)],
        in_specs=[SMEM, VMEM, VMEM, VMEM] + [HBM] * 4 + [VMEM] * 11,
        out_specs=[VMEM] * 3,
        scratch_shapes=HELD
        + [pltpu.VMEM((ROWS, WIDTH), BF)] * 3
        + [pltpu.VMEM((1, VECTOR), F32), pltpu.VMEM((128, WIDTH), F32)],
        compiler_params=PARAMS,
        cost_estimate=cost(15.0),
        name="layer_backward",
    )(section, gy, inputs, vectors, *mine, *other, *kept)
    return outs[0], outs[1:]


def spreads():
    row = lax.broadcasted_iota(jnp.int32, (96, 1), 0)
    device = row // 12
    within = row - 12 * device
    lane = lax.broadcasted_iota(jnp.int32, (96, GROUP), 1)
    return [(lane == 24 * device + within + 12 * n).astype(F32).astype(BF) for n in range(2)]


def expand_kernel(mine_ref, other_ref, out_ref):
    heads = spreads()
    for source, ref in enumerate((mine_ref, other_ref)):
        turned = ref[...].reshape(WIDTH, 128).astype(F32).T
        for name, (offset, width) in SHARD.items():
            at = PLACE[name][0]
            lane = 64 + offset // 12
            if name == "b_inter":
                for g in range(4):
                    for q in range(4):
                        spot = at + FF_GROUP * g + GROUP * q
                        out_ref[source, :, spot : spot + GROUP] = turned[lane + q : lane + q + 1, GROUP * g : GROUP * (g + 1)]
            elif name == "b_qv":
                for e in range(8):
                    rows = turned[lane : lane + 2, 96 * e : 96 * (e + 1)].astype(BF)
                    value = sum(dot(rows, heads[n])[n : n + 1] for n in range(2))
                    out_ref[source, :, at + GROUP * e : at + GROUP * (e + 1)] = value
            else:
                out_ref[source, :, at : at + WIDTH] = turned[lane : lane + 1]


def expand(mine, other):
    return pl.pallas_call(
        expand_kernel,
        grid=(1,),
        out_shape=spec_of((2, 1, VECTOR), F32),
        in_specs=[pl.BlockSpec((4, GROUP, 128), lambda i: (0, 0, 4))] * 2,
        out_specs=pl.BlockSpec((2, 1, VECTOR), lambda i: (0, 0, 0)),
        compiler_params=PARAMS,
        cost_estimate=cost(3.0),
        name="expand_vectors",
    )(mine, other)


def contract_into(gvec_ref, turned_ref, da_ref):
    heads = spreads()
    turned_ref[...] = jnp.zeros_like(turned_ref)
    for name, (offset, width) in SHARD.items():
        at = PLACE[name][0]
        lane = 64 + offset // 12
        if name == "b_inter":
            for g in range(4):
                for q in range(4):
                    spot = at + FF_GROUP * g + GROUP * q
                    turned_ref[lane + q : lane + q + 1, GROUP * g : GROUP * (g + 1)] = gvec_ref[:, spot : spot + GROUP]
        elif name == "b_qv":
            for e in range(8):
                value = gvec_ref[:, at + GROUP * e : at + GROUP * (e + 1)].astype(BF)
                for n in range(2):
                    turned_ref[lane + n : lane + n + 1, 96 * e : 96 * (e + 1)] = dot_nt(value, heads[n])
        else:
            turned_ref[lane : lane + 1] = gvec_ref[:, at : at + WIDTH]
    columns = turned_ref[...].T.astype(BF)
    for g in range(4):
        da_ref[g, :, 576:640] = columns[GROUP * g : GROUP * (g + 1), 64:]


def picks_of(feature_ref, part):
    row = lax.broadcasted_iota(jnp.int32, (WIDTH, WIDTH), 0)
    return (row == feature_ref[:, WIDTH * part : WIDTH * (part + 1)]).astype(F32).astype(BF)


def spread_kernel(sec_ref, feature_ref, mine_ref, other_ref, *refs):
    turned_ref, straight_ref, held_ref = refs[-3:]
    first = sec_ref[0] == 0
    held_ref[:ROWS] = jnp.where(first, mine_ref[...], other_ref[...])
    held_ref[ROWS:] = jnp.where(first, other_ref[...], mine_ref[...])
    for part in range(3):
        spot = slice(WIDTH * part, WIDTH * (part + 1))
        spread = dot(held_ref[...], picks_of(feature_ref, part)).astype(BF)
        straight_ref[:, spot] = spread
        turned_ref[spot] = spread.T


def spread_rows(section, feature, mine, other, after):
    return pl.pallas_call(
        spread_kernel,
        out_shape=[spec_of((3 * WIDTH, 256), BF), spec_of((256, 3 * WIDTH), BF)],
        in_specs=[SMEM] + [VMEM] * 3 + [HBM] * len(after),
        out_specs=[VMEM] * 2,
        scratch_shapes=[pltpu.VMEM((256, WIDTH), BF)],
        compiler_params=PARAMS,
        cost_estimate=cost(4.0),
        name="spread_rows",
    )(section, feature, mine, other, *after)


def word_chunks(words):
    starts = [[part * WORD_PART + step * WORD_STEP for step in range(STEPS)] for part in range(3)]
    return [[(start, min(WORD_STEP, words - start)) for start in part] for part in starts]


def grad_copies(grad_ref, held_ref, sems, words):
    copies = []
    for part, chunks in enumerate(word_chunks(words)):
        copies.append(
            [
                pltpu.make_async_copy(
                    grad_ref.at[pl.ds(start, size)],
                    held_ref.at[part % 2, pl.ds(step * WORD_STEP, size)],
                    sems.at[part % 2, step],
                )
                for step, (start, size) in enumerate(chunks)
            ]
        )
    return copies


def clear_rest(held_ref, part, words):
    used = min(WORD_PART, words - part * WORD_PART)
    if used < WORD_PART:
        held_ref[part % 2, used:] = jnp.zeros((WORD_PART - used, 256), BF)


def send_kernel(lhs_ref, grad_ref, *refs):
    outs, grad_buf, out_buf, grad_sems, out_sems = refs[:6], refs[6], refs[7], refs[8], refs[9]
    words = grad_ref.shape[0]
    arrive = grad_copies(grad_ref, grad_buf, grad_sems, words)
    leave = []
    start_all(arrive[0])
    start_all(arrive[1])
    for part in range(3):
        for step in range(STEPS):
            at = part * STEPS + step
            slot = at % 3
            columns = pl.ds(step * WORD_STEP, WORD_STEP)
            arrive[part][step].wait()
            if step == STEPS - 1:
                clear_rest(grad_buf, part, words)
            if at >= 3:
                wait_all(leave[at - 3])
            spot = slice(WIDTH * part + 2 * GROUP, WIDTH * (part + 1))
            term = dot_nt(lhs_ref[spot], grad_buf[part % 2, columns])
            for n in range(2):
                out_buf[slot, n] = term[GROUP * n : GROUP * (n + 1)].astype(BF)
            leave.append(
                [
                    pltpu.make_async_copy(out_buf.at[slot, n], outs[2 * part + n].at[:, columns], out_sems.at[slot, n])
                    for n in range(2)
                ]
            )
            start_all(leave[at])
        if part == 0:
            start_all(arrive[2])
    for copies in leave[-3:]:
        wait_all(copies)


def table_send(turned, logit_grad):
    return pl.pallas_call(
        send_kernel,
        out_shape=[spec_of((GROUP, WORD_PART), BF)] * 6,
        in_specs=[VMEM, HBM],
        out_specs=[HBM] * 6,
        scratch_shapes=[
            pltpu.VMEM((2, WORD_PART, 256), BF),
            pltpu.VMEM((3, 2, GROUP, WORD_STEP), BF),
            pltpu.SemaphoreType.DMA((2, STEPS)),
            pltpu.SemaphoreType.DMA((3, 2)),
        ],
        compiler_params=PARAMS,
        cost_estimate=cost(8.0),
        name="table_send",
    )(turned, logit_grad)


def term_kernel(part, extra, pieces, lhs_ref, grad_ref, *refs):
    added, outs = refs[:extra], refs[extra : extra + pieces]
    grad_buf, add_buf, out_buf, grad_sems, add_sems, out_sems = refs[extra + pieces :]
    words = grad_ref.shape[0]
    chunks = word_chunks(words)[part]
    rows = GROUP // pieces
    grads, adds, leave = [], [], []
    for step, (start, size) in enumerate(chunks):
        columns = pl.ds(step * WORD_STEP, WORD_STEP)
        grads.append(pltpu.make_async_copy(grad_ref.at[pl.ds(start, size)], grad_buf.at[step, pl.ds(0, size)], grad_sems.at[step]))
        adds.append([pltpu.make_async_copy(added[n].at[:, columns], add_buf.at[step, n], add_sems.at[step, n]) for n in range(extra)])
        leave.append(
            [
                pltpu.make_async_copy(out_buf.at[step, pl.ds(n * rows, rows)], outs[n].at[:, columns], out_sems.at[step, n])
                for n in range(pieces)
            ]
        )
        grads[step].start()
        start_all(adds[step])
    for step, (start, size) in enumerate(chunks):
        grads[step].wait()
        if size < WORD_STEP:
            grad_buf[step, size:] = jnp.zeros((WORD_STEP - size, 256), BF)
        total = dot_nt(lhs_ref[...], grad_buf[step])
        wait_all(adds[step])
        for n in range(extra):
            total = total + add_buf[step, n].astype(F32)
        out_buf[step] = total.astype(BF)
        start_all(leave[step])
    for copies in leave:
        wait_all(copies)


def table_term(part, block, turned, logit_grad, added, pieces):
    extra = len(added)
    rows = GROUP // pieces
    return pl.pallas_call(
        functools.partial(term_kernel, part, extra, pieces),
        grid=(1,),
        out_shape=[spec_of((rows, WORD_PART), BF)] * pieces,
        in_specs=[pl.BlockSpec((GROUP, 256), lambda i: (4 * part + block, 0))] + [HBM] * (1 + extra),
        out_specs=[HBM] * pieces,
        scratch_shapes=[
            pltpu.VMEM((STEPS, WORD_STEP, 256), BF),
            pltpu.VMEM((STEPS, extra, GROUP, WORD_STEP), BF),
            pltpu.VMEM((STEPS, GROUP, WORD_STEP), BF),
            pltpu.SemaphoreType.DMA((STEPS,)),
            pltpu.SemaphoreType.DMA((STEPS, extra)),
            pltpu.SemaphoreType.DMA((STEPS, pieces)),
        ],
        compiler_params=PARAMS,
        cost_estimate=cost(4.0),
        name="table_term",
    )(turned, logit_grad, *added)


def terms_kernel(parts, block, extra, pieces, lhs_ref, grad_ref, *refs):
    count = len(parts)
    added, outs = refs[: count * extra], refs[-6 - count * pieces : -6]
    grad_buf, add_buf, out_buf, grad_sems, add_sems, out_sems = refs[-6:]
    rows = GROUP // pieces
    words = word_chunks(grad_ref.shape[0])
    chunks = [(n, step, *chunk) for n, part in enumerate(parts) for step, chunk in enumerate(words[part])]
    arrive, leave = [], []
    for at, (part, step, start, size) in enumerate(chunks):
        slot = at % DEPTH
        columns = pl.ds(step * WORD_STEP, WORD_STEP)
        arrive.append(
            [pltpu.make_async_copy(grad_ref.at[pl.ds(start, size)], grad_buf.at[slot, pl.ds(0, size)], grad_sems.at[slot])]
            + [
                pltpu.make_async_copy(added[extra * part + n].at[:, columns], add_buf.at[slot, n], add_sems.at[slot, n])
                for n in range(extra)
            ]
        )
        leave.append(
            [
                pltpu.make_async_copy(out_buf.at[slot, pl.ds(n * rows, rows)], outs[pieces * part + n].at[:, columns], out_sems.at[slot, n])
                for n in range(pieces)
            ]
        )
    for at in range(DEPTH - 1):
        start_all(arrive[at])
    for at, (part, step, start, size) in enumerate(chunks):
        slot = at % DEPTH
        wait_all(arrive[at])
        if at + DEPTH - 1 < len(chunks):
            start_all(arrive[at + DEPTH - 1])
        if at >= DEPTH:
            wait_all(leave[at - DEPTH])
        if size < WORD_STEP:
            grad_buf[slot, size:] = jnp.zeros((WORD_STEP - size, 256), BF)
        spot = WIDTH * parts[part] + GROUP * block
        total = dot_nt(lhs_ref[spot : spot + GROUP], grad_buf[slot])
        for n in range(extra):
            total = total + add_buf[slot, n].astype(F32)
        out_buf[slot] = total.astype(BF)
        start_all(leave[at])
    for copies in leave[-DEPTH:]:
        wait_all(copies)


def table_terms(parts, block, turned, logit_grad, added, pieces, after=()):
    count = len(parts)
    extra = len(added) // count
    rows = GROUP // pieces
    return pl.pallas_call(
        functools.partial(terms_kernel, parts, block, extra, pieces),
        out_shape=[spec_of((rows, WORD_PART), BF)] * (count * pieces),
        in_specs=[VMEM] + [HBM] * (1 + count * extra + len(after)),
        out_specs=[HBM] * (count * pieces),
        scratch_shapes=[
            pltpu.VMEM((DEPTH, WORD_STEP, 256), BF),
            pltpu.VMEM((DEPTH, extra, GROUP, WORD_STEP), BF),
            pltpu.VMEM((DEPTH, GROUP, WORD_STEP), BF),
            pltpu.SemaphoreType.DMA((DEPTH,)),
            pltpu.SemaphoreType.DMA((DEPTH, extra)),
            pltpu.SemaphoreType.DMA((DEPTH, pieces)),
        ],
        compiler_params=PARAMS,
        cost_estimate=cost(1.5 + 3.0 * count),
        name="table_terms",
    )(turned, logit_grad, *added, *after)


def table_stream(ins, held_ref, sems, parts):
    copies = []
    for at in range(len(parts) * STEPS):
        columns = pl.ds(at % STEPS * WORD_STEP, WORD_STEP)
        copies.append(
            [
                pltpu.make_async_copy(
                    ins[4 * (at // STEPS) + n].at[:, columns], held_ref.at[at % DEPTH, pl.ds(GROUP * n, GROUP)], sems.at[at % DEPTH, n]
                )
                for n in range(4)
            ]
        )
    return copies


def head_grad_kernel(feature_ref, grad_ref, *refs):
    ins, (out_ref, total_ref, term_ref, table_buf, grad_buf, table_sems, grad_sems) = refs[:12], refs[-7:]
    chunks = [chunk for part in word_chunks(grad_ref.shape[0]) for chunk in part]
    arrive = table_stream(ins, table_buf, table_sems, range(3))
    for at, (start, size) in enumerate(chunks):
        slot = at % DEPTH
        arrive[at].append(pltpu.make_async_copy(grad_ref.at[pl.ds(start, size)], grad_buf.at[slot, pl.ds(0, size)], grad_sems.at[slot]))
    for at in range(DEPTH - 1):
        start_all(arrive[at])
    for at, (start, size) in enumerate(chunks):
        slot = at % DEPTH
        wait_all(arrive[at])
        if at + DEPTH - 1 < len(chunks):
            start_all(arrive[at + DEPTH - 1])
        if size < WORD_STEP:
            grad_buf[slot, size:] = jnp.zeros((WORD_STEP - size, 256), BF)
        term = dot(table_buf[slot], grad_buf[slot])
        if at % STEPS == 0:
            term_ref[...] = term
        else:
            term_ref[...] += term
        if at % STEPS == STEPS - 1:
            part = at // STEPS
            placed = dot(picks_of(feature_ref, part), term_ref[...].astype(BF))
            if part == 0:
                total_ref[...] = placed
            else:
                total_ref[...] += placed
    out_ref[...] = total_ref[...].T


def head_grad(feature, logit_grad, table, after):
    return pl.pallas_call(
        head_grad_kernel,
        out_shape=spec_of((256, WIDTH), F32),
        in_specs=[VMEM] + [HBM] * (13 + len(after)),
        out_specs=VMEM,
        scratch_shapes=[
            pltpu.VMEM((WIDTH, 256), F32),
            pltpu.VMEM((WIDTH, 256), F32),
            pltpu.VMEM((DEPTH, WIDTH, WORD_STEP), BF),
            pltpu.VMEM((DEPTH, WORD_STEP, 256), BF),
            pltpu.SemaphoreType.DMA((DEPTH, 4)),
            pltpu.SemaphoreType.DMA((DEPTH,)),
        ],
        compiler_params=PARAMS,
        cost_estimate=cost(14.0),
        name="head_grad",
    )(feature, logit_grad, *[block for blocks in table for block in blocks], *after)


def logits_kernel(parts, lhs_ref, *refs):
    ins, (out_ref, table_buf, out_buf, table_sems, out_sems) = refs[: 4 * len(parts)], refs[-5:]
    words = word_chunks(out_ref.shape[0])
    chunks = [chunk for part in parts for chunk in words[part]]
    arrive = table_stream(ins, table_buf, table_sems, parts)
    leave = []
    for at in range(DEPTH - 1):
        start_all(arrive[at])
    for at, (start, size) in enumerate(chunks):
        slot = at % DEPTH
        wait_all(arrive[at])
        if at + DEPTH - 1 < len(chunks):
            start_all(arrive[at + DEPTH - 1])
        if at >= DEPTH:
            leave[at - DEPTH].wait()
        part = parts[at // STEPS]
        lhs = lhs_ref[:, WIDTH * part : WIDTH * (part + 1)]
        out_buf[slot] = dot(lhs, table_buf[slot]).astype(BF).T
        leave.append(pltpu.make_async_copy(out_buf.at[slot, pl.ds(0, size)], out_ref.at[pl.ds(start, size)], out_sems.at[slot]))
        leave[at].start()
    wait_all(leave[-DEPTH:])


def logits_of(parts, straight, table, words, before, after):
    blocks = [block for part in parts for block in table[part]]
    extra = [] if before is None else [before]
    return pl.pallas_call(
        functools.partial(logits_kernel, parts),
        out_shape=spec_of((words, 256), BF),
        in_specs=[VMEM] + [HBM] * (len(blocks) + len(extra) + len(after)),
        out_specs=HBM,
        scratch_shapes=[
            pltpu.VMEM((DEPTH, WIDTH, WORD_STEP), BF),
            pltpu.VMEM((DEPTH, WORD_STEP, 256), BF),
            pltpu.SemaphoreType.DMA((DEPTH, 4)),
            pltpu.SemaphoreType.DMA((DEPTH,)),
        ],
        compiler_params=PARAMS,
        input_output_aliases={1 + len(blocks): 0} if extra else {},
        cost_estimate=cost(1.0 + 4.5 * len(parts)),
        name="logits",
    )(straight, *blocks, *extra, *after)


def combine_kernel(sec_ref, where_ref, *refs):
    kept, came, outs = refs[:4], refs[4:8], refs[8:12]
    bufs, sems = refs[12:16], refs[16]

    def copies(layer):
        return [
            [pltpu.make_async_copy(sources[2 * layer + n].at[g], bufs[2 * m + n].at[g], sems.at[2 * m + n, g]) for g in range(4)]
            for n in range(2)
            for m, sources in enumerate((kept, came))
        ]

    def bring(layer):
        for group in copies(layer):
            start_all(group)

    @pl.when(sec_ref[0] == 0)
    def _():
        bring(0)

    @pl.when(sec_ref[0] != 0)
    def _():
        bring(1)

    def added(first, second):
        return (first.astype(F32) + second.astype(F32)).astype(BF)

    arriving = copies(0)
    for group in arriving[:2]:
        wait_all(group)
    for n in range(4):
        a = where_ref[0, n]
        outs[n // 2][n % 2] = added(bufs[0][a], bufs[2][a])
    for group in arriving[2:]:
        wait_all(group)
    for n in range(4):
        b = where_ref[1, n]
        outs[2 + n // 2][n % 2] = added(bufs[1][:, b], bufs[3][:, b])


def combine(section, where, kept, came):
    shapes = [(2, GROUP, A_WIDTH)] * 2 + [(2, 4, 48, B_WIDTH)] * 2
    outs = pl.pallas_call(
        combine_kernel,
        out_shape=[spec_of(shape, BF) for shape in shapes],
        in_specs=[SMEM, SMEM] + [HBM] * 8,
        out_specs=[VMEM] * 4,
        scratch_shapes=[pltpu.VMEM(shape, BF) for shape in (A_SHAPE, B_SHAPE) * 2] + [pltpu.SemaphoreType.DMA((4, 4))],
        compiler_params=PARAMS,
        cost_estimate=cost(8.0),
        name="combine_grads",
    )(section, where, *kept, *came)
    return outs


def features():
    rows = []
    for order in ORDERS:
        steps = [jnp.stack(relative(axis)) * (12 * STRIDE[axis]) for axis in order[::-1]]
        feature = (
            steps[0][:, None, None, None]
            + steps[1][None, :, None, None]
            + steps[2][None, None, :, None]
            + jnp.arange(12)[None, None, None, :]
        )
        rows.append(feature.reshape(1, WIDTH))
    return jnp.concatenate(rows, axis=1).astype(jnp.int32)


def tied(values, *others):
    return lax.optimization_barrier((values, *others))[0]


def per_device(
    tokens, lengths, w_qkv, b_qv, w_post, b_post, gain_one, shift_one, w_inter, b_inter, w_out, b_out, gain_two, shift_two,
    embed_table, logit_grad,
):
    section_index = lax.axis_index("section")
    section = section_index.astype(jnp.int32)[None]
    is_first = section_index == 0
    words = embed_table.shape[1]
    where = wheres()
    given = dict(b_qv=b_qv, b_inter=b_inter, b_post=b_post, gain_one=gain_one, shift_one=shift_one, b_out=b_out, gain_two=gain_two, shift_two=shift_two)

    grad_turned = logit_grad.T
    turn = (1, 0, 2)

    rows = list(pack(
        w_qkv.transpose(turn),
        w_post.transpose(turn),
        w_inter.transpose(turn),
        w_out[0],
        embed_table,
        [given[name] for name in SHARD],
    ))
    names = ["table_weights", "table_b", "table_c"]

    def low_join(blocks):
        return jnp.concatenate(blocks, axis=0)

    for part in range(3):
        pairs = gather_pairs(rows[part], ORDERS[part][0], names[part], low_join)
        if part == 0:
            quarters = [pair[12 * n : 12 * (n + 1), WORD_PART:] for pair in pairs for n in range(2)]
            weights = low_join(in_place(quarters, "z"))
            pairs = [pair[:, :WORD_PART] for pair in pairs]
        rows[part] = low_join(pairs)
    rows[0] = jnp.concatenate([rows[0], weights[:, :A_WIDTH]], axis=1)
    rows[2] = jnp.concatenate([rows[2], weights[:, A_WIDTH:]], axis=1)
    names = ["table_a", "table_b", "table_c"]
    paired = [gather_pairs(rows[part], ORDERS[part][1], names[part], pair_rows) for part in range(3)]
    stacked = [stack_rows(paired[part], ORDERS[part][1]) for part in (0, 2, 1)]
    blocks_a = gather_stage(tied(stacked[0][1].reshape(GROUP, A_WIDTH), paired[1][0]), "x", "weights_a")
    blocks_b = gather_stage(tied(stacked[1][1], paired[1][0]), "y", "weights_b")
    blocks_b[0] = tied(blocks_b[0], stacked[2][0])
    mine = assemble(where, blocks_a, blocks_b)
    with jax.named_scope("weights_swap"):
        other = [swap(piece) for piece in mine]
    vectors = expand(mine[0], other[0])
    rows = [stacked[0][0], stacked[2][0], stacked[1][0]]
    rows[0] = tied(rows[0], blocks_a[1], blocks_a[2])
    rows[1] = tied(rows[1], blocks_b[1], blocks_b[2])
    last_axes = [order[2] for order in ORDERS]

    def sent(exchanged, part, block, label):
        with jax.named_scope(names[part] + "_" + last_axes[part] + "_" + label):
            return exchanged(block, last_axes[part])

    table_first = [sent(near, part, rows[part], "first") for part in range(3)]
    feature = features()

    inputs = lax.dynamic_slice_in_dim(tokens, section_index * ROWS, ROWS, 0)
    middle, kept_zero = forward(0, section, lengths, inputs, vectors, mine, other)
    held = tied(tuple(rows), middle)
    table_second = [sent(next_near, part, held[part], "second") for part in range(3)]
    top, kept_one = forward(1, section, lengths, middle, vectors, mine, other)
    with jax.named_scope("top_swap"):
        top_other = swap(top)
    turned, straight = spread_rows(section, feature, top, top_other, [])
    held = (*tied(tuple(table_first[:2]), top), tied(table_first[2], turned))
    table_across = [sent(next_near, part, held[part], "across") for part in range(3)]
    table = list(zip(rows, table_first, table_second, table_across, strict=True))
    leaving = table_send(tied(turned, *table_second), grad_turned)
    names = ["grad_a", "grad_b", "grad_c"]
    grad_rows = head_grad(feature, tied(grad_turned, *leaving), table, [])
    with jax.named_scope("head_swap"):
        head_came = swap(lax.dynamic_slice_in_dim(grad_rows, (1 - section_index) * ROWS, ROWS, 0))
    later = tied(turned, grad_rows)
    came, direct = [], []
    for part in range(3):
        axis = ORDERS[part][2]
        with jax.named_scope(names[part] + "_" + axis + "_across"):
            came.append(next_near(leaving[2 * part + 1], axis))
        with jax.named_scope(names[part] + "_" + axis + "_second"):
            direct.append(next_near(leaving[2 * part], axis))
    passed = table_terms((0, 1, 2), 1, later, grad_turned, came, 1)
    onward = []
    for part in range(3):
        axis = ORDERS[part][2]
        with jax.named_scope(names[part] + "_" + axis + "_first"):
            onward.append(near(passed[part], axis))
    pieces = [table_term(0, 0, turned, grad_turned, [onward[0], direct[0]], 2)]
    both = table_terms((1, 2), 0, turned, grad_turned, [onward[1], direct[1], onward[2], direct[2]], 2)
    pieces += [both[:2], both[2:]]

    grad_top = lax.dynamic_slice_in_dim(grad_rows, section_index * ROWS, ROWS, 0) + head_came
    grad_middle, terms_one = backward(1, section, grad_top, middle, vectors, mine, other, kept_one)
    with jax.named_scope("one_swap"):
        came_one = [swap(term) for term in terms_one]
    grad_middle = tied(grad_middle, *passed)
    grad_inputs, terms_zero = backward(0, section, grad_middle, inputs, vectors, mine, other, kept_zero)
    with jax.named_scope("zero_swap"):
        came_zero = [swap(term) for term in terms_zero]

    token_low = grad_inputs.astype(BF)
    half = WIDTH // 2
    own_half = lax.dynamic_slice_in_dim(token_low, section_index * half, half, 1)
    with jax.named_scope("token_swap"):
        came_half = swap(lax.dynamic_slice_in_dim(token_low, (1 - section_index) * half, half, 1))
    token_out = jnp.concatenate([jnp.where(is_first, own_half, came_half), jnp.where(is_first, came_half, own_half)], axis=0)

    combined = combine(section, where, [*terms_zero, *terms_one], [*came_zero, *came_one])

    kept_a, sent_a, kept_b, sent_b = combined

    def again(whole, axis):
        places = picked(whole, axis)
        return jnp.stack(places[:2]), jnp.stack(places[2:])

    parts_a = scatter_pairs(kept_a, sent_a, "x", "sum_a")
    parts_b = scatter_pairs(kept_b, sent_b, "y", "sum_b")
    whole = []
    for part in range(3):
        total = summed(scatter_pairs(*pieces[part], ORDERS[part][1], names[part], [parts_a[3], parts_b[3]])[:3])
        whole.append(total.astype(BF))
    kept_a, sent_a = again(summed(parts_a[:3]).astype(BF).reshape(4, 48, A_WIDTH), "y")
    kept_b, sent_b = again(summed(parts_b[:3]).astype(BF)[0], "x")
    sum_a = summed(scatter_pairs(kept_a, sent_a, "y", "sum_a")[:3]).astype(BF)
    sum_b = summed(scatter_pairs(kept_b, sent_b, "x", "sum_b")[:3]).astype(BF)
    whole = tied(whole, sent_a, sent_b)
    table_sums = []
    for part in range(3):
        table_sums.append(summed(scatter_pairs(whole[part][:24], whole[part][24:], ORDERS[part][0], names[part])[:3]))
    table_grad = jnp.concatenate(table_sums, axis=1)[:, :words]
    both = jnp.concatenate([sum_a, sum_b], axis=2).reshape(4, 12, A_WIDTH + B_WIDTH)
    own, first, second, across = picked(both, "z")
    with jax.named_scope("sum_z_across"):
        across = opposite(across, "z")
    with jax.named_scope("sum_z_first"):
        first = near(first, "z")
    with jax.named_scope("sum_z_second"):
        second = next_near(second, "z")
    g_qkv, g_post, g_inter, g_out, *g_vectors = unpack([own, first, second, across])
    sums = dict(zip(SHARD, g_vectors, strict=True))
    sums.update(w_qkv=g_qkv.transpose(turn), w_post=g_post.transpose(turn), w_inter=g_inter.transpose(turn), w_out=g_out[None])
    names = ("w_qkv", "b_qv", "w_post", "b_post", "gain_one", "shift_one", "w_inter", "b_inter", "w_out", "b_out", "gain_two", "shift_two")
    logits = logits_of((0, 1, 2), tied(straight, combined[0]), table, words, None, [])
    return (logits.T, token_out) + tuple(sums[name] for name in names) + (table_grad,)


def solution(mesh):
    matrix, vector = P("section", "dp", None), P("section", "dp")
    weights = (matrix, vector, matrix, vector, vector, vector, matrix, vector, matrix, vector, vector, vector)
    return jax.shard_map(
        per_device,
        mesh=mesh,
        in_specs=(P("dp", None), P("dp", None)) + weights + (P("dp", "section"), P("dp", "section")),
        out_specs=(P("dp", "section"), P("dp", "section")) + weights + (P("dp", "section"),),
        check_vma=False,
    )
```

```python
import functools
import jax
import jax.numpy as jnp
from jax import lax
from jax.experimental import pallas as pl
from jax.experimental.pallas import tpu as pltpu
from jax.sharding import PartitionSpec as P

BF = jnp.bfloat16
F32 = jnp.float32
ROWS, WIDTH, FF_GROUP, GROUP, HEADS = 128, 768, 768, 192, 12
SHARD = {
    "b_qv": (0, 24), "b_inter": (24, 48), "b_post": (72, 12), "gain_one": (84, 12),
    "shift_one": (96, 12), "b_out": (108, 12), "gain_two": (120, 12), "shift_two": (132, 12),
}
PLACE, _at = {}, 0
for _name, (_off, _width) in SHARD.items():
    PLACE[_name] = (_at, 64 * _width)
    _at += 64 * _width
VECTOR = _at


def dot(a, b):
    return lax.dot_general(a, b, (((1,), (0,)), ((), ())), preferred_element_type=F32)


def dot_nt(a, b):
    return lax.dot_general(a, b, (((1,), (1,)), ((), ())), preferred_element_type=F32)


def dot_tn(a, b):
    return lax.dot_general(a, b, (((0,), (0,)), ((), ())), preferred_element_type=F32)


def vector_of(vec_ref, name):
    at, size = PLACE[name]
    return vec_ref[:, at : at + size]


def norm_parts(values):
    mean = jnp.mean(values, axis=-1, keepdims=True)
    centred = values - mean
    scale = lax.rsqrt(jnp.mean(centred * centred, axis=-1, keepdims=True) + 1e-12)
    return centred * scale, scale


def same_doc(lengths_ref, first_row):
    row = lax.broadcasted_iota(jnp.int32, (ROWS, ROWS), 0)
    col = lax.broadcasted_iota(jnp.int32, (ROWS, ROWS), 1)
    row_id = jnp.zeros((ROWS, ROWS), jnp.int32)
    col_id = jnp.zeros((ROWS, ROWS), jnp.int32)
    for micro in range(2):
        end = micro * 64
        for doc in range(4):
            end = end + lengths_ref[first_row + micro, doc]
            row_id = row_id + (row >= end).astype(jnp.int32)
            col_id = col_id + (col >= end).astype(jnp.int32)
    return row_id == col_id


def gelu_parts(x):
    half = 0.5 * (1.0 + lax.erf(x * 0.7071067811865476))
    return half


def layer_forward(u_ref, same, wa, wb, wc, vec_ref, y_ref, q_ref, k_ref, v_ref, p_ref, ctx_ref, xh1_ref, rs1_ref, hid_ref, inter_ref, xh2_ref, rs2_ref):
    u = u_ref[...]
    for g in range(4):
        cols = slice(GROUP * g, GROUP * (g + 1))
        block = dot(u[:, cols], wa(g))
        b_q = vec_ref[:, PLACE["b_qv"][0] + GROUP * g : PLACE["b_qv"][0] + GROUP * (g + 1)]
        b_v = vec_ref[:, PLACE["b_qv"][0] + WIDTH + GROUP * g : PLACE["b_qv"][0] + WIDTH + GROUP * (g + 1)]
        q_ref[:, cols] = (block[:, :GROUP] + b_q).astype(BF)
        k_ref[:, cols] = block[:, GROUP : 2 * GROUP].astype(BF)
        v_ref[:, cols] = (block[:, 2 * GROUP : 3 * GROUP] + b_v).astype(BF)
    lane = lax.broadcasted_iota(jnp.int32, (ROWS, 128), 1)
    for pair in range(HEADS // 2):
        cols = slice(128 * pair, 128 * (pair + 1))
        qt, kt, vt = q_ref[:, cols], k_ref[:, cols], v_ref[:, cols]
        outs = []
        for half in range(2):
            mine = (lane >= 64) if half else (lane < 64)
            qm = jnp.where(mine, qt, jnp.zeros_like(qt))
            scores = jnp.where(same, dot_nt(qm, kt) * 0.125, -1e30)
            top = jnp.max(scores, axis=-1, keepdims=True)
            e = jnp.exp(scores - top)
            p = e / jnp.sum(e, axis=-1, keepdims=True)
            p_ref[2 * pair + half] = p
            outs.append(dot(p.astype(BF), vt))
        ctx_ref[:, cols] = jnp.where(lane < 64, outs[0], outs[1]).astype(BF)
    ctx = ctx_ref[...]
    w_post, _ = wb(None)
    r1 = dot(ctx, w_post) + vector_of(vec_ref, "b_post") + u.astype(F32)
    xh, rs = norm_parts(r1)
    xh1_ref[...] = xh
    rs1_ref[...] = jnp.broadcast_to(rs, (ROWS, 128))
    hidden = (xh * vector_of(vec_ref, "gain_one") + vector_of(vec_ref, "shift_one")).astype(BF)
    hid_ref[...] = hidden
    outs = []
    for g in range(4):
        cols = slice(GROUP * g, GROUP * (g + 1))
        _, w_inter = wb(g)
        at = PLACE["b_inter"][0] + FF_GROUP * g
        inter = dot(hidden[:, cols], w_inter) + vec_ref[:, at : at + FF_GROUP]
        inter_ref[:, FF_GROUP * g : FF_GROUP * (g + 1)] = inter
        act = (inter * gelu_parts(inter)).astype(BF)
        outs.append(dot(act, wc(g)))
    r2 = jnp.concatenate(outs, axis=1) + vector_of(vec_ref, "b_out") + hidden.astype(F32)
    xh, rs = norm_parts(r2)
    xh2_ref[...] = xh
    rs2_ref[...] = jnp.broadcast_to(rs, (ROWS, 128))
    y_ref[...] = (xh * vector_of(vec_ref, "gain_two") + vector_of(vec_ref, "shift_two")).astype(BF)


def norm_back(gy, xh, rs, gain):
    t = gy * gain
    m1 = jnp.mean(t, axis=-1, keepdims=True)
    m2 = jnp.mean(t * xh, axis=-1, keepdims=True)
    return rs[:, :1] * (t - m1 - xh * m2)


def layer_backward(gy, u_ref, wa, wb, wc, vec_ref, q_ref, k_ref, v_ref, p_ref, ctx_ref, xh1_ref, rs1_ref, hid_ref, inter_ref, xh2_ref, rs2_ref,
                   gu_ref, put_a, put_b, put_c, gvec_ref, gq_ref, gk_ref, gv_ref):
    def put_vec(name, row, start=0):
        at = PLACE[name][0] + start
        gvec_ref[:, at : at + row.shape[1]] = row

    def colsum(x):
        return jnp.sum(x.astype(F32), axis=0, keepdims=True)

    xh2 = xh2_ref[...]
    put_vec("gain_two", colsum(gy * xh2))
    put_vec("shift_two", colsum(gy))
    g_r2 = norm_back(gy, xh2, rs2_ref[...], vector_of(vec_ref, "gain_two"))
    g_out = g_r2.astype(BF)
    put_vec("b_out", colsum(g_out))
    hidden = hid_ref[...]
    hidden_t = hidden.T
    parts = []
    for g in range(4):
        cols = slice(GROUP * g, GROUP * (g + 1))
        wide = slice(FF_GROUP * g, FF_GROUP * (g + 1))
        inter = inter_ref[:, wide]
        half = gelu_parts(inter)
        act = (inter * half).astype(BF)
        slope = half + inter * (jnp.exp(-0.5 * inter * inter) * 0.3989422804014327)
        go = g_out[:, cols]
        put_c(g, dot(act.T, go))
        g_inter = (dot_nt(go, wc(g)) * slope).astype(BF)
        put_vec("b_inter", colsum(g_inter), FF_GROUP * g)
        put_b(g, dot(hidden_t[cols], g_inter))
        _, w_inter = wb(g)
        parts.append(dot_nt(g_inter, w_inter))
    g_hidden = (g_r2 + jnp.concatenate(parts, axis=1)).astype(BF).astype(F32)
    xh1 = xh1_ref[...]
    put_vec("gain_one", colsum(g_hidden * xh1))
    put_vec("shift_one", colsum(g_hidden))
    g_r1 = norm_back(g_hidden, xh1, rs1_ref[...], vector_of(vec_ref, "gain_one"))
    g_post = g_r1.astype(BF)
    put_vec("b_post", colsum(g_post))
    put_b(None, dot(ctx_ref[...].T, g_post))
    w_post, _ = wb(None)
    g_ctx = dot_nt(g_post, w_post).astype(BF)
    lane = lax.broadcasted_iota(jnp.int32, (ROWS, 128), 1)
    for pair in range(HEADS // 2):
        cols = slice(128 * pair, 128 * (pair + 1))
        qt, kt, vt, ct = q_ref[:, cols], k_ref[:, cols], v_ref[:, cols], g_ctx[:, cols]
        got = []
        for half in range(2):
            mine = (lane >= 64) if half else (lane < 64)
            cm = jnp.where(mine, ct, jnp.zeros_like(ct))
            p = p_ref[2 * pair + half]
            g_p = dot_nt(cm, vt)
            g_v = dot_tn(p.astype(BF), ct)
            g_s = (p * (g_p - jnp.sum(p * g_p, axis=-1, keepdims=True))).astype(BF)
            got.append((dot(g_s, kt) * 0.125, dot_tn(g_s, qt) * 0.125, g_v))
        gq_ref[:, cols] = jnp.where(lane < 64, got[0][0], got[1][0]).astype(BF)
        gk_ref[:, cols] = jnp.where(lane < 64, got[0][1], got[1][1]).astype(BF)
        gv_ref[:, cols] = jnp.where(lane < 64, got[0][2], got[1][2]).astype(BF)
    put_vec("b_qv", colsum(gq_ref[...]))
    put_vec("b_qv", colsum(gv_ref[...]), WIDTH)
    u_t = u_ref[...].T
    parts = []
    for g in range(4):
        cols = slice(GROUP * g, GROUP * (g + 1))
        gp = jnp.concatenate([gq_ref[:, cols], gk_ref[:, cols], gv_ref[:, cols]], axis=1)
        put_a(g, dot(u_t[cols], gp))
        parts.append(dot_nt(gp, wa(g)))
    gu_ref[...] = g_r1 + jnp.concatenate(parts, axis=1)


SIZE = 4
STRIDE = {"x": 16, "y": 4, "z": 1}
WORD_PART, WORD_STEP = 5120, 1280
STEPS = WORD_PART // WORD_STEP
DEPTH = 4
ORDERS = (("z", "y", "x"), ("x", "z", "y"), ("y", "x", "z"))
VMEM = pl.BlockSpec(memory_space=pltpu.VMEM)
SMEM = pl.BlockSpec(memory_space=pltpu.SMEM)
HBM = pl.BlockSpec(memory_space=pl.ANY)
PARAMS = pltpu.CompilerParams(vmem_limit_bytes=56 << 20)
A_WIDTH, B_WIDTH = 1408, 1536
A_SHAPE, B_SHAPE = (4, GROUP, A_WIDTH), (4, 4, 48, B_WIDTH)


def cost(us):
    return pl.CostEstimate(flops=int(us * 1e8), bytes_accessed=int(us * 3.2e6), transcendentals=0)


def spec_of(shape, dtype):
    return jax.ShapeDtypeStruct(shape, dtype)


def place_on(axis):
    return (lax.axis_index("dp") // STRIDE[axis]) % SIZE


def exchange(block, axis, pairs):
    stride, route = STRIDE[axis], []
    for section in range(2):
        for chip in range(64):
            at = (chip // stride) % SIZE
            mate = at ^ 1 if section == pairs else SIZE - 1 - at
            route.append((section * 64 + chip, section * 64 + chip + (mate - at) * stride))
    return lax.ppermute(block, ("section", "dp"), route)


def near(block, axis):
    return exchange(block, axis, 0)


def next_near(block, axis):
    return exchange(block, axis, 1)


def swap(block):
    return lax.ppermute(block, "section", [(0, 1), (1, 0)])


def opposite(block, axis):
    stride, route = STRIDE[axis], []
    for device in range(128):
        at = (device // stride) % SIZE
        route.append((device, device + ((at + 2) % SIZE - at) * stride))
    return lax.ppermute(block, ("section", "dp"), route)


def scatter_direct(blocks, axis, name):
    own, first, second, across = blocks
    with jax.named_scope(name + "_" + axis + "_across"):
        across = opposite(across, axis)
    with jax.named_scope(name + "_" + axis + "_first"):
        first = near(first, axis)
    with jax.named_scope(name + "_" + axis + "_second"):
        second = next_near(second, axis)
    return [own, first, second, across]


def start_all(copies):
    for copy in copies:
        copy.start()


def wait_all(copies):
    for copy in copies:
        copy.wait()


def gather_pairs(block, axis, name, join):
    with jax.named_scope(name + "_" + axis + "_first"):
        first = near(block, axis)
    pair = join([block, first])
    with jax.named_scope(name + "_" + axis + "_second"):
        second = next_near(pair, axis)
    return pair, second


def scatter_pairs(kept, sent, axis, name, after=()):
    with jax.named_scope(name + "_" + axis + "_second"):
        came = next_near(sent, axis)
    half = kept.shape[0] // 2
    with jax.named_scope(name + "_" + axis + "_add"):
        passed = (kept[half:].astype(F32) + came[half:].astype(F32)).astype(BF)
        passed = tied(passed, *after) if after else passed
    with jax.named_scope(name + "_" + axis + "_first"):
        last = near(passed, axis)
    return kept[:half], came[:half], last, passed


def summed(blocks):
    return sum(block.astype(F32) for block in blocks)


def gather_stage(block, axis, name):
    with jax.named_scope(name + "_" + axis + "_first"):
        first = near(block, axis)
    with jax.named_scope(name + "_" + axis + "_second"):
        second = next_near(block, axis)
    with jax.named_scope(name + "_" + axis + "_across"):
        across = next_near(first, axis)
    return [block, first, second, across]


def relative(axis):
    at = place_on(axis)
    one, two = at ^ 1, SIZE - 1 - at
    is_first = lax.axis_index("section") == 0
    return [at, jnp.where(is_first, one, two), jnp.where(is_first, two, one), (at + 2) % SIZE]


def wheres():
    return jnp.stack([jnp.stack(relative(axis)) for axis in "xyz"]).astype(jnp.int32)


def in_place(blocks, axis):
    which = relative(axis)
    ordered = []
    for spot in range(SIZE):
        picked = blocks[3]
        for number in range(3):
            picked = jnp.where(which[number] == spot, blocks[number], picked)
        ordered.append(picked)
    return ordered


def picked(pieces, axis):
    return [lax.dynamic_index_in_dim(pieces, at, 0, keepdims=False) for at in relative(axis)]


def gate_kernel(*refs):
    del refs


def gate(arrays, after):
    return pl.pallas_call(
        gate_kernel,
        out_shape=[spec_of(array.shape, array.dtype) for array in arrays],
        in_specs=[HBM] * (len(arrays) + len(after)),
        out_specs=[HBM] * len(arrays),
        input_output_aliases={n: n for n in range(len(arrays))},
        cost_estimate=cost(0.5),
        name="gate",
    )(*arrays, *after)


def pair_kernel(first_ref, second_ref, out_ref, held_ref, in_sems, out_sems):
    rows, columns = first_ref.shape
    half = columns // 256 * 128
    lanes = [pl.ds(0, half), pl.ds(half, columns - half)]
    spots = [(n // 2, lanes[n % 2]) for n in range(4)]
    held = [held_ref.at[pl.ds(n * rows, rows), lane] for n, lane in spots]
    arrive = [pltpu.make_async_copy((first_ref, second_ref)[spots[n][0]].at[:, spots[n][1]], held[n], in_sems.at[n]) for n in range(4)]
    leave = [pltpu.make_async_copy(held[n], out_ref.at[pl.ds(spots[n][0] * rows, rows), spots[n][1]], out_sems.at[n]) for n in range(4)]
    start_all(arrive)
    for copy_in, copy_out in zip(arrive, leave, strict=True):
        copy_in.wait()
        copy_out.start()
    wait_all(leave)


def pair_rows(blocks):
    rows, columns = blocks[0].shape
    shape = (2 * rows, columns)
    return pl.pallas_call(
        pair_kernel,
        out_shape=spec_of(shape, BF),
        in_specs=[HBM] * 2,
        out_specs=HBM,
        scratch_shapes=[pltpu.VMEM(shape, BF), pltpu.SemaphoreType.DMA((4,)), pltpu.SemaphoreType.DMA((4,))],
        compiler_params=PARAMS,
        cost_estimate=cost(1.0),
        name="pair_rows",
    )(*blocks)


def stack_kernel(extra, where_ref, *refs):
    ins, outs, refs = refs[:2], refs[2 : 3 + (extra > 0)], refs[3 + (extra > 0) :]
    held_ref, in_sems, out_sems = refs[:3]
    spots = [pl.ds(n * 48, 48) for n in range(4)]
    sources = [ref.at[pl.ds(n * 48, 48)] for ref in ins for n in range(2)]
    arrive = [pltpu.make_async_copy(sources[n].at[:, pl.ds(0, WORD_PART)], held_ref.at[spots[n]], in_sems.at[n]) for n in range(4)]
    leave = [pltpu.make_async_copy(held_ref.at[spots[n]], outs[0].at[spots[n]], out_sems.at[n]) for n in range(4)]
    if extra:
        side_ref, side_in, side_out = refs[3:]
        for n in range(4):
            arrive.append(pltpu.make_async_copy(sources[n].at[:, pl.ds(WORD_PART, extra)], side_ref.at[n], side_in.at[n]))
            leave.append(pltpu.make_async_copy(side_ref.at[n], outs[1].at[where_ref[n]], side_out.at[n]))
    start_all(arrive)
    for copy_in, copy_out in zip(arrive, leave, strict=True):
        copy_in.wait()
        copy_out.start()
    wait_all(leave)


def stack_rows(blocks, axis):
    extra = blocks[0].shape[1] - WORD_PART
    sems = [pltpu.SemaphoreType.DMA((4,))] * 2
    more = [pltpu.VMEM((4, 48, extra), BF), *sems] if extra else []
    return pl.pallas_call(
        functools.partial(stack_kernel, extra),
        out_shape=[spec_of((GROUP, WORD_PART), BF)] + ([spec_of((4, 48, extra), BF)] if extra else []),
        in_specs=[SMEM] + [HBM] * 2,
        out_specs=[HBM] * (2 if extra else 1),
        scratch_shapes=[pltpu.VMEM((GROUP, WORD_PART), BF), *sems, *more],
        compiler_params=PARAMS,
        cost_estimate=cost(1.5),
        name="stack_rows",
    )(jnp.stack(relative(axis)).astype(jnp.int32), *blocks)


def unit_order():
    spot = lax.broadcasted_iota(jnp.int32, (1, FF_GROUP), 1)
    quarter = spot // GROUP
    rest = spot - GROUP * quarter
    device = rest // 12
    unit = 48 * device + 12 * quarter + (rest - 12 * device)
    row = lax.broadcasted_iota(jnp.int32, (FF_GROUP, FF_GROUP), 0)
    return (row == unit).astype(F32).astype(BF)


def pack_kernel(qkv_ref, post_ref, inter_ref, out_ref, table_ref, *refs):
    vectors, (first_ref, second_ref, third_ref, held_ref, turned_ref) = refs[:8], refs[8:]
    words = table_ref.shape[1]
    for part, ref in enumerate((first_ref, second_ref, third_ref)):
        size = min(WORD_PART, words - part * WORD_PART)
        ref[:, :size] = table_ref[:, part * WORD_PART : part * WORD_PART + size].astype(BF)
        if size < WORD_PART:
            ref[:, size:] = jnp.zeros((12, WORD_PART - size), BF)
    packed_ref = first_ref.at[:, pl.ds(WORD_PART, A_WIDTH + B_WIDTH)]
    held_ref[...] = jnp.zeros_like(held_ref)
    turned_ref[...] = jnp.zeros_like(turned_ref)
    for row in range(12):
        held_ref[row : row + 1, :576] = qkv_ref[row]
        held_ref[row : row + 1, 640:A_WIDTH] = post_ref[row]
        held_ref[row : row + 1, A_WIDTH : A_WIDTH + FF_GROUP] = inter_ref[row]
    for ref, (offset, width) in zip(vectors, SHARD.values(), strict=True):
        for n in range(width // 12):
            lane = 64 + offset // 12 + n
            turned_ref[lane : lane + 1, :12] = ref[:, 12 * n : 12 * (n + 1)]
    columns = turned_ref[...].T
    inter = dot(held_ref[:, A_WIDTH : A_WIDTH + FF_GROUP].astype(BF), unit_order())
    packed_ref[:, :576] = held_ref[:12, :576].astype(BF)
    packed_ref[:, 576:640] = columns[:12, 64:].astype(BF)
    packed_ref[:, 640:A_WIDTH] = held_ref[:12, 640:A_WIDTH].astype(BF)
    packed_ref[:, A_WIDTH : A_WIDTH + FF_GROUP] = inter[:12].astype(BF)
    for n in range(4):
        at = A_WIDTH + FF_GROUP + GROUP * n
        packed_ref[:, at : at + GROUP] = out_ref[12 * n : 12 * (n + 1)].astype(BF)


def pack(qkv, post, inter, out, table, vectors):
    return pl.pallas_call(
        pack_kernel,
        out_shape=[spec_of((12, width), BF) for width in (WORD_PART + A_WIDTH + B_WIDTH, WORD_PART, WORD_PART)],
        in_specs=[VMEM] * 13,
        out_specs=[VMEM] * 3,
        scratch_shapes=[pltpu.VMEM((16, A_WIDTH + FF_GROUP), F32), pltpu.VMEM((128, 128), F32)],
        compiler_params=PARAMS,
        cost_estimate=cost(2.0),
        name="pack_weights",
    )(qkv, post, inter, out, table, *vectors)


def unpack_kernel(own_ref, first_ref, second_ref, across_ref, qkv_ref, post_ref, inter_ref, out_ref, *refs):
    vectors, turned_ref = refs[:8], refs[8]
    total = summed([own_ref[...], first_ref[...], second_ref[...], across_ref[...]])
    units = total[:, A_WIDTH : A_WIDTH + FF_GROUP]
    order = unit_order()
    high = units.astype(BF)
    rest = units - high.astype(F32)
    middle = rest.astype(BF)
    last = (rest - middle.astype(F32)).astype(BF)
    inter = dot_nt(high, order) + dot_nt(middle, order) + dot_nt(last, order)
    for row in range(12):
        qkv_ref[row] = total[row : row + 1, :576]
        post_ref[row] = total[row : row + 1, 640:A_WIDTH]
        inter_ref[row] = inter[row : row + 1]
    for n in range(4):
        at = A_WIDTH + FF_GROUP + GROUP * n
        out_ref[12 * n : 12 * (n + 1)] = total[:, at : at + GROUP]
    turned_ref[...] = jnp.zeros_like(turned_ref)
    turned_ref[:12] = total[:, 512:640]
    columns = turned_ref[...].T
    for ref, (offset, width) in zip(vectors, SHARD.values(), strict=True):
        for n in range(width // 12):
            lane = 64 + offset // 12 + n
            ref[:, 12 * n : 12 * (n + 1)] = columns[lane : lane + 1, :12]


def unpack(blocks):
    shapes = [(12, 1, 576), (12, 1, WIDTH), (12, 1, WIDTH), (48, GROUP)] + [(1, width) for _, width in SHARD.values()]
    return pl.pallas_call(
        unpack_kernel,
        out_shape=[spec_of(shape, F32) for shape in shapes],
        in_specs=[VMEM] * 4,
        out_specs=[VMEM] * 12,
        scratch_shapes=[pltpu.VMEM((128, 128), F32)],
        compiler_params=PARAMS,
        cost_estimate=cost(2.0),
        name="unpack_grads",
    )(*blocks)


def assemble_kernel(where_ref, *refs):
    ins, outs = refs[:8], refs[8:]
    for n in range(4):
        outs[0][where_ref[0, n]] = ins[n][...]
        outs[1][:, where_ref[1, n]] = ins[4 + n][...]


def assemble(where, blocks_a, blocks_b):
    return pl.pallas_call(
        assemble_kernel,
        out_shape=[spec_of(shape, BF) for shape in (A_SHAPE, B_SHAPE)],
        in_specs=[SMEM] + [VMEM] * 8,
        out_specs=[VMEM] * 2,
        compiler_params=PARAMS,
        cost_estimate=cost(5.0),
        name="assemble_weights",
    )(where, *blocks_a, *blocks_b)


def fetch(layer, sec_ref, mine, other, held, sems):
    def bring(sources):
        copies = [pltpu.make_async_copy(sources[n], held[n], sems.at[n]) for n in range(2)]
        for copy in copies:
            copy.start()
        for copy in copies:
            copy.wait()

    @pl.when(sec_ref[0] == layer)
    def _():
        bring(mine)

    @pl.when(sec_ref[0] != layer)
    def _():
        bring(other)


def views(held):
    held_a, held_b = held

    def wa(g):
        return held_a[g][:, :576]

    def wb(g):
        if g is None:
            return held_a[...].reshape(WIDTH, A_WIDTH)[:, 640:], None
        return None, held_b[g].reshape(GROUP, B_WIDTH)[:, :FF_GROUP]

    def wc(g):
        block = held_b[g].reshape(GROUP, B_WIDTH)
        return jnp.concatenate([block[:, FF_GROUP + GROUP * q : FF_GROUP + GROUP * (q + 1)] for q in range(4)], axis=0)

    return wa, wb, wc


HELD = [pltpu.VMEM(shape, BF) for shape in (A_SHAPE, B_SHAPE)] + [pltpu.SemaphoreType.DMA((2,))]
KEPT = [
    spec_of((ROWS, WIDTH), BF),
    spec_of((ROWS, WIDTH), BF),
    spec_of((ROWS, WIDTH), BF),
    spec_of((HEADS, ROWS, ROWS), F32),
    spec_of((ROWS, WIDTH), BF),
    spec_of((ROWS, WIDTH), F32),
    spec_of((ROWS, 128), F32),
    spec_of((ROWS, WIDTH), BF),
    spec_of((ROWS, 4 * FF_GROUP), F32),
    spec_of((ROWS, WIDTH), F32),
    spec_of((ROWS, 128), F32),
]


def forward_kernel(layer, sec_ref, lengths_ref, u_ref, vec_ref, *refs):
    mine, other, outs, held, sems = refs[:2], refs[2:4], refs[4:16], refs[16:18], refs[18]
    fetch(layer, sec_ref, mine, other, held, sems)
    wa, wb, wc = views(held)
    source = jnp.where(sec_ref[0] == layer, 0, 1)
    layer_forward(u_ref, same_doc(lengths_ref, 2 * sec_ref[0]), wa, wb, wc, vec_ref.at[source], *outs)


def forward(layer, section, lengths, inputs, vectors, mine, other):
    outs = pl.pallas_call(
        functools.partial(forward_kernel, layer),
        out_shape=[spec_of((ROWS, WIDTH), BF)] + KEPT,
        in_specs=[SMEM, SMEM, VMEM, VMEM] + [HBM] * 4,
        out_specs=[VMEM] * 12,
        scratch_shapes=HELD,
        compiler_params=PARAMS,
        cost_estimate=cost(10.0),
        name="layer_forward",
    )(section, lengths, inputs, vectors, *mine, *other)
    return outs[0], outs[1:]


def backward_kernel(layer, sec_ref, gy_ref, u_ref, vec_ref, *refs):
    mine, other, kept = refs[:2], refs[2:4], refs[4:15]
    gu_ref, da_ref, db_ref = refs[15:18]
    held, sems, grads, gvec_ref, turned_ref = refs[18:20], refs[20], refs[21:24], refs[24], refs[25]
    fetch(layer, sec_ref, mine, other, held, sems)
    wa, wb, wc = views(held)

    def put_a(g, term):
        da_ref[g, :, :576] = term.astype(BF)

    def put_b(g, term):
        if g is None:
            da_ref[:, :, 640:] = term.astype(BF).reshape(4, GROUP, WIDTH)
        else:
            db_ref[g, :, :, :FF_GROUP] = term.astype(BF).reshape(4, 48, FF_GROUP)

    def put_c(g, term):
        low = term.astype(BF)
        for q in range(4):
            lanes = slice(FF_GROUP + GROUP * q, FF_GROUP + GROUP * (q + 1))
            db_ref[g, :, :, lanes] = low[GROUP * q : GROUP * (q + 1)].reshape(4, 48, GROUP)

    source = jnp.where(sec_ref[0] == layer, 0, 1)
    gy = gy_ref[...].astype(BF).astype(F32) if layer == 0 else gy_ref[...]
    layer_backward(gy, u_ref, wa, wb, wc, vec_ref.at[source], *kept, gu_ref, put_a, put_b, put_c, gvec_ref, *grads)
    contract_into(gvec_ref, turned_ref, da_ref)


def backward(layer, section, gy, inputs, vectors, mine, other, kept):
    outs = pl.pallas_call(
        functools.partial(backward_kernel, layer),
        out_shape=[spec_of((ROWS, WIDTH), F32), spec_of(A_SHAPE, BF), spec_of(B_SHAPE, BF)],
        in_specs=[SMEM, VMEM, VMEM, VMEM] + [HBM] * 4 + [VMEM] * 11,
        out_specs=[VMEM] * 3,
        scratch_shapes=HELD
        + [pltpu.VMEM((ROWS, WIDTH), BF)] * 3
        + [pltpu.VMEM((1, VECTOR), F32), pltpu.VMEM((128, WIDTH), F32)],
        compiler_params=PARAMS,
        cost_estimate=cost(15.0),
        name="layer_backward",
    )(section, gy, inputs, vectors, *mine, *other, *kept)
    return outs[0], outs[1:]


def spreads():
    row = lax.broadcasted_iota(jnp.int32, (96, 1), 0)
    device = row // 12
    within = row - 12 * device
    lane = lax.broadcasted_iota(jnp.int32, (96, GROUP), 1)
    return [(lane == 24 * device + within + 12 * n).astype(F32).astype(BF) for n in range(2)]


def expand_kernel(mine_ref, other_ref, out_ref):
    heads = spreads()
    for source, ref in enumerate((mine_ref, other_ref)):
        turned = ref[...].reshape(WIDTH, 128).astype(F32).T
        for name, (offset, width) in SHARD.items():
            at = PLACE[name][0]
            lane = 64 + offset // 12
            if name == "b_inter":
                for g in range(4):
                    for q in range(4):
                        spot = at + FF_GROUP * g + GROUP * q
                        out_ref[source, :, spot : spot + GROUP] = turned[lane + q : lane + q + 1, GROUP * g : GROUP * (g + 1)]
            elif name == "b_qv":
                for e in range(8):
                    rows = turned[lane : lane + 2, 96 * e : 96 * (e + 1)].astype(BF)
                    value = sum(dot(rows, heads[n])[n : n + 1] for n in range(2))
                    out_ref[source, :, at + GROUP * e : at + GROUP * (e + 1)] = value
            else:
                out_ref[source, :, at : at + WIDTH] = turned[lane : lane + 1]


def expand(mine, other):
    return pl.pallas_call(
        expand_kernel,
        grid=(1,),
        out_shape=spec_of((2, 1, VECTOR), F32),
        in_specs=[pl.BlockSpec((4, GROUP, 128), lambda i: (0, 0, 4))] * 2,
        out_specs=pl.BlockSpec((2, 1, VECTOR), lambda i: (0, 0, 0)),
        compiler_params=PARAMS,
        cost_estimate=cost(3.0),
        name="expand_vectors",
    )(mine, other)


def contract_into(gvec_ref, turned_ref, da_ref):
    heads = spreads()
    turned_ref[...] = jnp.zeros_like(turned_ref)
    for name, (offset, width) in SHARD.items():
        at = PLACE[name][0]
        lane = 64 + offset // 12
        if name == "b_inter":
            for g in range(4):
                for q in range(4):
                    spot = at + FF_GROUP * g + GROUP * q
                    turned_ref[lane + q : lane + q + 1, GROUP * g : GROUP * (g + 1)] = gvec_ref[:, spot : spot + GROUP]
        elif name == "b_qv":
            for e in range(8):
                value = gvec_ref[:, at + GROUP * e : at + GROUP * (e + 1)].astype(BF)
                for n in range(2):
                    turned_ref[lane + n : lane + n + 1, 96 * e : 96 * (e + 1)] = dot_nt(value, heads[n])
        else:
            turned_ref[lane : lane + 1] = gvec_ref[:, at : at + WIDTH]
    columns = turned_ref[...].T.astype(BF)
    for g in range(4):
        da_ref[g, :, 576:640] = columns[GROUP * g : GROUP * (g + 1), 64:]


def picks_of(feature_ref, part):
    row = lax.broadcasted_iota(jnp.int32, (WIDTH, WIDTH), 0)
    return (row == feature_ref[:, WIDTH * part : WIDTH * (part + 1)]).astype(F32).astype(BF)


def spread_kernel(sec_ref, feature_ref, mine_ref, other_ref, *refs):
    turned_ref, straight_ref, held_ref = refs[-3:]
    first = sec_ref[0] == 0
    held_ref[:ROWS] = jnp.where(first, mine_ref[...], other_ref[...])
    held_ref[ROWS:] = jnp.where(first, other_ref[...], mine_ref[...])
    for part in range(3):
        spot = slice(WIDTH * part, WIDTH * (part + 1))
        spread = dot(held_ref[...], picks_of(feature_ref, part)).astype(BF)
        straight_ref[:, spot] = spread
        turned_ref[spot] = spread.T


def spread_rows(section, feature, mine, other, after):
    return pl.pallas_call(
        spread_kernel,
        out_shape=[spec_of((3 * WIDTH, 256), BF), spec_of((256, 3 * WIDTH), BF)],
        in_specs=[SMEM] + [VMEM] * 3 + [HBM] * len(after),
        out_specs=[VMEM] * 2,
        scratch_shapes=[pltpu.VMEM((256, WIDTH), BF)],
        compiler_params=PARAMS,
        cost_estimate=cost(4.0),
        name="spread_rows",
    )(section, feature, mine, other, *after)


def word_chunks(words):
    starts = [[part * WORD_PART + step * WORD_STEP for step in range(STEPS)] for part in range(3)]
    return [[(start, min(WORD_STEP, words - start)) for start in part] for part in starts]


def grad_copies(grad_ref, held_ref, sems, words):
    copies = []
    for part, chunks in enumerate(word_chunks(words)):
        copies.append(
            [
                pltpu.make_async_copy(
                    grad_ref.at[pl.ds(start, size)],
                    held_ref.at[part % 2, pl.ds(step * WORD_STEP, size)],
                    sems.at[part % 2, step],
                )
                for step, (start, size) in enumerate(chunks)
            ]
        )
    return copies


def clear_rest(held_ref, part, words):
    used = min(WORD_PART, words - part * WORD_PART)
    if used < WORD_PART:
        held_ref[part % 2, used:] = jnp.zeros((WORD_PART - used, 256), BF)


def send_kernel(lhs_ref, grad_ref, *refs):
    outs, grad_buf, out_buf, grad_sems, out_sems = refs[:6], refs[6], refs[7], refs[8], refs[9]
    words = grad_ref.shape[0]
    arrive = grad_copies(grad_ref, grad_buf, grad_sems, words)
    leave = []
    start_all(arrive[0])
    start_all(arrive[1])
    for part in range(3):
        for step in range(STEPS):
            at = part * STEPS + step
            slot = at % 3
            columns = pl.ds(step * WORD_STEP, WORD_STEP)
            arrive[part][step].wait()
            if step == STEPS - 1:
                clear_rest(grad_buf, part, words)
            if at >= 3:
                wait_all(leave[at - 3])
            spot = slice(WIDTH * part + 2 * GROUP, WIDTH * (part + 1))
            term = dot_nt(lhs_ref[spot], grad_buf[part % 2, columns])
            for n in range(2):
                out_buf[slot, n] = term[GROUP * n : GROUP * (n + 1)].astype(BF)
            leave.append(
                [
                    pltpu.make_async_copy(out_buf.at[slot, n], outs[2 * part + n].at[:, columns], out_sems.at[slot, n])
                    for n in range(2)
                ]
            )
            start_all(leave[at])
        if part == 0:
            start_all(arrive[2])
    for copies in leave[-3:]:
        wait_all(copies)


def table_send(turned, logit_grad):
    return pl.pallas_call(
        send_kernel,
        out_shape=[spec_of((GROUP, WORD_PART), BF)] * 6,
        in_specs=[VMEM, HBM],
        out_specs=[HBM] * 6,
        scratch_shapes=[
            pltpu.VMEM((2, WORD_PART, 256), BF),
            pltpu.VMEM((3, 2, GROUP, WORD_STEP), BF),
            pltpu.SemaphoreType.DMA((2, STEPS)),
            pltpu.SemaphoreType.DMA((3, 2)),
        ],
        compiler_params=PARAMS,
        cost_estimate=cost(8.0),
        name="table_send",
    )(turned, logit_grad)


def term_kernel(part, extra, pieces, lhs_ref, grad_ref, *refs):
    added, outs = refs[:extra], refs[extra : extra + pieces]
    grad_buf, add_buf, out_buf, grad_sems, add_sems, out_sems = refs[extra + pieces :]
    words = grad_ref.shape[0]
    chunks = word_chunks(words)[part]
    rows = GROUP // pieces
    grads, adds, leave = [], [], []
    for step, (start, size) in enumerate(chunks):
        columns = pl.ds(step * WORD_STEP, WORD_STEP)
        grads.append(pltpu.make_async_copy(grad_ref.at[pl.ds(start, size)], grad_buf.at[step, pl.ds(0, size)], grad_sems.at[step]))
        adds.append([pltpu.make_async_copy(added[n].at[:, columns], add_buf.at[step, n], add_sems.at[step, n]) for n in range(extra)])
        leave.append(
            [
                pltpu.make_async_copy(out_buf.at[step, pl.ds(n * rows, rows)], outs[n].at[:, columns], out_sems.at[step, n])
                for n in range(pieces)
            ]
        )
        grads[step].start()
        start_all(adds[step])
    for step, (start, size) in enumerate(chunks):
        grads[step].wait()
        if size < WORD_STEP:
            grad_buf[step, size:] = jnp.zeros((WORD_STEP - size, 256), BF)
        total = dot_nt(lhs_ref[...], grad_buf[step])
        wait_all(adds[step])
        for n in range(extra):
            total = total + add_buf[step, n].astype(F32)
        out_buf[step] = total.astype(BF)
        start_all(leave[step])
    for copies in leave:
        wait_all(copies)


def table_term(part, block, turned, logit_grad, added, pieces):
    extra = len(added)
    rows = GROUP // pieces
    return pl.pallas_call(
        functools.partial(term_kernel, part, extra, pieces),
        grid=(1,),
        out_shape=[spec_of((rows, WORD_PART), BF)] * pieces,
        in_specs=[pl.BlockSpec((GROUP, 256), lambda i: (4 * part + block, 0))] + [HBM] * (1 + extra),
        out_specs=[HBM] * pieces,
        scratch_shapes=[
            pltpu.VMEM((STEPS, WORD_STEP, 256), BF),
            pltpu.VMEM((STEPS, extra, GROUP, WORD_STEP), BF),
            pltpu.VMEM((STEPS, GROUP, WORD_STEP), BF),
            pltpu.SemaphoreType.DMA((STEPS,)),
            pltpu.SemaphoreType.DMA((STEPS, extra)),
            pltpu.SemaphoreType.DMA((STEPS, pieces)),
        ],
        compiler_params=PARAMS,
        cost_estimate=cost(4.0),
        name="table_term",
    )(turned, logit_grad, *added)


def terms_kernel(parts, block, extra, pieces, lhs_ref, grad_ref, *refs):
    count = len(parts)
    added, outs = refs[: count * extra], refs[-6 - count * pieces : -6]
    grad_buf, add_buf, out_buf, grad_sems, add_sems, out_sems = refs[-6:]
    rows = GROUP // pieces
    words = word_chunks(grad_ref.shape[0])
    chunks = [(n, step, *chunk) for n, part in enumerate(parts) for step, chunk in enumerate(words[part])]
    arrive, leave = [], []
    for at, (part, step, start, size) in enumerate(chunks):
        slot = at % DEPTH
        columns = pl.ds(step * WORD_STEP, WORD_STEP)
        arrive.append(
            [pltpu.make_async_copy(grad_ref.at[pl.ds(start, size)], grad_buf.at[slot, pl.ds(0, size)], grad_sems.at[slot])]
            + [
                pltpu.make_async_copy(added[extra * part + n].at[:, columns], add_buf.at[slot, n], add_sems.at[slot, n])
                for n in range(extra)
            ]
        )
        leave.append(
            [
                pltpu.make_async_copy(out_buf.at[slot, pl.ds(n * rows, rows)], outs[pieces * part + n].at[:, columns], out_sems.at[slot, n])
                for n in range(pieces)
            ]
        )
    for at in range(DEPTH - 1):
        start_all(arrive[at])
    for at, (part, step, start, size) in enumerate(chunks):
        slot = at % DEPTH
        wait_all(arrive[at])
        if at + DEPTH - 1 < len(chunks):
            start_all(arrive[at + DEPTH - 1])
        if at >= DEPTH:
            wait_all(leave[at - DEPTH])
        if size < WORD_STEP:
            grad_buf[slot, size:] = jnp.zeros((WORD_STEP - size, 256), BF)
        spot = WIDTH * parts[part] + GROUP * block
        total = dot_nt(lhs_ref[spot : spot + GROUP], grad_buf[slot])
        for n in range(extra):
            total = total + add_buf[slot, n].astype(F32)
        out_buf[slot] = total.astype(BF)
        start_all(leave[at])
    for copies in leave[-DEPTH:]:
        wait_all(copies)


def table_terms(parts, block, turned, logit_grad, added, pieces, after=()):
    count = len(parts)
    extra = len(added) // count
    rows = GROUP // pieces
    return pl.pallas_call(
        functools.partial(terms_kernel, parts, block, extra, pieces),
        out_shape=[spec_of((rows, WORD_PART), BF)] * (count * pieces),
        in_specs=[VMEM] + [HBM] * (1 + count * extra + len(after)),
        out_specs=[HBM] * (count * pieces),
        scratch_shapes=[
            pltpu.VMEM((DEPTH, WORD_STEP, 256), BF),
            pltpu.VMEM((DEPTH, extra, GROUP, WORD_STEP), BF),
            pltpu.VMEM((DEPTH, GROUP, WORD_STEP), BF),
            pltpu.SemaphoreType.DMA((DEPTH,)),
            pltpu.SemaphoreType.DMA((DEPTH, extra)),
            pltpu.SemaphoreType.DMA((DEPTH, pieces)),
        ],
        compiler_params=PARAMS,
        cost_estimate=cost(1.5 + 3.0 * count),
        name="table_terms",
    )(turned, logit_grad, *added, *after)


def table_stream(ins, held_ref, sems, parts):
    copies = []
    for at in range(len(parts) * STEPS):
        columns = pl.ds(at % STEPS * WORD_STEP, WORD_STEP)
        copies.append(
            [
                pltpu.make_async_copy(
                    ins[4 * (at // STEPS) + n].at[:, columns], held_ref.at[at % DEPTH, pl.ds(GROUP * n, GROUP)], sems.at[at % DEPTH, n]
                )
                for n in range(4)
            ]
        )
    return copies


def head_grad_kernel(feature_ref, grad_ref, *refs):
    ins, (out_ref, total_ref, term_ref, table_buf, grad_buf, table_sems, grad_sems) = refs[:12], refs[-7:]
    chunks = [chunk for part in word_chunks(grad_ref.shape[0]) for chunk in part]
    arrive = table_stream(ins, table_buf, table_sems, range(3))
    for at, (start, size) in enumerate(chunks):
        slot = at % DEPTH
        arrive[at].append(pltpu.make_async_copy(grad_ref.at[pl.ds(start, size)], grad_buf.at[slot, pl.ds(0, size)], grad_sems.at[slot]))
    for at in range(DEPTH - 1):
        start_all(arrive[at])
    for at, (start, size) in enumerate(chunks):
        slot = at % DEPTH
        wait_all(arrive[at])
        if at + DEPTH - 1 < len(chunks):
            start_all(arrive[at + DEPTH - 1])
        if size < WORD_STEP:
            grad_buf[slot, size:] = jnp.zeros((WORD_STEP - size, 256), BF)
        term = dot(table_buf[slot], grad_buf[slot])
        if at % STEPS == 0:
            term_ref[...] = term
        else:
            term_ref[...] += term
        if at % STEPS == STEPS - 1:
            part = at // STEPS
            placed = dot(picks_of(feature_ref, part), term_ref[...].astype(BF))
            if part == 0:
                total_ref[...] = placed
            else:
                total_ref[...] += placed
    out_ref[...] = total_ref[...].T


def head_grad(feature, logit_grad, table, after):
    return pl.pallas_call(
        head_grad_kernel,
        out_shape=spec_of((256, WIDTH), F32),
        in_specs=[VMEM] + [HBM] * (13 + len(after)),
        out_specs=VMEM,
        scratch_shapes=[
            pltpu.VMEM((WIDTH, 256), F32),
            pltpu.VMEM((WIDTH, 256), F32),
            pltpu.VMEM((DEPTH, WIDTH, WORD_STEP), BF),
            pltpu.VMEM((DEPTH, WORD_STEP, 256), BF),
            pltpu.SemaphoreType.DMA((DEPTH, 4)),
            pltpu.SemaphoreType.DMA((DEPTH,)),
        ],
        compiler_params=PARAMS,
        cost_estimate=cost(14.0),
        name="head_grad",
    )(feature, logit_grad, *[block for blocks in table for block in blocks], *after)


def logits_kernel(parts, lhs_ref, *refs):
    ins, (out_ref, table_buf, out_buf, table_sems, out_sems) = refs[: 4 * len(parts)], refs[-5:]
    words = word_chunks(out_ref.shape[0])
    chunks = [chunk for part in parts for chunk in words[part]]
    arrive = table_stream(ins, table_buf, table_sems, parts)
    leave = []
    for at in range(DEPTH - 1):
        start_all(arrive[at])
    for at, (start, size) in enumerate(chunks):
        slot = at % DEPTH
        wait_all(arrive[at])
        if at + DEPTH - 1 < len(chunks):
            start_all(arrive[at + DEPTH - 1])
        if at >= DEPTH:
            leave[at - DEPTH].wait()
        part = parts[at // STEPS]
        lhs = lhs_ref[:, WIDTH * part : WIDTH * (part + 1)]
        out_buf[slot] = dot(lhs, table_buf[slot]).astype(BF).T
        leave.append(pltpu.make_async_copy(out_buf.at[slot, pl.ds(0, size)], out_ref.at[pl.ds(start, size)], out_sems.at[slot]))
        leave[at].start()
    wait_all(leave[-DEPTH:])


def logits_of(parts, straight, table, words, before, after):
    blocks = [block for part in parts for block in table[part]]
    extra = [] if before is None else [before]
    return pl.pallas_call(
        functools.partial(logits_kernel, parts),
        out_shape=spec_of((words, 256), BF),
        in_specs=[VMEM] + [HBM] * (len(blocks) + len(extra) + len(after)),
        out_specs=HBM,
        scratch_shapes=[
            pltpu.VMEM((DEPTH, WIDTH, WORD_STEP), BF),
            pltpu.VMEM((DEPTH, WORD_STEP, 256), BF),
            pltpu.SemaphoreType.DMA((DEPTH, 4)),
            pltpu.SemaphoreType.DMA((DEPTH,)),
        ],
        compiler_params=PARAMS,
        input_output_aliases={1 + len(blocks): 0} if extra else {},
        cost_estimate=cost(1.0 + 4.5 * len(parts)),
        name="logits",
    )(straight, *blocks, *extra, *after)


def combine_kernel(sec_ref, where_ref, *refs):
    kept, came, outs = refs[:4], refs[4:8], refs[8:12]
    bufs, sems = refs[12:16], refs[16]

    def copies(layer):
        return [
            [pltpu.make_async_copy(sources[2 * layer + n].at[g], bufs[2 * m + n].at[g], sems.at[2 * m + n, g]) for g in range(4)]
            for n in range(2)
            for m, sources in enumerate((kept, came))
        ]

    def bring(layer):
        for group in copies(layer):
            start_all(group)

    @pl.when(sec_ref[0] == 0)
    def _():
        bring(0)

    @pl.when(sec_ref[0] != 0)
    def _():
        bring(1)

    def added(first, second):
        return (first.astype(F32) + second.astype(F32)).astype(BF)

    arriving = copies(0)
    for group in arriving[:2]:
        wait_all(group)
    for n in range(4):
        a = where_ref[0, n]
        outs[n // 2][n % 2] = added(bufs[0][a], bufs[2][a])
    for group in arriving[2:]:
        wait_all(group)
    for n in range(4):
        b = where_ref[1, n]
        outs[2 + n // 2][n % 2] = added(bufs[1][:, b], bufs[3][:, b])


def combine(section, where, kept, came):
    shapes = [(2, GROUP, A_WIDTH)] * 2 + [(2, 4, 48, B_WIDTH)] * 2
    outs = pl.pallas_call(
        combine_kernel,
        out_shape=[spec_of(shape, BF) for shape in shapes],
        in_specs=[SMEM, SMEM] + [HBM] * 8,
        out_specs=[VMEM] * 4,
        scratch_shapes=[pltpu.VMEM(shape, BF) for shape in (A_SHAPE, B_SHAPE) * 2] + [pltpu.SemaphoreType.DMA((4, 4))],
        compiler_params=PARAMS,
        cost_estimate=cost(8.0),
        name="combine_grads",
    )(section, where, *kept, *came)
    return outs


def features():
    rows = []
    for order in ORDERS:
        steps = [jnp.stack(relative(axis)) * (12 * STRIDE[axis]) for axis in order[::-1]]
        feature = (
            steps[0][:, None, None, None]
            + steps[1][None, :, None, None]
            + steps[2][None, None, :, None]
            + jnp.arange(12)[None, None, None, :]
        )
        rows.append(feature.reshape(1, WIDTH))
    return jnp.concatenate(rows, axis=1).astype(jnp.int32)


def tied(values, *others):
    return lax.optimization_barrier((values, *others))[0]


def per_device(
    tokens, lengths, w_qkv, b_qv, w_post, b_post, gain_one, shift_one, w_inter, b_inter, w_out, b_out, gain_two, shift_two,
    embed_table, logit_grad,
):
    section_index = lax.axis_index("section")
    section = section_index.astype(jnp.int32)[None]
    is_first = section_index == 0
    words = embed_table.shape[1]
    where = wheres()
    given = dict(b_qv=b_qv, b_inter=b_inter, b_post=b_post, gain_one=gain_one, shift_one=shift_one, b_out=b_out, gain_two=gain_two, shift_two=shift_two)

    grad_turned = logit_grad.T
    turn = (1, 0, 2)

    rows = list(pack(
        w_qkv.transpose(turn),
        w_post.transpose(turn),
        w_inter.transpose(turn),
        w_out[0],
        embed_table,
        [given[name] for name in SHARD],
    ))
    names = ["table_weights", "table_b", "table_c"]

    def low_join(blocks):
        return jnp.concatenate(blocks, axis=0)

    for part in range(3):
        pairs = gather_pairs(rows[part], ORDERS[part][0], names[part], low_join)
        if part == 0:
            quarters = [pair[12 * n : 12 * (n + 1), WORD_PART:] for pair in pairs for n in range(2)]
            weights = low_join(in_place(quarters, "z"))
            pairs = [pair[:, :WORD_PART] for pair in pairs]
        rows[part] = low_join(pairs)
    rows[0] = jnp.concatenate([rows[0], weights[:, :A_WIDTH]], axis=1)
    rows[2] = jnp.concatenate([rows[2], weights[:, A_WIDTH:]], axis=1)
    names = ["table_a", "table_b", "table_c"]
    paired = [gather_pairs(rows[part], ORDERS[part][1], names[part], pair_rows) for part in range(3)]
    stacked = [stack_rows(paired[part], ORDERS[part][1]) for part in (0, 2, 1)]
    blocks_a = gather_stage(tied(stacked[0][1].reshape(GROUP, A_WIDTH), paired[1][0]), "x", "weights_a")
    blocks_b = gather_stage(tied(stacked[1][1], paired[1][0]), "y", "weights_b")
    blocks_b[0] = tied(blocks_b[0], stacked[2][0])
    mine = assemble(where, blocks_a, blocks_b)
    with jax.named_scope("weights_swap"):
        other = [swap(piece) for piece in mine]
    vectors = expand(mine[0], other[0])
    rows = [stacked[0][0], stacked[2][0], stacked[1][0]]
    rows[0] = tied(rows[0], blocks_a[1], blocks_a[2])
    rows[1] = tied(rows[1], blocks_b[1], blocks_b[2])
    last_axes = [order[2] for order in ORDERS]

    def sent(exchanged, part, block, label):
        with jax.named_scope(names[part] + "_" + last_axes[part] + "_" + label):
            return exchanged(block, last_axes[part])

    table_first = [sent(near, part, rows[part], "first") for part in range(3)]
    feature = features()

    inputs = lax.dynamic_slice_in_dim(tokens, section_index * ROWS, ROWS, 0)
    middle, kept_zero = forward(0, section, lengths, inputs, vectors, mine, other)
    held = tied(tuple(rows), middle)
    table_second = [sent(next_near, part, held[part], "second") for part in range(3)]
    top, kept_one = forward(1, section, lengths, middle, vectors, mine, other)
    with jax.named_scope("top_swap"):
        top_other = swap(top)
    turned, straight = spread_rows(section, feature, top, top_other, [])
    held = (*tied(tuple(table_first[:2]), top), tied(table_first[2], turned))
    table_across = [sent(next_near, part, held[part], "across") for part in range(3)]
    table = list(zip(rows, table_first, table_second, table_across, strict=True))
    leaving = table_send(tied(turned, *table_second), grad_turned)
    names = ["grad_a", "grad_b", "grad_c"]
    grad_rows = head_grad(feature, tied(grad_turned, *leaving), table, [])
    with jax.named_scope("head_swap"):
        head_came = swap(lax.dynamic_slice_in_dim(grad_rows, (1 - section_index) * ROWS, ROWS, 0))
    later = tied(turned, grad_rows)
    came, direct = [], []
    for part in range(3):
        axis = ORDERS[part][2]
        with jax.named_scope(names[part] + "_" + axis + "_across"):
            came.append(next_near(leaving[2 * part + 1], axis))
        with jax.named_scope(names[part] + "_" + axis + "_second"):
            direct.append(next_near(leaving[2 * part], axis))
    passed = table_terms((0, 1, 2), 1, later, grad_turned, came, 1)
    onward = []
    for part in range(3):
        axis = ORDERS[part][2]
        with jax.named_scope(names[part] + "_" + axis + "_first"):
            onward.append(near(passed[part], axis))
    pieces = [table_term(0, 0, turned, grad_turned, [onward[0], direct[0]], 2)]
    both = table_terms((1, 2), 0, turned, grad_turned, [onward[1], direct[1], onward[2], direct[2]], 2)
    pieces += [both[:2], both[2:]]

    grad_top = lax.dynamic_slice_in_dim(grad_rows, section_index * ROWS, ROWS, 0) + head_came
    grad_middle, terms_one = backward(1, section, grad_top, middle, vectors, mine, other, kept_one)
    with jax.named_scope("one_swap"):
        came_one = [swap(term) for term in terms_one]
    grad_middle = tied(grad_middle, *passed)
    grad_inputs, terms_zero = backward(0, section, grad_middle, inputs, vectors, mine, other, kept_zero)
    with jax.named_scope("zero_swap"):
        came_zero = [swap(term) for term in terms_zero]

    token_low = grad_inputs.astype(BF)
    half = WIDTH // 2
    own_half = lax.dynamic_slice_in_dim(token_low, section_index * half, half, 1)
    with jax.named_scope("token_swap"):
        came_half = swap(lax.dynamic_slice_in_dim(token_low, (1 - section_index) * half, half, 1))
    token_out = jnp.concatenate([jnp.where(is_first, own_half, came_half), jnp.where(is_first, came_half, own_half)], axis=0)

    combined = combine(section, where, [*terms_zero, *terms_one], [*came_zero, *came_one])

    kept_a, sent_a, kept_b, sent_b = combined
    logits = logits_of((0, 1, 2), tied(straight, combined[0]), table, words, None, [])
    kept_a, kept_b = gate([kept_a, kept_b], [logits])

    parts_a = scatter_pairs(kept_a, sent_a, "x", "sum_a")
    parts_b = scatter_pairs(kept_b, sent_b, "y", "sum_b")
    whole = []
    for part in range(3):
        total = summed(scatter_pairs(*pieces[part], ORDERS[part][1], names[part], [parts_a[3], parts_b[3]])[:3])
        whole.append(total.astype(BF))
    places_a = picked(summed(parts_a[:3]).astype(BF).reshape(4, 48, A_WIDTH), "y")
    places_b = picked(summed(parts_b[:3]).astype(BF)[0], "x")
    sum_a = summed(scatter_direct(places_a, "y", "sum_a")).astype(BF)
    sum_b = summed(scatter_direct(places_b, "x", "sum_b")).astype(BF)
    whole = tied(whole, places_a[3], places_b[3])
    ends = [scatter_pairs(whole[part][:24], whole[part][24:], ORDERS[part][0], names[part]) for part in range(3)]
    table_sums = [summed(end[:3]) for end in ends]
    table_grad = jnp.concatenate(table_sums, axis=1)[:, :words]
    both = jnp.concatenate([sum_a, sum_b], axis=1).reshape(4, 12, A_WIDTH + B_WIDTH)
    pieces = scatter_direct(tied(picked(both, "z"), *[end[3] for end in ends]), "z", "sum")
    g_qkv, g_post, g_inter, g_out, *g_vectors = unpack(pieces)
    sums = dict(zip(SHARD, g_vectors, strict=True))
    sums.update(w_qkv=g_qkv.transpose(turn), w_post=g_post.transpose(turn), w_inter=g_inter.transpose(turn), w_out=g_out[None])
    names = ("w_qkv", "b_qv", "w_post", "b_post", "gain_one", "shift_one", "w_inter", "b_inter", "w_out", "b_out", "gain_two", "shift_two")
    return (logits.T, token_out) + tuple(sums[name] for name in names) + (table_grad,)


def solution(mesh):
    matrix, vector = P("section", "dp", None), P("section", "dp")
    weights = (matrix, vector, matrix, vector, vector, vector, matrix, vector, matrix, vector, vector, vector)
    return jax.shard_map(
        per_device,
        mesh=mesh,
        in_specs=(P("dp", None), P("dp", None)) + weights + (P("dp", "section"), P("dp", "section")),
        out_specs=(P("dp", "section"), P("dp", "section")) + weights + (P("dp", "section"),),
        check_vma=False,
    )
```
